32 devices in a mesh: dom: 2 (over x), col: 4 (over y, core), row: 4 (over z).
Axes of the slice: x: 2, y: 2, z: 4, core: 2. Of those that a mesh axis runs over, the one named last changes fastest.
Arguments:
- vectors: bfloat16 [4096, 512], P(('col', 'row'), 'dom'), parts along dimension 1, may hold values from -6 to 6
- blocks: bfloat16 [8, 4, 16, 128, 128], P(('dom', 'col'), 'row'), parts along dimension 0, may hold values from -0.0625 to 0.0625
- cols: int32 [8, 4, 16], P(('dom', 'col'), 'row'), parts along dimension 0, may hold values from 0 to 7
Outputs:
- last: float32 [4096, 512], P(('col', 'row'), 'dom'), parts along dimension 1
- before: float32 [4096, 512], P(('col', 'row'), 'dom'), parts along dimension 1
The draws below stay inside these ranges and needn't reach their ends.
There are 2 independent parts, one for each index of `dom`. The reference program is written for one: setup_inputs(seed, part) draws one part's arguments, and reference() takes and returns one part's arrays. A program takes and returns all parts, laid end to end along the dimension named above; each array names one. Nothing has to cross between parts.
All inputs are finite; a program needn't handle non-finite values.
Results may differ from the reference program's by a relative error of at most 0.025.
Values may be sent and summed in bfloat16 or wider, within the bound.
No kernel may reach another device: no remote copies, remote signals or barrier semaphores. Data moves between devices by JAX's collectives and lax.ppermute only.
A program may use at most 64 MiB of HBM per device.

```python
import jax
import jax.numpy as jnp
from jax import lax

ORB = 128
VECS = 256
BP = 2
PER_ROW = 2
DEG = 4
SLOTS = 16
NORB = 4096
N_COL = 4
N_ROW = 4


def set_ends(values, own_key, low, top_value):
    place = [jax.random.randint(jax.random.fold_in(own_key, axis), (), 0, length) for axis, length in enumerate(values.shape)]
    widest = values.shape.index(max(values.shape))
    neighbour = place[:widest] + [(place[widest] + 1) % values.shape[widest]] + place[widest + 1:]
    return values.at[tuple(place)].set(low).at[tuple(neighbour)].set(top_value)


def shard_levels(rng, dims, split, low, high):
    level, own = 1.0, jax.random.fold_in(rng, 6)
    for axis_at, shards_of in split:
        draws = jnp.exp(jax.random.uniform(jax.random.fold_in(own, axis_at), (shards_of,), jnp.float32, low / len(split), high / len(split)))
        level = level * jnp.repeat(draws, dims[axis_at] // shards_of).reshape([-1 if axis == axis_at else 1 for axis in range(len(dims))])
    return level


def centred(rng, shape, width, reach, shards=(), kind=jnp.bfloat16):
    values = jax.random.normal(rng, shape, jnp.float32) * width
    if len(shards) > 0:
        values = shard_levels(rng, shape, shards, -0.22, 0.18) * values
    return jnp.clip(values, min=-reach, max=reach).astype(kind)


def setup_inputs(seed: int = 0, part: int = 0) -> dict:
    streams_of = jax.random.split(jax.random.key(seed), 4)
    own_keys = jax.random.split(jax.random.fold_in(streams_of[3], part), 4)
    return {
        "vectors": centred(own_keys[0], (NORB, VECS), 1.0, 6.0, ((0, 16),)),
        "blocks": centred(own_keys[1], (N_COL, N_ROW, SLOTS, ORB, ORB), (8 * N_ROW * PER_ROW * ORB) ** -0.5, 0.0625, ((0, 4), (1, 4))),
        "cols": set_ends(jax.random.randint(own_keys[2], (N_COL, N_ROW, SLOTS), 0, N_COL * BP), jax.random.fold_in(own_keys[2], 1), 0, (N_COL * BP) - 1).astype(jnp.int32),
    }


def tile_terms(tile, ids, wide, tall):
    grouped = tile.astype(jnp.float32).reshape(N_ROW * BP, PER_ROW, ORB, ORB)
    picked = jnp.take(wide, ids, axis=0).reshape(N_ROW * BP, PER_ROW, ORB, VECS)
    direct = jnp.einsum('tpio,tpok->tik', grouped, picked)
    mirrored = jnp.einsum('tpio,tik->tpok', grouped, tall).reshape(N_ROW * BP * PER_ROW, ORB, VECS)
    onehot = (ids[:, None] == jnp.arange(N_COL * BP, dtype=jnp.int32)[None, :]).astype(jnp.float32)
    summed = jnp.einsum('su,sok->uok', onehot, mirrored, precision=lax.Precision.HIGHEST)
    return direct.reshape(N_ROW * BP * ORB, VECS).astype(jnp.bfloat16), summed.reshape(N_COL * BP * ORB, VECS).astype(jnp.bfloat16)


def apply_pair(send, blocks, cols):
    pieces = send.astype(jnp.float32).reshape(N_COL, N_ROW, BP * ORB, VECS)

    def per_tile(index):
        across = (index // N_ROW).astype(jnp.int32)
        down = (index % N_ROW).astype(jnp.int32)
        tile = lax.dynamic_index_in_dim(lax.dynamic_index_in_dim(blocks, across, 0, False), down, 0, False)
        ids = lax.dynamic_index_in_dim(lax.dynamic_index_in_dim(cols, across, 0, False), down, 0, False)
        wide = lax.dynamic_index_in_dim(pieces, down, 1, False).reshape(N_COL * BP, ORB, VECS)
        tall = lax.dynamic_index_in_dim(pieces, across, 0, False).reshape(N_ROW * BP, ORB, VECS)
        return tile_terms(tile, ids, wide, tall)

    direct, summed = lax.map(per_tile, jnp.arange(N_COL * N_ROW, dtype=jnp.int32))
    part_rows = direct.astype(jnp.float32).reshape(N_COL, N_ROW, N_ROW * BP * ORB, VECS).sum(axis=1)
    part_rows = part_rows.reshape(N_COL * N_ROW * BP * ORB, VECS)
    part_cols = summed.astype(jnp.float32).reshape(N_COL, N_ROW, N_COL, BP * ORB, VECS).sum(axis=0)
    part_cols = jnp.transpose(part_cols, (1, 0, 2, 3)).reshape(N_COL * N_ROW * BP * ORB, VECS)
    return part_rows + part_cols


def reference(vectors, blocks, cols):
    prev = vectors.astype(jnp.float32)
    now = apply_pair(vectors, blocks, cols)
    for step in range(DEG - 1):
        nxt = 2.0 * apply_pair(now.astype(jnp.bfloat16), blocks, cols) - prev
        prev, now = now, nxt
    return now, prev
```

```python
import functools

import jax
import jax.numpy as jnp
from jax import lax
from jax.experimental import pallas as pl
from jax.experimental.pallas import tpu as pltpu
from jax.sharding import PartitionSpec as P

PER_ROW = 2
DEG = 4
GATHER_LIMIT = 12 * 2**20
LANES = ("col", "row")


def onehot_sum(selected, high_part, low_part):
    first = jnp.einsum("su,sok->uok", selected, high_part, preferred_element_type=jnp.float32)
    second = jnp.einsum("su,sok->uok", selected, low_part, preferred_element_type=jnp.float32)
    return first + second


def apply_pair(send, grouped, col_ids, onehot):
    tile_rows, per_row, orb, _ = grouped.shape
    piece_rows, width = send.shape
    tile_cols = onehot.shape[1]
    wide = lax.all_gather(send, "col", axis=0, tiled=True).reshape(tile_cols, orb, width)
    picked = jnp.take(wide, col_ids, axis=0).reshape(tile_rows, per_row, orb, width)
    direct = jnp.einsum("tpio,tpok->tik", grouped, picked, preferred_element_type=jnp.float32)
    part_rows = lax.psum_scatter(
        direct.reshape(tile_rows * orb, width).astype(jnp.bfloat16),
        "row",
        scatter_dimension=0,
        tiled=True,
    ).astype(jnp.float32)
    tall = lax.all_gather(send, "row", axis=0, tiled=True).reshape(tile_rows, orb, width)
    mirrored = jnp.einsum("tpio,tik->tpok", grouped, tall, preferred_element_type=jnp.float32)
    mirrored = mirrored.reshape(tile_rows * per_row, orb, width)
    high_part = mirrored.astype(jnp.bfloat16)
    low_part = (mirrored - high_part.astype(jnp.float32)).astype(jnp.bfloat16)
    summed = onehot_sum(onehot, high_part, low_part)
    part_cols = lax.psum_scatter(
        summed.reshape(tile_cols * orb, width).astype(jnp.bfloat16),
        "col",
        scatter_dimension=0,
        tiled=True,
    ).astype(jnp.float32)
    return part_rows + part_cols


def spread_plan(vectors, blocks, cols):
    tiles = blocks[0, 0]
    col_ids = cols[0, 0]
    slots, orb, _ = tiles.shape
    tile_rows = slots // PER_ROW
    tile_cols = lax.axis_size("col") * (vectors.shape[0] // orb)
    grouped = tiles.reshape(tile_rows, PER_ROW, orb, orb)
    onehot = (col_ids[:, None] == jnp.arange(tile_cols, dtype=jnp.int32)[None, :]).astype(
        jnp.bfloat16
    )
    prev = vectors.astype(jnp.float32)
    now = apply_pair(vectors, grouped, col_ids, onehot)
    for step in range(DEG - 1):
        nxt = 2.0 * apply_pair(now.astype(jnp.bfloat16), grouped, col_ids, onehot) - prev
        prev, now = (now, nxt)
    return (now, prev)


def filter_kernel(n_row, per_piece, cols_ref, zt_ref, s_ref, out_ref, z, acc, now, prev):
    tiles, slots = s_ref.shape[:2]
    orb = s_ref.shape[2]
    tile_rows = slots // PER_ROW
    pieces = zt_ref.shape[0]

    for p in range(pieces):
        for b in range(per_piece):
            own = zt_ref[p, :, b * orb : (b + 1) * orb]
            z[p * per_piece + b] = own
            prev[p * per_piece + b] = own.astype(jnp.float32)

    def tile_step(tile, carry):
        across = tile // n_row
        down = tile % n_row

        def block_of(slot):
            u = cols_ref[tile, slot]
            return (u // per_piece * n_row + down) * per_piece + u % per_piece

        direct, mirrored, places = [], [], []
        for t in range(tile_rows):
            pair = jnp.concatenate([s_ref[tile, t * PER_ROW + p] for p in range(PER_ROW)], axis=1)
            where = [block_of(t * PER_ROW + p) for p in range(PER_ROW)]
            wide = jnp.concatenate([z[g] for g in where], axis=1)
            tall = z[across * tile_rows + t]
            direct.append(
                lax.dot_general(wide, pair, (((1,), (1,)), ((), ())), preferred_element_type=jnp.float32)
            )
            both = jnp.dot(tall, pair, preferred_element_type=jnp.float32)
            for p in range(PER_ROW):
                places.append(where[p])
                mirrored.append(both[:, p * orb : (p + 1) * orb])
        for t in range(tile_rows):
            acc[across * tile_rows + t] += direct[t]
        for g, term in zip(places, mirrored):
            acc[g] += term
        return carry

    for step in range(DEG):
        acc[...] = jnp.zeros_like(acc)
        lax.fori_loop(0, tiles, tile_step, 0)
        if step == 0:
            now[...] = acc[...]
        else:
            nxt = 2.0 * acc[...] - prev[...]
            prev[...] = now[...]
            now[...] = nxt
        if step < DEG - 1:
            z[...] = now[...].astype(z.dtype)
    for p in range(pieces):
        for b in range(per_piece):
            g = p * per_piece + b
            out_ref[p, 0, :, b * orb : (b + 1) * orb] = now[g].astype(out_ref.dtype)
            out_ref[p, 1, :, b * orb : (b + 1) * orb] = prev[g].astype(out_ref.dtype)


def gather_plan(vectors, blocks, cols):
    n_dev = lax.axis_size(LANES)
    n_row = lax.axis_size("row")
    rows, width = vectors.shape
    slots, orb = blocks.shape[2:4]
    share = width // n_dev
    per_piece = rows // orb

    tiles = lax.all_gather(blocks[0, 0], LANES, axis=0)
    ids = lax.all_gather(cols[0, 0], LANES, axis=0)
    turned = vectors.T.reshape(n_dev, share, rows)
    zt = lax.all_to_all(turned, LANES, split_axis=0, concat_axis=0, tiled=True)

    n_blocks = n_dev * per_piece
    done = pl.pallas_call(
        functools.partial(filter_kernel, n_row, per_piece),
        out_shape=jax.ShapeDtypeStruct((n_dev, 2, share, rows), jnp.bfloat16),
        in_specs=[
            pl.BlockSpec(memory_space=pltpu.SMEM),
            pl.BlockSpec(memory_space=pltpu.VMEM),
            pl.BlockSpec(memory_space=pltpu.VMEM),
        ],
        out_specs=pl.BlockSpec(memory_space=pltpu.VMEM),
        scratch_shapes=[
            pltpu.VMEM((n_blocks, share, orb), jnp.bfloat16),
            pltpu.VMEM((n_blocks, share, orb), jnp.float32),
            pltpu.VMEM((n_blocks, share, orb), jnp.float32),
            pltpu.VMEM((n_blocks, share, orb), jnp.float32),
        ],
        compiler_params=pltpu.CompilerParams(vmem_limit_bytes=32 * 2**20),
    )(ids, zt, tiles)
    back = lax.all_to_all(done, LANES, split_axis=0, concat_axis=0, tiled=True)
    outs = jnp.transpose(back, (1, 3, 0, 2)).reshape(2, rows, width).astype(jnp.float32)
    return outs[0], outs[1]


def per_device(vectors, blocks, cols):
    n_dev = lax.axis_size(LANES)
    if n_dev * blocks.size * blocks.dtype.itemsize <= GATHER_LIMIT:
        return gather_plan(vectors, blocks, cols)
    return spread_plan(vectors, blocks, cols)


def solution(mesh):
    return jax.shard_map(
        per_device,
        mesh=mesh,
        in_specs=(
            P(("col", "row"), "dom"),
            P(("dom", "col"), "row", None, None, None),
            P(("dom", "col"), "row", None),
        ),
        out_specs=(P(("col", "row"), "dom"), P(("col", "row"), "dom")),
        check_vma=False,
    )
```

```python
import functools

import jax
import jax.numpy as jnp
from jax import lax
from jax.experimental import pallas as pl
from jax.experimental.pallas import tpu as pltpu
from jax.sharding import PartitionSpec as P

PER_ROW = 2
DEG = 4
GATHER_LIMIT = 12 * 2**20
LANES = ("col", "row")


def onehot_sum(selected, high_part, low_part):
    first = jnp.einsum("su,sok->uok", selected, high_part, preferred_element_type=jnp.float32)
    second = jnp.einsum("su,sok->uok", selected, low_part, preferred_element_type=jnp.float32)
    return first + second


def apply_pair(send, grouped, col_ids, onehot):
    tile_rows, per_row, orb, _ = grouped.shape
    piece_rows, width = send.shape
    tile_cols = onehot.shape[1]
    wide = lax.all_gather(send, "col", axis=0, tiled=True).reshape(tile_cols, orb, width)
    picked = jnp.take(wide, col_ids, axis=0).reshape(tile_rows, per_row, orb, width)
    direct = jnp.einsum("tpio,tpok->tik", grouped, picked, preferred_element_type=jnp.float32)
    part_rows = lax.psum_scatter(
        direct.reshape(tile_rows * orb, width).astype(jnp.bfloat16),
        "row",
        scatter_dimension=0,
        tiled=True,
    ).astype(jnp.float32)
    tall = lax.all_gather(send, "row", axis=0, tiled=True).reshape(tile_rows, orb, width)
    mirrored = jnp.einsum("tpio,tik->tpok", grouped, tall, preferred_element_type=jnp.float32)
    mirrored = mirrored.reshape(tile_rows * per_row, orb, width)
    high_part = mirrored.astype(jnp.bfloat16)
    low_part = (mirrored - high_part.astype(jnp.float32)).astype(jnp.bfloat16)
    summed = onehot_sum(onehot, high_part, low_part)
    part_cols = lax.psum_scatter(
        summed.reshape(tile_cols * orb, width).astype(jnp.bfloat16),
        "col",
        scatter_dimension=0,
        tiled=True,
    ).astype(jnp.float32)
    return part_rows + part_cols


def spread_plan(vectors, blocks, cols):
    tiles = blocks[0, 0]
    col_ids = cols[0, 0]
    slots, orb, _ = tiles.shape
    tile_rows = slots // PER_ROW
    tile_cols = lax.axis_size("col") * (vectors.shape[0] // orb)
    grouped = tiles.reshape(tile_rows, PER_ROW, orb, orb)
    onehot = (col_ids[:, None] == jnp.arange(tile_cols, dtype=jnp.int32)[None, :]).astype(
        jnp.bfloat16
    )
    prev = vectors.astype(jnp.float32)
    now = apply_pair(vectors, grouped, col_ids, onehot)
    for step in range(DEG - 1):
        nxt = 2.0 * apply_pair(now.astype(jnp.bfloat16), grouped, col_ids, onehot) - prev
        prev, now = (now, nxt)
    return (now, prev)


def filter_kernel(per_piece, sources, ids_ref, where_ref, zt_ref, *refs):
    bufs, (out_ref, s_ref, z, acc, now, prev, sems) = refs[:sources], refs[sources:]
    tiles, slots = s_ref.shape[:2]
    orb = s_ref.shape[2]
    tile_rows = slots // PER_ROW
    pieces = zt_ref.shape[0]
    n_row = tile_rows // per_piece

    for i, buf in enumerate(bufs):
        tile = where_ref[i]

        @pl.when(tile >= 0)
        def _():
            pltpu.make_async_copy(buf, s_ref.at[tile], sems.at[tile]).start()

    for p in range(pieces):
        for b in range(per_piece):
            own = zt_ref[p, :, b * orb : (b + 1) * orb]
            z[p * per_piece + b] = own
            prev[p * per_piece + b] = own.astype(jnp.float32)

    def tile_step(first, tile, carry):
        if first:
            pltpu.make_async_copy(bufs[0], s_ref.at[tile], sems.at[tile]).wait()
        row_base = tile // n_row * tile_rows

        direct, mirrored, places = [], [], []
        for t in range(tile_rows):
            pair = jnp.concatenate([s_ref[tile, t * PER_ROW + p] for p in range(PER_ROW)], axis=1)
            where = [ids_ref[tile, t * PER_ROW + p] for p in range(PER_ROW)]
            wide = jnp.concatenate([z[g] for g in where], axis=1)
            tall = z[row_base + t]
            direct.append(
                lax.dot_general(wide, pair, (((1,), (1,)), ((), ())), preferred_element_type=jnp.float32)
            )
            both = jnp.dot(tall, pair, preferred_element_type=jnp.float32)
            for p in range(PER_ROW):
                places.append(where[p])
                mirrored.append(both[:, p * orb : (p + 1) * orb])
        for t in range(tile_rows):
            acc[row_base + t] += direct[t]
        for g, term in zip(places, mirrored):
            acc[g] += term
        return carry

    for step in range(DEG):
        acc[...] = jnp.zeros_like(acc)
        lax.fori_loop(0, tiles, functools.partial(tile_step, step == 0), 0)
        if step == 0:
            now[...] = acc[...]
        else:
            nxt = 2.0 * acc[...] - prev[...]
            prev[...] = now[...]
            now[...] = nxt
        if step < DEG - 1:
            z[...] = now[...].astype(z.dtype)
    for p in range(pieces):
        for b in range(per_piece):
            g = p * per_piece + b
            out_ref[p, 0, :, b * orb : (b + 1) * orb] = now[g].astype(out_ref.dtype)
            out_ref[p, 1, :, b * orb : (b + 1) * orb] = prev[g].astype(out_ref.dtype)


def gather_tiles(own, n_col, n_row):
    col, row = lax.axis_index("col"), lax.axis_index("row")
    index = lambda c, r: c * n_row + r

    def send(buf, pairs):
        return lax.ppermute(buf, LANES, pairs)

    held = [(own, 0, 0)]
    for sign in (1, -1):
        buf = own
        for hop in range(1, n_row):
            pairs = []
            for r in range(n_row):
                source = r - sign * (hop - 1)
                if 0 <= r + sign < n_row and 0 <= source < n_row:
                    pairs += [(index(c, r), index(c, r + sign)) for c in range(n_col)]
            buf = send(buf, pairs)
            held.append((buf, -sign * hop, 0))
    held.sort(key=lambda item: abs(item[1]))
    bit = n_col // 2
    while bit:
        for buf, shift, flips in list(held):
            pairs = [
                (index(c, r), index(c ^ bit, r))
                for c in range(n_col)
                for r in range(n_row)
                if 0 <= r + shift < n_row
            ]
            held.append((send(buf, pairs), shift, flips | bit))
        bit //= 2
    where = []
    for _, shift, flips in held:
        r = row + shift
        where.append(jnp.where((r >= 0) & (r < n_row), (col ^ flips) * n_row + r, -1))
    return [buf for buf, _, _ in held], jnp.stack(where).astype(jnp.int32)


def gather_plan(vectors, blocks, cols):
    n_dev = lax.axis_size(LANES)
    n_col, n_row = lax.axis_size("col"), lax.axis_size("row")
    rows, width = vectors.shape
    slots, orb = blocks.shape[2:4]
    share = width // n_dev
    per_piece = rows // orb
    n_blocks = n_dev * per_piece

    bufs, where = gather_tiles(blocks[0, 0], n_col, n_row)

    turned = vectors.T.reshape(n_dev, share, rows)
    own_ids = jnp.pad(cols[0, 0].astype(jnp.bfloat16), (0, rows - slots))
    own_ids = jnp.broadcast_to(own_ids, (n_dev, share, rows))
    both = lax.all_to_all(
        jnp.concatenate([turned, own_ids], axis=1), LANES, split_axis=0, concat_axis=0, tiled=True
    )
    zt = both[:, :share]
    local = both[:, share, :slots].astype(jnp.int32)
    down = (jnp.arange(n_dev, dtype=jnp.int32) % n_row)[:, None]
    ids = (local // per_piece * n_row + down) * per_piece + local % per_piece

    done = pl.pallas_call(
        functools.partial(filter_kernel, per_piece, len(bufs)),
        out_shape=jax.ShapeDtypeStruct((n_dev, 2, share, rows), jnp.bfloat16),
        in_specs=[
            pl.BlockSpec(memory_space=pltpu.SMEM),
            pl.BlockSpec(memory_space=pltpu.SMEM),
            pl.BlockSpec(memory_space=pltpu.VMEM),
        ]
        + [pl.BlockSpec(memory_space=pl.ANY)] * len(bufs),
        out_specs=pl.BlockSpec(memory_space=pltpu.VMEM),
        scratch_shapes=[
            pltpu.VMEM((n_dev, slots, orb, orb), blocks.dtype),
            pltpu.VMEM((n_blocks, share, orb), jnp.bfloat16),
            pltpu.VMEM((n_blocks, share, orb), jnp.float32),
            pltpu.VMEM((n_blocks, share, orb), jnp.float32),
            pltpu.VMEM((n_blocks, share, orb), jnp.float32),
            pltpu.SemaphoreType.DMA((n_dev,)),
        ],
        compiler_params=pltpu.CompilerParams(vmem_limit_bytes=32 * 2**20),
    )(ids, where, zt, *bufs)
    back = lax.all_to_all(done, LANES, split_axis=0, concat_axis=0, tiled=True)
    outs = jnp.transpose(back, (1, 3, 0, 2)).reshape(2, rows, width).astype(jnp.float32)
    return outs[0], outs[1]


def per_device(vectors, blocks, cols):
    n_dev = lax.axis_size(LANES)
    if n_dev * blocks.size * blocks.dtype.itemsize <= GATHER_LIMIT:
        return gather_plan(vectors, blocks, cols)
    return spread_plan(vectors, blocks, cols)


def solution(mesh):
    return jax.shard_map(
        per_device,
        mesh=mesh,
        in_specs=(
            P(("col", "row"), "dom"),
            P(("dom", "col"), "row", None, None, None),
            P(("dom", "col"), "row", None),
        ),
        out_specs=(P(("col", "row"), "dom"), P(("col", "row"), "dom")),
        check_vma=False,
    )
```

```python
import functools

import jax
import jax.numpy as jnp
from jax import lax
from jax.experimental import pallas as pl
from jax.experimental.pallas import tpu as pltpu
from jax.sharding import PartitionSpec as P

PER_ROW = 2
DEG = 4
SPLIT = 4
GATHER_LIMIT = 12 * 2**20
LANES = ("col", "row")


def onehot_sum(selected, high_part, low_part):
    first = jnp.einsum("su,sok->uok", selected, high_part, preferred_element_type=jnp.float32)
    second = jnp.einsum("su,sok->uok", selected, low_part, preferred_element_type=jnp.float32)
    return first + second


def apply_pair(send, grouped, col_ids, onehot):
    tile_rows, per_row, orb, _ = grouped.shape
    piece_rows, width = send.shape
    tile_cols = onehot.shape[1]
    wide = lax.all_gather(send, "col", axis=0, tiled=True).reshape(tile_cols, orb, width)
    picked = jnp.take(wide, col_ids, axis=0).reshape(tile_rows, per_row, orb, width)
    direct = jnp.einsum("tpio,tpok->tik", grouped, picked, preferred_element_type=jnp.float32)
    part_rows = lax.psum_scatter(
        direct.reshape(tile_rows * orb, width).astype(jnp.bfloat16),
        "row",
        scatter_dimension=0,
        tiled=True,
    ).astype(jnp.float32)
    tall = lax.all_gather(send, "row", axis=0, tiled=True).reshape(tile_rows, orb, width)
    mirrored = jnp.einsum("tpio,tik->tpok", grouped, tall, preferred_element_type=jnp.float32)
    mirrored = mirrored.reshape(tile_rows * per_row, orb, width)
    high_part = mirrored.astype(jnp.bfloat16)
    low_part = (mirrored - high_part.astype(jnp.float32)).astype(jnp.bfloat16)
    summed = onehot_sum(onehot, high_part, low_part)
    part_cols = lax.psum_scatter(
        summed.reshape(tile_cols * orb, width).astype(jnp.bfloat16),
        "col",
        scatter_dimension=0,
        tiled=True,
    ).astype(jnp.float32)
    return part_rows + part_cols


def spread_plan(vectors, blocks, cols):
    tiles = blocks[0, 0]
    col_ids = cols[0, 0]
    slots, orb, _ = tiles.shape
    tile_rows = slots // PER_ROW
    tile_cols = lax.axis_size("col") * (vectors.shape[0] // orb)
    grouped = tiles.reshape(tile_rows, PER_ROW, orb, orb)
    onehot = (col_ids[:, None] == jnp.arange(tile_cols, dtype=jnp.int32)[None, :]).astype(
        jnp.bfloat16
    )
    prev = vectors.astype(jnp.float32)
    now = apply_pair(vectors, grouped, col_ids, onehot)
    for step in range(DEG - 1):
        nxt = 2.0 * apply_pair(now.astype(jnp.bfloat16), grouped, col_ids, onehot) - prev
        prev, now = (now, nxt)
    return (now, prev)


def filter_kernel(per_piece, n_row, sources, ids_ref, where_ref, zt_ref, *refs):
    bufs, (out_ref, s_ref, z, now, prev, straight, *scattered, sems) = refs[:sources], refs[sources:]
    tiles, slots = s_ref.shape[:2]
    orb = s_ref.shape[2]
    tile_rows = slots // PER_ROW
    pieces = zt_ref.shape[0]

    for i, buf in enumerate(bufs):
        tile = where_ref[i]

        @pl.when(tile >= 0)
        def _():
            pltpu.make_async_copy(buf, s_ref.at[tile], sems.at[tile]).start()

    for p in range(pieces):
        for b in range(per_piece):
            own = zt_ref[p, :, b * orb : (b + 1) * orb]
            z[p * per_piece + b] = own
            now[p * per_piece + b] = own.astype(jnp.float32)
    prev[...] = jnp.zeros_like(prev)

    def row_group(step, across, carry):
        group = [across * n_row + r for r in range(n_row)]

        @pl.when(step == 0)
        def _():
            for tile in group:
                pltpu.make_async_copy(bufs[0], s_ref.at[tile], sems.at[tile]).wait()

        for t in range(tile_rows):
            places = [(tile, t * PER_ROW + p) for tile in group for p in range(PER_ROW)]
            strip = jnp.concatenate([s_ref[tile, slot] for tile, slot in places], axis=1)
            where = [ids_ref[tile, slot] for tile, slot in places]
            wide = jnp.concatenate([z[g] for g in where], axis=1)
            tall = z[across * tile_rows + t]
            straight[across * tile_rows + t] = lax.dot_general(
                wide, strip, (((1,), (1,)), ((), ())), preferred_element_type=jnp.float32
            )
            turned = jnp.dot(tall, strip, preferred_element_type=jnp.float32)
            for i, g in enumerate(where):
                scattered[i % len(scattered)][g] += turned[:, i * orb : (i + 1) * orb]
        return carry

    def one_step(step, carry):
        for ref in scattered:
            ref[...] = jnp.zeros_like(ref)
        lax.fori_loop(0, tiles // n_row, functools.partial(row_group, step), 0)
        total = straight[...]
        for ref in scattered:
            total += ref[...]
        later = step > 0
        total = jnp.where(later, 2.0, 1.0) * total - jnp.where(later, 1.0, 0.0) * prev[...]
        prev[...] = now[...]
        now[...] = total
        z[...] = total.astype(z.dtype)
        return carry

    lax.fori_loop(0, DEG, one_step, 0)
    for p in range(pieces):
        for b in range(per_piece):
            g = p * per_piece + b
            out_ref[p, 0, :, b * orb : (b + 1) * orb] = now[g].astype(out_ref.dtype)
            out_ref[p, 1, :, b * orb : (b + 1) * orb] = prev[g].astype(out_ref.dtype)


def gather_tiles(own, n_col, n_row):
    col, row = lax.axis_index("col"), lax.axis_index("row")
    index = lambda c, r: c * n_row + r

    def send(buf, pairs):
        return lax.ppermute(buf, LANES, pairs)

    held = [(own, 0, 0)]
    for sign in (1, -1):
        buf = own
        for hop in range(1, n_row):
            pairs = []
            for r in range(n_row):
                source = r - sign * (hop - 1)
                if 0 <= r + sign < n_row and 0 <= source < n_row:
                    pairs += [(index(c, r), index(c, r + sign)) for c in range(n_col)]
            buf = send(buf, pairs)
            held.append((buf, -sign * hop, 0))
    held.sort(key=lambda item: abs(item[1]))
    bit = n_col // 2
    while bit:
        for buf, shift, flips in list(held):
            pairs = [
                (index(c, r), index(c ^ bit, r))
                for c in range(n_col)
                for r in range(n_row)
                if 0 <= r + shift < n_row
            ]
            held.append((send(buf, pairs), shift, flips | bit))
        bit //= 2
    where = []
    for _, shift, flips in held:
        r = row + shift
        where.append(jnp.where((r >= 0) & (r < n_row), (col ^ flips) * n_row + r, -1))
    return [buf for buf, _, _ in held], jnp.stack(where).astype(jnp.int32)


def gather_plan(vectors, blocks, cols):
    n_dev = lax.axis_size(LANES)
    n_col, n_row = lax.axis_size("col"), lax.axis_size("row")
    rows, width = vectors.shape
    slots, orb = blocks.shape[2:4]
    share = width // n_dev
    per_piece = rows // orb
    n_blocks = n_dev * per_piece

    bufs, where = gather_tiles(blocks[0, 0], n_col, n_row)

    turned = vectors.T.reshape(n_dev, share, rows)
    own_ids = jnp.pad(cols[0, 0].astype(jnp.bfloat16), (0, rows - slots))
    own_ids = jnp.broadcast_to(own_ids, (n_dev, share, rows))
    both = lax.all_to_all(
        jnp.concatenate([turned, own_ids], axis=1), LANES, split_axis=0, concat_axis=0, tiled=True
    )
    zt = both[:, :share]
    local = both[:, share, :slots].astype(jnp.int32)
    down = (jnp.arange(n_dev, dtype=jnp.int32) % n_row)[:, None]
    ids = (local // per_piece * n_row + down) * per_piece + local % per_piece

    done = pl.pallas_call(
        functools.partial(filter_kernel, per_piece, n_row, len(bufs)),
        out_shape=jax.ShapeDtypeStruct((n_dev, 2, share, rows), jnp.bfloat16),
        in_specs=[
            pl.BlockSpec(memory_space=pltpu.SMEM),
            pl.BlockSpec(memory_space=pltpu.SMEM),
            pl.BlockSpec(memory_space=pltpu.VMEM),
        ]
        + [pl.BlockSpec(memory_space=pl.ANY)] * len(bufs),
        out_specs=pl.BlockSpec(memory_space=pltpu.VMEM),
        scratch_shapes=[
            pltpu.VMEM((n_dev, slots, orb, orb), blocks.dtype),
            pltpu.VMEM((n_blocks, share, orb), jnp.bfloat16),
            *[pltpu.VMEM((n_blocks, share, orb), jnp.float32)] * (3 + SPLIT),
            pltpu.SemaphoreType.DMA((n_dev,)),
        ],
        compiler_params=pltpu.CompilerParams(vmem_limit_bytes=32 * 2**20),
    )(ids, where, zt, *bufs)
    back = lax.all_to_all(done, LANES, split_axis=0, concat_axis=0, tiled=True)
    outs = jnp.transpose(back, (1, 3, 0, 2)).reshape(2, rows, width).astype(jnp.float32)
    return outs[0], outs[1]


def per_device(vectors, blocks, cols):
    n_dev = lax.axis_size(LANES)
    if n_dev * blocks.size * blocks.dtype.itemsize <= GATHER_LIMIT:
        return gather_plan(vectors, blocks, cols)
    return spread_plan(vectors, blocks, cols)


def solution(mesh):
    return jax.shard_map(
        per_device,
        mesh=mesh,
        in_specs=(
            P(("col", "row"), "dom"),
            P(("dom", "col"), "row", None, None, None),
            P(("dom", "col"), "row", None),
        ),
        out_specs=(P(("col", "row"), "dom"), P(("col", "row"), "dom")),
        check_vma=False,
    )
```

```python
import functools

import jax
import jax.numpy as jnp
from jax import lax
from jax.experimental import pallas as pl
from jax.experimental.pallas import tpu as pltpu
from jax.sharding import PartitionSpec as P

PER_ROW = 2
DEG = 4
SPLIT = 4
GATHER_LIMIT = 12 * 2**20
LANES = ("col", "row")


def onehot_sum(selected, high_part, low_part):
    first = jnp.einsum("su,sok->uok", selected, high_part, preferred_element_type=jnp.float32)
    second = jnp.einsum("su,sok->uok", selected, low_part, preferred_element_type=jnp.float32)
    return first + second


def apply_pair(send, grouped, col_ids, onehot):
    tile_rows, per_row, orb, _ = grouped.shape
    piece_rows, width = send.shape
    tile_cols = onehot.shape[1]
    wide = lax.all_gather(send, "col", axis=0, tiled=True).reshape(tile_cols, orb, width)
    picked = jnp.take(wide, col_ids, axis=0).reshape(tile_rows, per_row, orb, width)
    direct = jnp.einsum("tpio,tpok->tik", grouped, picked, preferred_element_type=jnp.float32)
    part_rows = lax.psum_scatter(
        direct.reshape(tile_rows * orb, width).astype(jnp.bfloat16),
        "row",
        scatter_dimension=0,
        tiled=True,
    ).astype(jnp.float32)
    tall = lax.all_gather(send, "row", axis=0, tiled=True).reshape(tile_rows, orb, width)
    mirrored = jnp.einsum("tpio,tik->tpok", grouped, tall, preferred_element_type=jnp.float32)
    mirrored = mirrored.reshape(tile_rows * per_row, orb, width)
    high_part = mirrored.astype(jnp.bfloat16)
    low_part = (mirrored - high_part.astype(jnp.float32)).astype(jnp.bfloat16)
    summed = onehot_sum(onehot, high_part, low_part)
    part_cols = lax.psum_scatter(
        summed.reshape(tile_cols * orb, width).astype(jnp.bfloat16),
        "col",
        scatter_dimension=0,
        tiled=True,
    ).astype(jnp.float32)
    return part_rows + part_cols


def spread_plan(vectors, blocks, cols):
    tiles = blocks[0, 0]
    col_ids = cols[0, 0]
    slots, orb, _ = tiles.shape
    tile_rows = slots // PER_ROW
    tile_cols = lax.axis_size("col") * (vectors.shape[0] // orb)
    grouped = tiles.reshape(tile_rows, PER_ROW, orb, orb)
    onehot = (col_ids[:, None] == jnp.arange(tile_cols, dtype=jnp.int32)[None, :]).astype(
        jnp.bfloat16
    )
    prev = vectors.astype(jnp.float32)
    now = apply_pair(vectors, grouped, col_ids, onehot)
    for step in range(DEG - 1):
        nxt = 2.0 * apply_pair(now.astype(jnp.bfloat16), grouped, col_ids, onehot) - prev
        prev, now = (now, nxt)
    return (now, prev)


def filter_kernel(per_piece, n_row, starts, ids_ref, where_ref, zt_ref, *refs):
    bufs, (out_ref, s_ref, z, now, prev, straight, *scattered, sems) = refs[: len(starts)], refs[len(starts) :]
    tiles, slots = s_ref.shape[:2]
    orb = s_ref.shape[2]
    tile_rows = slots // PER_ROW
    pieces = zt_ref.shape[0]

    copies = []
    for i, (buf, start) in enumerate(zip(bufs, starts)):
        place = s_ref.at[where_ref[i], pl.ds(start, buf.shape[0])]
        copies.append(pltpu.make_async_copy(buf, place, sems.at[i]))
        copies[-1].start()

    for p in range(pieces):
        for b in range(per_piece):
            own = zt_ref[p, :, b * orb : (b + 1) * orb]
            z[p * per_piece + b] = own
            now[p * per_piece + b] = own.astype(jnp.float32)
    prev[...] = jnp.zeros_like(prev)

    for copy in copies:
        copy.wait()

    def row_group(across, carry):
        group = [across * n_row + r for r in range(n_row)]
        for t in range(tile_rows):
            places = [(tile, t * PER_ROW + p) for tile in group for p in range(PER_ROW)]
            strip = jnp.concatenate([s_ref[tile, slot] for tile, slot in places], axis=1)
            where = [ids_ref[tile, slot] for tile, slot in places]
            wide = jnp.concatenate([z[g] for g in where], axis=1)
            tall = z[across * tile_rows + t]
            straight[across * tile_rows + t] = lax.dot_general(
                wide, strip, (((1,), (1,)), ((), ())), preferred_element_type=jnp.float32
            )
            turned = jnp.dot(tall, strip, preferred_element_type=jnp.float32)
            for i, g in enumerate(where):
                scattered[i % len(scattered)][g] += turned[:, i * orb : (i + 1) * orb]
        return carry

    def one_step(step, carry):
        for ref in scattered:
            ref[...] = jnp.zeros_like(ref)
        lax.fori_loop(0, tiles // n_row, row_group, 0)
        total = straight[...]
        for ref in scattered:
            total += ref[...]
        later = step > 0
        total = jnp.where(later, 2.0, 1.0) * total - jnp.where(later, 1.0, 0.0) * prev[...]
        prev[...] = now[...]
        now[...] = total
        z[...] = total.astype(z.dtype)
        return carry

    lax.fori_loop(0, DEG, one_step, 0)
    for p in range(pieces):
        for b in range(per_piece):
            g = p * per_piece + b
            out_ref[p, 0, :, b * orb : (b + 1) * orb] = now[g].astype(out_ref.dtype)
            out_ref[p, 1, :, b * orb : (b + 1) * orb] = prev[g].astype(out_ref.dtype)


def gather_tiles(own, n_col, n_row):
    col, row = lax.axis_index("col"), lax.axis_index("row")
    half = own.shape[0] // 2

    def send(buf, flip_col, flip_row):
        pairs = [
            (c * n_row + r, (c ^ flip_col) * n_row + (r ^ flip_row))
            for c in range(n_col)
            for r in range(n_row)
        ]
        return lax.ppermute(buf, LANES, pairs)

    near = send(own, 0, 1)
    over_own = send(own, 2, 0)
    far = send(own, 0, 3)
    over_near = send(near, 2, 0)
    last = send(far, 0, 1)
    over_far = send(far, 2, 0)
    over_last = send(last[:half], 2, 0)
    side_last = send(over_far[half:], 0, 1)
    held = [
        (own, 0, 0, 0),
        (near, 0, 1, 0),
        (over_own, 2, 0, 0),
        (far, 0, 3, 0),
        (over_near, 2, 1, 0),
        (last, 0, 2, 0),
        (over_far, 2, 3, 0),
        (over_last, 2, 2, 0),
        (side_last, 2, 2, half),
    ]
    held += [(send(buf, 1, 0), c ^ 1, r, slot) for buf, c, r, slot in held]
    where = jnp.stack([(col ^ c) * n_row + (row ^ r) for _, c, r, _ in held]).astype(jnp.int32)
    return [buf for buf, _, _, _ in held], [slot for _, _, _, slot in held], where


def gather_plan(vectors, blocks, cols):
    n_dev = lax.axis_size(LANES)
    n_col, n_row = lax.axis_size("col"), lax.axis_size("row")
    rows, width = vectors.shape
    slots, orb = blocks.shape[2:4]
    share = width // n_dev
    per_piece = rows // orb
    n_blocks = n_dev * per_piece

    bufs, starts, where = gather_tiles(blocks[0, 0], n_col, n_row)

    turned = vectors.T.reshape(n_dev, share, rows)
    own_ids = jnp.pad(cols[0, 0].astype(jnp.bfloat16), (0, rows - slots))
    own_ids = jnp.broadcast_to(own_ids, (n_dev, share, rows))
    both = lax.all_to_all(
        jnp.concatenate([turned, own_ids], axis=1), LANES, split_axis=0, concat_axis=0, tiled=True
    )
    zt = both[:, :share]
    local = both[:, share, :slots].astype(jnp.int32)
    down = (jnp.arange(n_dev, dtype=jnp.int32) % n_row)[:, None]
    ids = (local // per_piece * n_row + down) * per_piece + local % per_piece

    done = pl.pallas_call(
        functools.partial(filter_kernel, per_piece, n_row, starts),
        out_shape=jax.ShapeDtypeStruct((n_dev, 2, share, rows), jnp.bfloat16),
        in_specs=[
            pl.BlockSpec(memory_space=pltpu.SMEM),
            pl.BlockSpec(memory_space=pltpu.SMEM),
            pl.BlockSpec(memory_space=pltpu.VMEM),
        ]
        + [pl.BlockSpec(memory_space=pl.ANY)] * len(bufs),
        out_specs=pl.BlockSpec(memory_space=pltpu.VMEM),
        scratch_shapes=[
            pltpu.VMEM((n_dev, slots, orb, orb), blocks.dtype),
            pltpu.VMEM((n_blocks, share, orb), jnp.bfloat16),
            *[pltpu.VMEM((n_blocks, share, orb), jnp.float32)] * (3 + SPLIT),
            pltpu.SemaphoreType.DMA((len(bufs),)),
        ],
        compiler_params=pltpu.CompilerParams(vmem_limit_bytes=32 * 2**20),
    )(ids, where, zt, *bufs)
    back = lax.all_to_all(done, LANES, split_axis=0, concat_axis=0, tiled=True)
    outs = jnp.transpose(back, (1, 3, 0, 2)).reshape(2, rows, width).astype(jnp.float32)
    return outs[0], outs[1]


def per_device(vectors, blocks, cols):
    n_dev = lax.axis_size(LANES)
    line_of_four = lax.axis_size("col") == 4 and lax.axis_size("row") == 4
    if line_of_four and n_dev * blocks.size * blocks.dtype.itemsize <= GATHER_LIMIT:
        return gather_plan(vectors, blocks, cols)
    return spread_plan(vectors, blocks, cols)


def solution(mesh):
    return jax.shard_map(
        per_device,
        mesh=mesh,
        in_specs=(
            P(("col", "row"), "dom"),
            P(("dom", "col"), "row", None, None, None),
            P(("dom", "col"), "row", None),
        ),
        out_specs=(P(("col", "row"), "dom"), P(("col", "row"), "dom")),
        check_vma=False,
    )
```

```python
import functools

import jax
import jax.numpy as jnp
from jax import lax
from jax.experimental import pallas as pl
from jax.experimental.pallas import tpu as pltpu
from jax.sharding import PartitionSpec as P

PER_ROW = 2
DEG = 4
SPLIT = 4
GATHER_LIMIT = 12 * 2**20
LANES = ("col", "row")


def onehot_sum(selected, high_part, low_part):
    first = jnp.einsum("su,sok->uok", selected, high_part, preferred_element_type=jnp.float32)
    second = jnp.einsum("su,sok->uok", selected, low_part, preferred_element_type=jnp.float32)
    return first + second


def apply_pair(send, grouped, col_ids, onehot):
    tile_rows, per_row, orb, _ = grouped.shape
    piece_rows, width = send.shape
    tile_cols = onehot.shape[1]
    wide = lax.all_gather(send, "col", axis=0, tiled=True).reshape(tile_cols, orb, width)
    picked = jnp.take(wide, col_ids, axis=0).reshape(tile_rows, per_row, orb, width)
    direct = jnp.einsum("tpio,tpok->tik", grouped, picked, preferred_element_type=jnp.float32)
    part_rows = lax.psum_scatter(
        direct.reshape(tile_rows * orb, width).astype(jnp.bfloat16),
        "row",
        scatter_dimension=0,
        tiled=True,
    ).astype(jnp.float32)
    tall = lax.all_gather(send, "row", axis=0, tiled=True).reshape(tile_rows, orb, width)
    mirrored = jnp.einsum("tpio,tik->tpok", grouped, tall, preferred_element_type=jnp.float32)
    mirrored = mirrored.reshape(tile_rows * per_row, orb, width)
    high_part = mirrored.astype(jnp.bfloat16)
    low_part = (mirrored - high_part.astype(jnp.float32)).astype(jnp.bfloat16)
    summed = onehot_sum(onehot, high_part, low_part)
    part_cols = lax.psum_scatter(
        summed.reshape(tile_cols * orb, width).astype(jnp.bfloat16),
        "col",
        scatter_dimension=0,
        tiled=True,
    ).astype(jnp.float32)
    return part_rows + part_cols


def spread_plan(vectors, blocks, cols):
    tiles = blocks[0, 0]
    col_ids = cols[0, 0]
    slots, orb, _ = tiles.shape
    tile_rows = slots // PER_ROW
    tile_cols = lax.axis_size("col") * (vectors.shape[0] // orb)
    grouped = tiles.reshape(tile_rows, PER_ROW, orb, orb)
    onehot = (col_ids[:, None] == jnp.arange(tile_cols, dtype=jnp.int32)[None, :]).astype(
        jnp.bfloat16
    )
    prev = vectors.astype(jnp.float32)
    now = apply_pair(vectors, grouped, col_ids, onehot)
    for step in range(DEG - 1):
        nxt = 2.0 * apply_pair(now.astype(jnp.bfloat16), grouped, col_ids, onehot) - prev
        prev, now = (now, nxt)
    return (now, prev)


def filter_kernel(per_piece, n_row, starts, ids_ref, where_ref, zt_ref, *refs):
    bufs, (out_ref, s_ref, z, now, prev, straight, *scattered, sems) = refs[: len(starts)], refs[len(starts) :]
    tiles, slots = s_ref.shape[:2]
    orb = s_ref.shape[2]
    tile_rows = slots // PER_ROW
    pieces = zt_ref.shape[0]

    copies = []
    for i, (buf, start) in enumerate(zip(bufs, starts)):
        place = s_ref.at[where_ref[i], pl.ds(start, buf.shape[0])]
        copies.append(pltpu.make_async_copy(buf, place, sems.at[i]))
        copies[-1].start()

    for p in range(pieces):
        for b in range(per_piece):
            own = zt_ref[p, :, b * orb : (b + 1) * orb]
            z[p * per_piece + b] = own
            now[p * per_piece + b] = own.astype(jnp.float32)
    prev[...] = jnp.zeros_like(prev)

    for copy in copies:
        copy.wait()

    def row_group(across, carry):
        group = [across * n_row + r for r in range(n_row)]
        for t in range(tile_rows):
            places = [(tile, t * PER_ROW + p) for tile in group for p in range(PER_ROW)]
            strip = jnp.concatenate([s_ref[tile, slot] for tile, slot in places], axis=1)
            where = [ids_ref[tile, slot] for tile, slot in places]
            wide = jnp.concatenate([z[g] for g in where], axis=1)
            tall = z[across * tile_rows + t]
            straight[across * tile_rows + t] = lax.dot_general(
                wide, strip, (((1,), (1,)), ((), ())), preferred_element_type=jnp.float32
            )
            turned = jnp.dot(tall, strip, preferred_element_type=jnp.float32)
            for i, g in enumerate(where):
                scattered[i % len(scattered)][g] += turned[:, i * orb : (i + 1) * orb]
        return carry

    def one_step(step, carry):
        for ref in scattered:
            ref[...] = jnp.zeros_like(ref)
        lax.fori_loop(0, tiles // n_row, row_group, 0)
        total = straight[...]
        for ref in scattered:
            total += ref[...]
        later = step > 0
        total = jnp.where(later, 2.0, 1.0) * total - jnp.where(later, 1.0, 0.0) * prev[...]
        prev[...] = now[...]
        now[...] = total
        z[...] = total.astype(z.dtype)
        return carry

    lax.fori_loop(0, DEG, one_step, 0)
    for p in range(pieces):
        for b in range(per_piece):
            g = p * per_piece + b
            out_ref[p, 0, :, b * orb : (b + 1) * orb] = now[g].astype(out_ref.dtype)
            out_ref[p, 1, :, b * orb : (b + 1) * orb] = prev[g].astype(out_ref.dtype)


def nothing(*refs):
    pass


def after(value, *others):
    return pl.pallas_call(
        nothing,
        out_shape=jax.ShapeDtypeStruct(value.shape, value.dtype),
        in_specs=[pl.BlockSpec(memory_space=pl.ANY)] * (1 + len(others)),
        out_specs=pl.BlockSpec(memory_space=pl.ANY),
        input_output_aliases={0: 0},
        compiler_params=pltpu.CompilerParams(vmem_limit_bytes=2**20),
    )(value, *others)


def gather_tiles(own, n_col, n_row, meanwhile):
    col, row = lax.axis_index("col"), lax.axis_index("row")
    half = own.shape[0] // 2

    def send(buf, flip_col, flip_row):
        pairs = [
            (c * n_row + r, (c ^ flip_col) * n_row + (r ^ flip_row))
            for c in range(n_col)
            for r in range(n_row)
        ]
        return lax.ppermute(buf, LANES, pairs)

    def to_mate(*bufs):
        return [send(buf, 1, 0) for buf in bufs]

    over_own = send(own, 2, 0)
    near = send(own, 0, 1)
    far = send(own, 0, 3)
    near = after(near, over_own)
    over_near = send(near, 2, 0)
    mates = to_mate(own, near, over_own)
    far = after(far, over_near, *mates)
    over_far = send(far, 2, 0)
    last = send(far, 0, 1)
    mates += to_mate(far, over_near)
    other = meanwhile(over_near)
    last = after(last, over_far, other, *mates[3:])
    over_last = send(last[:half], 2, 0)
    side_last = send(over_far[half:], 0, 1)
    mates += to_mate(last, over_far, over_last, side_last)
    held = [
        (own, 0, 0, 0),
        (near, 0, 1, 0),
        (over_own, 2, 0, 0),
        (far, 0, 3, 0),
        (over_near, 2, 1, 0),
        (last, 0, 2, 0),
        (over_far, 2, 3, 0),
        (over_last, 2, 2, 0),
        (side_last, 2, 2, half),
    ]
    held += [(buf, c ^ 1, r, slot) for buf, (_, c, r, slot) in zip(mates, held)]
    where = jnp.stack([(col ^ c) * n_row + (row ^ r) for _, c, r, _ in held]).astype(jnp.int32)
    return [buf for buf, _, _, _ in held], [slot for _, _, _, slot in held], where, other


def gather_plan(vectors, blocks, cols):
    n_dev = lax.axis_size(LANES)
    n_col, n_row = lax.axis_size("col"), lax.axis_size("row")
    rows, width = vectors.shape
    slots, orb = blocks.shape[2:4]
    share = width // n_dev
    per_piece = rows // orb
    n_blocks = n_dev * per_piece

    def exchange(ready):
        turned = after(vectors, ready).T.reshape(n_dev, share, rows)
        own_ids = jnp.pad(cols[0, 0].astype(jnp.bfloat16), (0, rows - slots))
        own_ids = jnp.broadcast_to(own_ids, (n_dev, share, rows))
        both = jnp.concatenate([turned, own_ids], axis=1)
        return lax.all_to_all(both, LANES, split_axis=0, concat_axis=0, tiled=True)

    bufs, starts, where, both = gather_tiles(blocks[0, 0], n_col, n_row, exchange)
    zt = both[:, :share]
    local = both[:, share, :slots].astype(jnp.int32)
    down = (jnp.arange(n_dev, dtype=jnp.int32) % n_row)[:, None]
    ids = (local // per_piece * n_row + down) * per_piece + local % per_piece

    done = pl.pallas_call(
        functools.partial(filter_kernel, per_piece, n_row, starts),
        out_shape=jax.ShapeDtypeStruct((n_dev, 2, share, rows), jnp.bfloat16),
        in_specs=[
            pl.BlockSpec(memory_space=pltpu.SMEM),
            pl.BlockSpec(memory_space=pltpu.SMEM),
            pl.BlockSpec(memory_space=pltpu.VMEM),
        ]
        + [pl.BlockSpec(memory_space=pl.ANY)] * len(bufs),
        out_specs=pl.BlockSpec(memory_space=pltpu.VMEM),
        scratch_shapes=[
            pltpu.VMEM((n_dev, slots, orb, orb), blocks.dtype),
            pltpu.VMEM((n_blocks, share, orb), jnp.bfloat16),
            *[pltpu.VMEM((n_blocks, share, orb), jnp.float32)] * (3 + SPLIT),
            pltpu.SemaphoreType.DMA((len(bufs),)),
        ],
        compiler_params=pltpu.CompilerParams(vmem_limit_bytes=32 * 2**20),
    )(ids, where, zt, *bufs)
    back = lax.all_to_all(done, LANES, split_axis=0, concat_axis=0, tiled=True)
    outs = jnp.transpose(back, (1, 3, 0, 2)).reshape(2, rows, width).astype(jnp.float32)
    return outs[0], outs[1]


def per_device(vectors, blocks, cols):
    n_dev = lax.axis_size(LANES)
    line_of_four = lax.axis_size("col") == 4 and lax.axis_size("row") == 4
    if line_of_four and n_dev * blocks.size * blocks.dtype.itemsize <= GATHER_LIMIT:
        return gather_plan(vectors, blocks, cols)
    return spread_plan(vectors, blocks, cols)


def solution(mesh):
    return jax.shard_map(
        per_device,
        mesh=mesh,
        in_specs=(
            P(("col", "row"), "dom"),
            P(("dom", "col"), "row", None, None, None),
            P(("dom", "col"), "row", None),
        ),
        out_specs=(P(("col", "row"), "dom"), P(("col", "row"), "dom")),
        check_vma=False,
    )
```

```python
import functools

import jax
import jax.numpy as jnp
from jax import lax
from jax.experimental import pallas as pl
from jax.experimental.pallas import tpu as pltpu
from jax.sharding import PartitionSpec as P

PER_ROW = 2
DEG = 4
SPLIT = 4
GATHER_LIMIT = 12 * 2**20
LANES = ("col", "row")


def onehot_sum(selected, high_part, low_part):
    first = jnp.einsum("su,sok->uok", selected, high_part, preferred_element_type=jnp.float32)
    second = jnp.einsum("su,sok->uok", selected, low_part, preferred_element_type=jnp.float32)
    return first + second


def apply_pair(send, grouped, col_ids, onehot):
    tile_rows, per_row, orb, _ = grouped.shape
    piece_rows, width = send.shape
    tile_cols = onehot.shape[1]
    wide = lax.all_gather(send, "col", axis=0, tiled=True).reshape(tile_cols, orb, width)
    picked = jnp.take(wide, col_ids, axis=0).reshape(tile_rows, per_row, orb, width)
    direct = jnp.einsum("tpio,tpok->tik", grouped, picked, preferred_element_type=jnp.float32)
    part_rows = lax.psum_scatter(
        direct.reshape(tile_rows * orb, width).astype(jnp.bfloat16),
        "row",
        scatter_dimension=0,
        tiled=True,
    ).astype(jnp.float32)
    tall = lax.all_gather(send, "row", axis=0, tiled=True).reshape(tile_rows, orb, width)
    mirrored = jnp.einsum("tpio,tik->tpok", grouped, tall, preferred_element_type=jnp.float32)
    mirrored = mirrored.reshape(tile_rows * per_row, orb, width)
    high_part = mirrored.astype(jnp.bfloat16)
    low_part = (mirrored - high_part.astype(jnp.float32)).astype(jnp.bfloat16)
    summed = onehot_sum(onehot, high_part, low_part)
    part_cols = lax.psum_scatter(
        summed.reshape(tile_cols * orb, width).astype(jnp.bfloat16),
        "col",
        scatter_dimension=0,
        tiled=True,
    ).astype(jnp.float32)
    return part_rows + part_cols


def spread_plan(vectors, blocks, cols):
    tiles = blocks[0, 0]
    col_ids = cols[0, 0]
    slots, orb, _ = tiles.shape
    tile_rows = slots // PER_ROW
    tile_cols = lax.axis_size("col") * (vectors.shape[0] // orb)
    grouped = tiles.reshape(tile_rows, PER_ROW, orb, orb)
    onehot = (col_ids[:, None] == jnp.arange(tile_cols, dtype=jnp.int32)[None, :]).astype(
        jnp.bfloat16
    )
    prev = vectors.astype(jnp.float32)
    now = apply_pair(vectors, grouped, col_ids, onehot)
    for step in range(DEG - 1):
        nxt = 2.0 * apply_pair(now.astype(jnp.bfloat16), grouped, col_ids, onehot) - prev
        prev, now = (now, nxt)
    return (now, prev)


def filter_kernel(per_piece, n_row, starts, ids_ref, where_ref, zt_ref, *refs):
    bufs, (out_ref, s_ref, z, now, prev, straight, *scattered, sems) = refs[: len(starts)], refs[len(starts) :]
    tiles, slots = s_ref.shape[:2]
    orb = s_ref.shape[2]
    share = z.shape[1]
    tile_rows = slots // PER_ROW
    pieces = zt_ref.shape[0]

    for buf, start, i in zip(bufs, starts, range(len(bufs))):
        tile = where_ref[i]
        pltpu.make_async_copy(buf, s_ref.at[tile, pl.ds(start, buf.shape[0])], sems.at[tile]).start()

    for p in range(pieces):
        for b in range(per_piece):
            own = zt_ref[p, :, b * orb : (b + 1) * orb]
            z[p * per_piece + b] = own
            now[p * per_piece + b] = own.astype(jnp.float32)
    prev[...] = jnp.zeros_like(prev)

    def row_group(step, across, carry):
        group = [across * n_row + r for r in range(n_row)]

        @pl.when(step == 0)
        def _():
            for tile in group:
                pltpu.make_async_copy(s_ref.at[tile], s_ref.at[tile], sems.at[tile]).wait()

        for t in range(0, tile_rows, 2):
            strips, wides, where = [], [], []
            for row in (t, t + 1):
                places = [(tile, row * PER_ROW + p) for tile in group for p in range(PER_ROW)]
                strips.append(jnp.concatenate([s_ref[tile, slot] for tile, slot in places], axis=1))
                where.append([ids_ref[tile, slot] for tile, slot in places])
                wides.append(jnp.concatenate([z[g] for g in where[-1]], axis=1))
            strip = jnp.concatenate(strips, axis=0)
            wide = jnp.concatenate(wides, axis=0)
            base = across * tile_rows + t
            none = jnp.zeros((share, orb), z.dtype)
            tall = jnp.concatenate(
                [
                    jnp.concatenate([z[base], none], axis=1),
                    jnp.concatenate([none, z[base + 1]], axis=1),
                ],
                axis=0,
            )
            direct = lax.dot_general(
                wide, strip, (((1,), (1,)), ((), ())), preferred_element_type=jnp.float32
            )
            turned = jnp.dot(tall, strip, preferred_element_type=jnp.float32)
            for k in range(2):
                rows = slice(k * share, (k + 1) * share)
                straight[base + k] = direct[rows, k * orb : (k + 1) * orb]
                for i, g in enumerate(where[k]):
                    scattered[i % len(scattered)][g] += turned[rows, i * orb : (i + 1) * orb]
        return carry

    def one_step(step, carry):
        for ref in scattered:
            ref[...] = jnp.zeros_like(ref)
        lax.fori_loop(0, tiles // n_row, functools.partial(row_group, step), 0)
        total = straight[...]
        for ref in scattered:
            total += ref[...]
        later = step > 0
        total = jnp.where(later, 2.0, 1.0) * total - jnp.where(later, 1.0, 0.0) * prev[...]
        prev[...] = now[...]
        now[...] = total
        z[...] = total.astype(z.dtype)
        return carry

    lax.fori_loop(0, DEG, one_step, 0)
    for p in range(pieces):
        for b in range(per_piece):
            g = p * per_piece + b
            out_ref[p, 0, :, b * orb : (b + 1) * orb] = now[g].astype(out_ref.dtype)
            out_ref[p, 1, :, b * orb : (b + 1) * orb] = prev[g].astype(out_ref.dtype)


def gather_tiles(own, n_col, n_row):
    col, row = lax.axis_index("col"), lax.axis_index("row")
    half = own.shape[0] // 2

    def send(buf, flip_col, flip_row):
        pairs = [
            (c * n_row + r, (c ^ flip_col) * n_row + (r ^ flip_row))
            for c in range(n_col)
            for r in range(n_row)
        ]
        return lax.ppermute(buf, LANES, pairs)

    near = send(own, 0, 1)
    over_own = send(own, 2, 0)
    far = send(own, 0, 3)
    over_near = send(near, 2, 0)
    last = send(far, 0, 1)
    over_far = send(far, 2, 0)
    over_last = send(last[:half], 2, 0)
    side_last = send(over_far[half:], 0, 1)
    held = [
        (own, 0, 0, 0),
        (near, 0, 1, 0),
        (over_own, 2, 0, 0),
        (far, 0, 3, 0),
        (over_near, 2, 1, 0),
        (last, 0, 2, 0),
        (over_far, 2, 3, 0),
        (over_last, 2, 2, 0),
        (side_last, 2, 2, half),
    ]
    held += [(send(buf, 1, 0), c ^ 1, r, slot) for buf, c, r, slot in held]
    where = jnp.stack([(col ^ c) * n_row + (row ^ r) for _, c, r, _ in held]).astype(jnp.int32)
    return [buf for buf, _, _, _ in held], [slot for _, _, _, slot in held], where


def gather_plan(vectors, blocks, cols):
    n_dev = lax.axis_size(LANES)
    n_col, n_row = lax.axis_size("col"), lax.axis_size("row")
    rows, width = vectors.shape
    slots, orb = blocks.shape[2:4]
    share = width // n_dev
    per_piece = rows // orb
    n_blocks = n_dev * per_piece

    bufs, starts, where = gather_tiles(blocks[0, 0], n_col, n_row)

    turned = vectors.T.reshape(n_dev, share, rows)
    own_ids = jnp.pad(cols[0, 0].astype(jnp.bfloat16), (0, rows - slots))
    own_ids = jnp.broadcast_to(own_ids, (n_dev, share, rows))
    both = lax.all_to_all(
        jnp.concatenate([turned, own_ids], axis=1), LANES, split_axis=0, concat_axis=0, tiled=True
    )
    zt = both[:, :share]
    local = both[:, share, :slots].astype(jnp.int32)
    down = (jnp.arange(n_dev, dtype=jnp.int32) % n_row)[:, None]
    ids = (local // per_piece * n_row + down) * per_piece + local % per_piece

    done = pl.pallas_call(
        functools.partial(filter_kernel, per_piece, n_row, starts),
        out_shape=jax.ShapeDtypeStruct((n_dev, 2, share, rows), jnp.bfloat16),
        in_specs=[
            pl.BlockSpec(memory_space=pltpu.SMEM),
            pl.BlockSpec(memory_space=pltpu.SMEM),
            pl.BlockSpec(memory_space=pltpu.VMEM),
        ]
        + [pl.BlockSpec(memory_space=pl.ANY)] * len(bufs),
        out_specs=pl.BlockSpec(memory_space=pltpu.VMEM),
        scratch_shapes=[
            pltpu.VMEM((n_dev, slots, orb, orb), blocks.dtype),
            pltpu.VMEM((n_blocks, share, orb), jnp.bfloat16),
            *[pltpu.VMEM((n_blocks, share, orb), jnp.float32)] * (3 + SPLIT),
            pltpu.SemaphoreType.DMA((n_dev,)),
        ],
        compiler_params=pltpu.CompilerParams(vmem_limit_bytes=32 * 2**20),
    )(ids, where, zt, *bufs)
    back = lax.all_to_all(done, LANES, split_axis=0, concat_axis=0, tiled=True)
    outs = jnp.transpose(back, (1, 3, 0, 2)).reshape(2, rows, width).astype(jnp.float32)
    return outs[0], outs[1]


def per_device(vectors, blocks, cols):
    n_dev = lax.axis_size(LANES)
    line_of_four = lax.axis_size("col") == 4 and lax.axis_size("row") == 4
    if line_of_four and n_dev * blocks.size * blocks.dtype.itemsize <= GATHER_LIMIT:
        return gather_plan(vectors, blocks, cols)
    return spread_plan(vectors, blocks, cols)


def solution(mesh):
    return jax.shard_map(
        per_device,
        mesh=mesh,
        in_specs=(
            P(("col", "row"), "dom"),
            P(("dom", "col"), "row", None, None, None),
            P(("dom", "col"), "row", None),
        ),
        out_specs=(P(("col", "row"), "dom"), P(("col", "row"), "dom")),
        check_vma=False,
    )
```

```python
import functools

import jax
import jax.numpy as jnp
from jax import lax
from jax.experimental import pallas as pl
from jax.experimental.pallas import tpu as pltpu
from jax.sharding import PartitionSpec as P

PER_ROW = 2
DEG = 4
SPLIT = 4
GATHER_LIMIT = 12 * 2**20
LANES = ("col", "row")


def onehot_sum(selected, high_part, low_part):
    first = jnp.einsum("su,sok->uok", selected, high_part, preferred_element_type=jnp.float32)
    second = jnp.einsum("su,sok->uok", selected, low_part, preferred_element_type=jnp.float32)
    return first + second


def apply_pair(send, grouped, col_ids, onehot):
    tile_rows, per_row, orb, _ = grouped.shape
    piece_rows, width = send.shape
    tile_cols = onehot.shape[1]
    wide = lax.all_gather(send, "col", axis=0, tiled=True).reshape(tile_cols, orb, width)
    picked = jnp.take(wide, col_ids, axis=0).reshape(tile_rows, per_row, orb, width)
    direct = jnp.einsum("tpio,tpok->tik", grouped, picked, preferred_element_type=jnp.float32)
    part_rows = lax.psum_scatter(
        direct.reshape(tile_rows * orb, width).astype(jnp.bfloat16),
        "row",
        scatter_dimension=0,
        tiled=True,
    ).astype(jnp.float32)
    tall = lax.all_gather(send, "row", axis=0, tiled=True).reshape(tile_rows, orb, width)
    mirrored = jnp.einsum("tpio,tik->tpok", grouped, tall, preferred_element_type=jnp.float32)
    mirrored = mirrored.reshape(tile_rows * per_row, orb, width)
    high_part = mirrored.astype(jnp.bfloat16)
    low_part = (mirrored - high_part.astype(jnp.float32)).astype(jnp.bfloat16)
    summed = onehot_sum(onehot, high_part, low_part)
    part_cols = lax.psum_scatter(
        summed.reshape(tile_cols * orb, width).astype(jnp.bfloat16),
        "col",
        scatter_dimension=0,
        tiled=True,
    ).astype(jnp.float32)
    return part_rows + part_cols


def spread_plan(vectors, blocks, cols):
    tiles = blocks[0, 0]
    col_ids = cols[0, 0]
    slots, orb, _ = tiles.shape
    tile_rows = slots // PER_ROW
    tile_cols = lax.axis_size("col") * (vectors.shape[0] // orb)
    grouped = tiles.reshape(tile_rows, PER_ROW, orb, orb)
    onehot = (col_ids[:, None] == jnp.arange(tile_cols, dtype=jnp.int32)[None, :]).astype(
        jnp.bfloat16
    )
    prev = vectors.astype(jnp.float32)
    now = apply_pair(vectors, grouped, col_ids, onehot)
    for step in range(DEG - 1):
        nxt = 2.0 * apply_pair(now.astype(jnp.bfloat16), grouped, col_ids, onehot) - prev
        prev, now = (now, nxt)
    return (now, prev)


def filter_kernel(per_piece, n_row, starts, ids_ref, where_ref, zt_ref, *refs):
    bufs, (out_ref, s_ref, st_ref, z, now, prev, straight, *scattered, sems) = refs[: len(starts)], refs[len(starts) :]
    tiles, slots = s_ref.shape[:2]
    orb = s_ref.shape[2]
    tile_rows = slots // PER_ROW
    pieces = zt_ref.shape[0]

    for buf, start, i in zip(bufs, starts, range(len(bufs))):
        tile = where_ref[i]
        pltpu.make_async_copy(buf, s_ref.at[tile, pl.ds(start, buf.shape[0])], sems.at[tile]).start()

    for p in range(pieces):
        for b in range(per_piece):
            own = zt_ref[p, :, b * orb : (b + 1) * orb]
            z[p * per_piece + b] = own
            now[p * per_piece + b] = own.astype(jnp.float32)
    prev[...] = jnp.zeros_like(prev)

    def row_group(step, across, carry):
        group = [across * n_row + r for r in range(n_row)]

        @pl.when(step == 0)
        def _():
            for tile in group:
                pltpu.make_async_copy(s_ref.at[tile], s_ref.at[tile], sems.at[tile]).wait()
                for slot in range(slots):
                    st_ref[tile, slot] = s_ref[tile, slot].T

        for t in range(tile_rows):
            places = [(tile, t * PER_ROW + p) for tile in group for p in range(PER_ROW)]
            strip = jnp.concatenate([s_ref[tile, slot] for tile, slot in places], axis=1)
            turned_strip = jnp.concatenate([st_ref[tile, slot] for tile, slot in places], axis=0)
            where = [ids_ref[tile, slot] for tile, slot in places]
            wide = jnp.concatenate([z[g] for g in where], axis=1)
            tall = z[across * tile_rows + t]
            straight[across * tile_rows + t] = jnp.dot(
                wide, turned_strip, preferred_element_type=jnp.float32
            )
            turned = jnp.dot(tall, strip, preferred_element_type=jnp.float32)
            for i, g in enumerate(where):
                scattered[i % len(scattered)][g] += turned[:, i * orb : (i + 1) * orb]
        return carry

    def one_step(step, carry):
        for ref in scattered:
            ref[...] = jnp.zeros_like(ref)
        lax.fori_loop(0, tiles // n_row, functools.partial(row_group, step), 0)
        total = straight[...]
        for ref in scattered:
            total += ref[...]
        later = step > 0
        total = jnp.where(later, 2.0, 1.0) * total - jnp.where(later, 1.0, 0.0) * prev[...]
        prev[...] = now[...]
        now[...] = total
        z[...] = total.astype(z.dtype)
        return carry

    lax.fori_loop(0, DEG, one_step, 0)
    for p in range(pieces):
        for b in range(per_piece):
            g = p * per_piece + b
            out_ref[p, 0, :, b * orb : (b + 1) * orb] = now[g].astype(out_ref.dtype)
            out_ref[p, 1, :, b * orb : (b + 1) * orb] = prev[g].astype(out_ref.dtype)


def gather_tiles(own, n_col, n_row):
    col, row = lax.axis_index("col"), lax.axis_index("row")
    half = own.shape[0] // 2

    def send(buf, flip_col, flip_row):
        pairs = [
            (c * n_row + r, (c ^ flip_col) * n_row + (r ^ flip_row))
            for c in range(n_col)
            for r in range(n_row)
        ]
        return lax.ppermute(buf, LANES, pairs)

    near = send(own, 0, 1)
    over_own = send(own, 2, 0)
    far = send(own, 0, 3)
    over_near = send(near, 2, 0)
    last = send(far, 0, 1)
    over_far = send(far, 2, 0)
    over_last = send(last[:half], 2, 0)
    side_last = send(over_far[half:], 0, 1)
    held = [
        (own, 0, 0, 0),
        (near, 0, 1, 0),
        (over_own, 2, 0, 0),
        (far, 0, 3, 0),
        (over_near, 2, 1, 0),
        (last, 0, 2, 0),
        (over_far, 2, 3, 0),
        (over_last, 2, 2, 0),
        (side_last, 2, 2, half),
    ]
    held += [(send(buf, 1, 0), c ^ 1, r, slot) for buf, c, r, slot in held]
    where = jnp.stack([(col ^ c) * n_row + (row ^ r) for _, c, r, _ in held]).astype(jnp.int32)
    return [buf for buf, _, _, _ in held], [slot for _, _, _, slot in held], where


def gather_plan(vectors, blocks, cols):
    n_dev = lax.axis_size(LANES)
    n_col, n_row = lax.axis_size("col"), lax.axis_size("row")
    rows, width = vectors.shape
    slots, orb = blocks.shape[2:4]
    share = width // n_dev
    per_piece = rows // orb
    n_blocks = n_dev * per_piece

    bufs, starts, where = gather_tiles(blocks[0, 0], n_col, n_row)

    turned = vectors.T.reshape(n_dev, share, rows)
    own_ids = jnp.pad(cols[0, 0].astype(jnp.bfloat16), (0, rows - slots))
    own_ids = jnp.broadcast_to(own_ids, (n_dev, share, rows))
    both = lax.all_to_all(
        jnp.concatenate([turned, own_ids], axis=1), LANES, split_axis=0, concat_axis=0, tiled=True
    )
    zt = both[:, :share]
    local = both[:, share, :slots].astype(jnp.int32)
    down = (jnp.arange(n_dev, dtype=jnp.int32) % n_row)[:, None]
    ids = (local // per_piece * n_row + down) * per_piece + local % per_piece

    done = pl.pallas_call(
        functools.partial(filter_kernel, per_piece, n_row, starts),
        out_shape=jax.ShapeDtypeStruct((n_dev, 2, share, rows), jnp.bfloat16),
        in_specs=[
            pl.BlockSpec(memory_space=pltpu.SMEM),
            pl.BlockSpec(memory_space=pltpu.SMEM),
            pl.BlockSpec(memory_space=pltpu.VMEM),
        ]
        + [pl.BlockSpec(memory_space=pl.ANY)] * len(bufs),
        out_specs=pl.BlockSpec(memory_space=pltpu.VMEM),
        scratch_shapes=[
            pltpu.VMEM((n_dev, slots, orb, orb), blocks.dtype),
            pltpu.VMEM((n_dev, slots, orb, orb), blocks.dtype),
            pltpu.VMEM((n_blocks, share, orb), jnp.bfloat16),
            *[pltpu.VMEM((n_blocks, share, orb), jnp.float32)] * (3 + SPLIT),
            pltpu.SemaphoreType.DMA((n_dev,)),
        ],
        compiler_params=pltpu.CompilerParams(vmem_limit_bytes=32 * 2**20),
    )(ids, where, zt, *bufs)
    back = lax.all_to_all(done, LANES, split_axis=0, concat_axis=0, tiled=True)
    outs = jnp.transpose(back, (1, 3, 0, 2)).reshape(2, rows, width).astype(jnp.float32)
    return outs[0], outs[1]


def per_device(vectors, blocks, cols):
    n_dev = lax.axis_size(LANES)
    line_of_four = lax.axis_size("col") == 4 and lax.axis_size("row") == 4
    if line_of_four and n_dev * blocks.size * blocks.dtype.itemsize <= GATHER_LIMIT:
        return gather_plan(vectors, blocks, cols)
    return spread_plan(vectors, blocks, cols)


def solution(mesh):
    return jax.shard_map(
        per_device,
        mesh=mesh,
        in_specs=(
            P(("col", "row"), "dom"),
            P(("dom", "col"), "row", None, None, None),
            P(("dom", "col"), "row", None),
        ),
        out_specs=(P(("col", "row"), "dom"), P(("col", "row"), "dom")),
        check_vma=False,
    )
```

```python
import functools

import jax
import jax.numpy as jnp
from jax import lax
from jax.experimental import pallas as pl
from jax.experimental.pallas import tpu as pltpu
from jax.sharding import PartitionSpec as P

PER_ROW = 2
DEG = 4
SPLIT = 4
GATHER_LIMIT = 12 * 2**20
LANES = ("col", "row")


def onehot_sum(selected, high_part, low_part):
    first = jnp.einsum("su,sok->uok", selected, high_part, preferred_element_type=jnp.float32)
    second = jnp.einsum("su,sok->uok", selected, low_part, preferred_element_type=jnp.float32)
    return first + second


def apply_pair(send, grouped, col_ids, onehot):
    tile_rows, per_row, orb, _ = grouped.shape
    piece_rows, width = send.shape
    tile_cols = onehot.shape[1]
    wide = lax.all_gather(send, "col", axis=0, tiled=True).reshape(tile_cols, orb, width)
    picked = jnp.take(wide, col_ids, axis=0).reshape(tile_rows, per_row, orb, width)
    direct = jnp.einsum("tpio,tpok->tik", grouped, picked, preferred_element_type=jnp.float32)
    part_rows = lax.psum_scatter(
        direct.reshape(tile_rows * orb, width).astype(jnp.bfloat16),
        "row",
        scatter_dimension=0,
        tiled=True,
    ).astype(jnp.float32)
    tall = lax.all_gather(send, "row", axis=0, tiled=True).reshape(tile_rows, orb, width)
    mirrored = jnp.einsum("tpio,tik->tpok", grouped, tall, preferred_element_type=jnp.float32)
    mirrored = mirrored.reshape(tile_rows * per_row, orb, width)
    high_part = mirrored.astype(jnp.bfloat16)
    low_part = (mirrored - high_part.astype(jnp.float32)).astype(jnp.bfloat16)
    summed = onehot_sum(onehot, high_part, low_part)
    part_cols = lax.psum_scatter(
        summed.reshape(tile_cols * orb, width).astype(jnp.bfloat16),
        "col",
        scatter_dimension=0,
        tiled=True,
    ).astype(jnp.float32)
    return part_rows + part_cols


def spread_plan(vectors, blocks, cols):
    tiles = blocks[0, 0]
    col_ids = cols[0, 0]
    slots, orb, _ = tiles.shape
    tile_rows = slots // PER_ROW
    tile_cols = lax.axis_size("col") * (vectors.shape[0] // orb)
    grouped = tiles.reshape(tile_rows, PER_ROW, orb, orb)
    onehot = (col_ids[:, None] == jnp.arange(tile_cols, dtype=jnp.int32)[None, :]).astype(
        jnp.bfloat16
    )
    prev = vectors.astype(jnp.float32)
    now = apply_pair(vectors, grouped, col_ids, onehot)
    for step in range(DEG - 1):
        nxt = 2.0 * apply_pair(now.astype(jnp.bfloat16), grouped, col_ids, onehot) - prev
        prev, now = (now, nxt)
    return (now, prev)


def vmem(count=1):
    return [pl.BlockSpec(memory_space=pltpu.VMEM)] * count


def smem(count=1):
    return [pl.BlockSpec(memory_space=pltpu.SMEM)] * count


def anywhere(count=1):
    return [pl.BlockSpec(memory_space=pl.ANY)] * count


def nothing(*refs):
    pass


def after(value, *others, rank=0):
    return pl.pallas_call(
        nothing,
        out_shape=jax.ShapeDtypeStruct(value.shape, value.dtype),
        in_specs=anywhere(1 + len(others)),
        out_specs=anywhere()[0],
        input_output_aliases={0: 0},
        compiler_params=pltpu.CompilerParams(vmem_limit_bytes=2**20),
        cost_estimate=pl.CostEstimate(flops=0, bytes_accessed=rank * 2**26, transcendentals=0),
    )(value, *others)


def multiply(t, groups, across_ref, down_ref, ids_ref, z, straight, scattered):
    tile_rows = z.shape[0] // len(groups)
    n_row = ids_ref.shape[0] // len(groups)
    orb = z.shape[2]
    for g, group in enumerate(groups):
        if not group:
            continue
        here = across_ref[g] * tile_rows + t
        places = [(tile, t * PER_ROW + p) for tile in group for p in range(PER_ROW)]
        strip = jnp.concatenate([s[i, slot] for (_, s, _, i), slot in places], axis=1)
        turned = jnp.concatenate([st[i, slot] for (_, _, st, i), slot in places], axis=0)
        where = [ids_ref[across_ref[g] * n_row + down_ref[f], slot] for (f, _, _, _), slot in places]
        wide = jnp.concatenate([z[u] for u in where], axis=1)
        straight[here] = jnp.dot(wide, turned, preferred_element_type=jnp.float32)
        mirrored = jnp.dot(z[here], strip, preferred_element_type=jnp.float32)
        for i, u in enumerate(where):
            scattered[i % len(scattered)][u] += mirrored[:, i * orb : (i + 1) * orb]


def clear(refs):
    for ref in refs:
        ref[...] = jnp.zeros_like(ref)


def filter_kernel(order, n_col, n_row, across_ref, down_ref, ids_ref, zt_ref, *refs):
    bufs, (out_ref, s_ref, st_ref, z, now, prev, straight, *scattered, sems) = (
        refs[: len(order)],
        refs[len(order) :],
    )
    n_blocks, share, orb = z.shape
    slots = s_ref.shape[1]
    per_piece = n_blocks // (n_col * n_row)
    tile_rows = slots // PER_ROW

    copies = []
    for i, (buf, (g, f, start)) in enumerate(zip(bufs, order)):
        place = s_ref.at[g * n_row + f, pl.ds(start, buf.shape[0])]
        copies.append(pltpu.make_async_copy(buf, place, sems.at[i]))
        copies[-1].start()
    for p in range(n_col * n_row):
        for b in range(per_piece):
            own = zt_ref[p, :, b * orb : (b + 1) * orb]
            z[p * per_piece + b] = own
            now[p * per_piece + b] = own.astype(jnp.float32)
    clear([prev])
    for copy, (g, f, start) in zip(copies, order):
        copy.wait()
        tile = g * n_row + f
        for slot in range(start, start + copy.src_ref.shape[0]):
            st_ref[tile, slot] = s_ref[tile, slot].T

    groups = [[(f, s_ref, st_ref, g * n_row + f) for f in range(n_row)] for g in range(n_col)]

    def one_step(step, carry):
        clear(scattered)

        def block_row(t, carry):
            multiply(t, groups, across_ref, down_ref, ids_ref, z, straight, scattered)
            return carry

        lax.fori_loop(0, tile_rows, block_row, 0)
        total = straight[...]
        for ref in scattered:
            total += ref[...]
        later = step > 0
        total = jnp.where(later, 2.0, 1.0) * total - jnp.where(later, 1.0, 0.0) * prev[...]
        prev[...] = now[...]
        now[...] = total
        z[...] = total.astype(z.dtype)
        return carry

    lax.fori_loop(0, DEG, one_step, 0)
    for p in range(n_col * n_row):
        for b in range(per_piece):
            u = p * per_piece + b
            out_ref[p, 0, :, b * orb : (b + 1) * orb] = now[u].astype(out_ref.dtype)
            out_ref[p, 1, :, b * orb : (b + 1) * orb] = prev[u].astype(out_ref.dtype)


def gather_plan(vectors, blocks, cols):
    n_dev = lax.axis_size(LANES)
    n_col, n_row = lax.axis_size("col"), lax.axis_size("row")
    rows, width = vectors.shape
    slots, orb = blocks.shape[2:4]
    share = width // n_dev
    per_piece = rows // orb
    n_blocks = n_dev * per_piece
    half = slots // 2
    across = lax.axis_index("col") ^ jnp.arange(n_col, dtype=jnp.int32)
    down = lax.axis_index("row") ^ jnp.arange(n_row, dtype=jnp.int32)

    def send(buf, flip_col, flip_row):
        pairs = [
            (c * n_row + r, (c ^ flip_col) * n_row + (r ^ flip_row))
            for c in range(n_col)
            for r in range(n_row)
        ]
        return lax.ppermute(buf, LANES, pairs)

    def to_mate(*bufs):
        return [send(buf, 1, 0) for buf in bufs]

    own = blocks[0, 0]
    far = send(own, 0, 3)
    near = send(own, 0, 1)
    over_own = send(own, 2, 0)

    near = after(near, over_own)
    over_near = send(near, 2, 0)
    mates = to_mate(own, near, over_own)
    far = after(after(far, rank=1), over_near, *mates[1:])
    over_far = send(far, 2, 0)
    last = send(far, 0, 1)

    mates += to_mate(far, over_near)
    last = after(last, over_far, mates[0], *mates[3:])
    over_last = send(last[:half], 2, 0)
    side_last = send(over_far[half:], 0, 1)
    mates += to_mate(last, over_far, over_last, side_last)

    turned = vectors.T.reshape(n_dev, share, rows)
    own_ids = jnp.pad(cols[0, 0].astype(vectors.dtype), (0, rows - slots))
    own_ids = jnp.broadcast_to(own_ids, (n_dev, share, rows))
    payload = after(jnp.concatenate([turned, own_ids], axis=1), last)
    both = lax.all_to_all(payload, LANES, split_axis=0, concat_axis=0, tiled=True)
    local = both[:, share, :slots].astype(jnp.int32)
    at_row = (jnp.arange(n_dev, dtype=jnp.int32) % n_row)[:, None]
    ids = (local // per_piece * n_row + at_row) * per_piece + local % per_piece

    bufs = [own, near, over_own, far, over_near, last, over_far, over_last, side_last]
    order = [(0, 0, 0), (0, 1, 0), (2, 0, 0), (0, 3, 0), (2, 1, 0), (0, 2, 0), (2, 3, 0), (2, 2, 0), (2, 2, half)]
    order += [(g ^ 1, f, slot) for g, f, slot in order]
    bufs += mates
    done = pl.pallas_call(
        functools.partial(filter_kernel, order, n_col, n_row),
        out_shape=jax.ShapeDtypeStruct((n_dev, 2, share, rows), jnp.bfloat16),
        in_specs=smem(3) + vmem() + anywhere(len(bufs)),
        out_specs=vmem()[0],
        scratch_shapes=[
            *[pltpu.VMEM((n_dev, slots, orb, orb), blocks.dtype)] * 2,
            pltpu.VMEM((n_blocks, share, orb), jnp.bfloat16),
            *[pltpu.VMEM((n_blocks, share, orb), jnp.float32)] * (3 + SPLIT),
            pltpu.SemaphoreType.DMA((len(bufs),)),
        ],
        compiler_params=pltpu.CompilerParams(vmem_limit_bytes=32 * 2**20),
    )(across, down, ids, both[:, :share], *bufs)
    back = lax.all_to_all(done, LANES, split_axis=0, concat_axis=0, tiled=True)
    outs = jnp.transpose(back, (1, 3, 0, 2)).reshape(2, rows, width).astype(jnp.float32)
    return outs[0], outs[1]


def per_device(vectors, blocks, cols):
    n_dev = lax.axis_size(LANES)
    line_of_four = lax.axis_size("col") == 4 and lax.axis_size("row") == 4
    if line_of_four and n_dev * blocks.size * blocks.dtype.itemsize <= GATHER_LIMIT:
        return gather_plan(vectors, blocks, cols)
    return spread_plan(vectors, blocks, cols)


def solution(mesh):
    return jax.shard_map(
        per_device,
        mesh=mesh,
        in_specs=(
            P(("col", "row"), "dom"),
            P(("dom", "col"), "row", None, None, None),
            P(("dom", "col"), "row", None),
        ),
        out_specs=(P(("col", "row"), "dom"), P(("col", "row"), "dom")),
        check_vma=False,
    )
```

```python
import functools

import jax
import jax.numpy as jnp
from jax import lax
from jax.experimental import pallas as pl
from jax.experimental.pallas import tpu as pltpu
from jax.sharding import PartitionSpec as P

PER_ROW = 2
DEG = 4
SPLIT = 4
GATHER_LIMIT = 12 * 2**20
LANES = ("col", "row")


def onehot_sum(selected, high_part, low_part):
    first = jnp.einsum("su,sok->uok", selected, high_part, preferred_element_type=jnp.float32)
    second = jnp.einsum("su,sok->uok", selected, low_part, preferred_element_type=jnp.float32)
    return first + second


def apply_pair(send, grouped, col_ids, onehot):
    tile_rows, per_row, orb, _ = grouped.shape
    piece_rows, width = send.shape
    tile_cols = onehot.shape[1]
    wide = lax.all_gather(send, "col", axis=0, tiled=True).reshape(tile_cols, orb, width)
    picked = jnp.take(wide, col_ids, axis=0).reshape(tile_rows, per_row, orb, width)
    direct = jnp.einsum("tpio,tpok->tik", grouped, picked, preferred_element_type=jnp.float32)
    part_rows = lax.psum_scatter(
        direct.reshape(tile_rows * orb, width).astype(jnp.bfloat16),
        "row",
        scatter_dimension=0,
        tiled=True,
    ).astype(jnp.float32)
    tall = lax.all_gather(send, "row", axis=0, tiled=True).reshape(tile_rows, orb, width)
    mirrored = jnp.einsum("tpio,tik->tpok", grouped, tall, preferred_element_type=jnp.float32)
    mirrored = mirrored.reshape(tile_rows * per_row, orb, width)
    high_part = mirrored.astype(jnp.bfloat16)
    low_part = (mirrored - high_part.astype(jnp.float32)).astype(jnp.bfloat16)
    summed = onehot_sum(onehot, high_part, low_part)
    part_cols = lax.psum_scatter(
        summed.reshape(tile_cols * orb, width).astype(jnp.bfloat16),
        "col",
        scatter_dimension=0,
        tiled=True,
    ).astype(jnp.float32)
    return part_rows + part_cols


def spread_plan(vectors, blocks, cols):
    tiles = blocks[0, 0]
    col_ids = cols[0, 0]
    slots, orb, _ = tiles.shape
    tile_rows = slots // PER_ROW
    tile_cols = lax.axis_size("col") * (vectors.shape[0] // orb)
    grouped = tiles.reshape(tile_rows, PER_ROW, orb, orb)
    onehot = (col_ids[:, None] == jnp.arange(tile_cols, dtype=jnp.int32)[None, :]).astype(
        jnp.bfloat16
    )
    prev = vectors.astype(jnp.float32)
    now = apply_pair(vectors, grouped, col_ids, onehot)
    for step in range(DEG - 1):
        nxt = 2.0 * apply_pair(now.astype(jnp.bfloat16), grouped, col_ids, onehot) - prev
        prev, now = (now, nxt)
    return (now, prev)


def vmem(count=1):
    return [pl.BlockSpec(memory_space=pltpu.VMEM)] * count


def smem(count=1):
    return [pl.BlockSpec(memory_space=pltpu.SMEM)] * count


def anywhere(count=1):
    return [pl.BlockSpec(memory_space=pl.ANY)] * count


def nothing(*refs):
    pass


def after(value, *others):
    return pl.pallas_call(
        nothing,
        out_shape=jax.ShapeDtypeStruct(value.shape, value.dtype),
        in_specs=anywhere(1 + len(others)),
        out_specs=anywhere()[0],
        input_output_aliases={0: 0},
        compiler_params=pltpu.CompilerParams(vmem_limit_bytes=2**20),
    )(value, *others)


def pick_kernel(first_ref, one_ref, other_ref, *refs):
    out_ref, sem = refs[-2:]

    @pl.when(first_ref[0] != 0)
    def _():
        copy = pltpu.make_async_copy(one_ref, out_ref, sem)
        copy.start()
        copy.wait()

    @pl.when(first_ref[0] == 0)
    def _():
        copy = pltpu.make_async_copy(other_ref, out_ref, sem)
        copy.start()
        copy.wait()


def pick(first, one, other, *others):
    return pl.pallas_call(
        pick_kernel,
        out_shape=jax.ShapeDtypeStruct(one.shape, one.dtype),
        in_specs=smem() + anywhere(2 + len(others)),
        out_specs=anywhere()[0],
        scratch_shapes=[pltpu.SemaphoreType.DMA(())],
        compiler_params=pltpu.CompilerParams(vmem_limit_bytes=2**20),
    )(first, one, other, *others)


def split_kernel(peers_ref, vectors_ref, ids_ref, keep_ref, go_ref, turned):
    count, share, rows = turned.shape
    whole = vectors_ref[...].T
    for d in range(count):
        turned[d] = whole[d * share : (d + 1) * share]
    for k in range(count):
        out_ref = (keep_ref, go_ref)[k // (count // 2)]
        out_ref[k % (count // 2), :, :rows] = turned[peers_ref[k]]
        out_ref[k % (count // 2), :, rows:] = ids_ref[...]


def place(g, f):
    return (f >> 1) * 8 + ((f & 1) ^ (f >> 1)) * 4 + g


def multiply(t, groups, across_ref, ids_ref, z, straight, scattered):
    tile_rows = z.shape[0] // len(groups)
    orb = z.shape[2]
    for g, group in enumerate(groups):
        if not group:
            continue
        here = across_ref[g] * tile_rows + t
        places = [(tile, t * PER_ROW + p) for tile in group for p in range(PER_ROW)]
        strip = jnp.concatenate([s[i, slot] for (_, s, _, i), slot in places], axis=1)
        turned = jnp.concatenate([st[i, slot] for (_, _, st, i), slot in places], axis=0)
        where = [ids_ref[place(g, f), slot] for (f, _, _, _), slot in places]
        wide = jnp.concatenate([z[u] for u in where], axis=1)
        straight[here] = jnp.dot(wide, turned, preferred_element_type=jnp.float32)
        mirrored = jnp.dot(z[here], strip, preferred_element_type=jnp.float32)
        for i, u in enumerate(where):
            scattered[i % len(scattered)][u] += mirrored[:, i * orb : (i + 1) * orb]


def clear(refs):
    for ref in refs:
        ref[...] = jnp.zeros_like(ref)


def filter_kernel(order, n_col, n_row, across_ref, down_ref, ids_ref, zt_ref, *refs):
    bufs, (out_ref, s_ref, st_ref, z, now, prev, straight, *scattered, sems) = (
        refs[: len(order)],
        refs[len(order) :],
    )
    n_blocks, share, orb = z.shape
    slots = s_ref.shape[1]
    per_piece = n_blocks // (n_col * n_row)
    tile_rows = slots // PER_ROW

    copies = []
    for i, (buf, (g, f, start)) in enumerate(zip(bufs, order)):
        target = s_ref.at[g * n_row + f, pl.ds(start, buf.shape[0])]
        copies.append(pltpu.make_async_copy(buf, target, sems.at[i]))
        copies[-1].start()
    for g in range(n_col):
        for f in range(n_row):
            for b in range(per_piece):
                u = (across_ref[g] * n_row + down_ref[f]) * per_piece + b
                own = zt_ref[place(g, f), :, b * orb : (b + 1) * orb]
                z[u] = own
                now[u] = own.astype(jnp.float32)
    clear([prev])
    for copy, (g, f, start) in zip(copies, order):
        copy.wait()
        tile = g * n_row + f
        for slot in range(start, start + copy.src_ref.shape[0]):
            st_ref[tile, slot] = s_ref[tile, slot].T

    groups = [[(f, s_ref, st_ref, g * n_row + f) for f in range(n_row)] for g in range(n_col)]

    def one_step(step, carry):
        clear(scattered)

        def block_row(t, carry):
            multiply(t, groups, across_ref, ids_ref, z, straight, scattered)
            return carry

        lax.fori_loop(0, tile_rows, block_row, 0)
        total = straight[...]
        for ref in scattered:
            total += ref[...]
        later = step > 0
        total = jnp.where(later, 2.0, 1.0) * total - jnp.where(later, 1.0, 0.0) * prev[...]
        prev[...] = now[...]
        now[...] = total
        z[...] = total.astype(z.dtype)
        return carry

    lax.fori_loop(0, DEG, one_step, 0)
    for p in range(n_col * n_row):
        for b in range(per_piece):
            u = p * per_piece + b
            out_ref[p, 0, :, b * orb : (b + 1) * orb] = now[u].astype(out_ref.dtype)
            out_ref[p, 1, :, b * orb : (b + 1) * orb] = prev[u].astype(out_ref.dtype)


def gather_plan(vectors, blocks, cols):
    n_dev = lax.axis_size(LANES)
    n_col, n_row = lax.axis_size("col"), lax.axis_size("row")
    rows, width = vectors.shape
    slots, orb = blocks.shape[2:4]
    share = width // n_dev
    per_piece = rows // orb
    n_blocks = n_dev * per_piece
    half = slots // 2
    across = lax.axis_index("col") ^ jnp.arange(n_col, dtype=jnp.int32)
    down = lax.axis_index("row") ^ jnp.arange(n_row, dtype=jnp.int32)

    def send(buf, flip_col, flip_row, from_rows=range(n_row)):
        pairs = [
            (c * n_row + r, (c ^ flip_col) * n_row + (r ^ flip_row))
            for c in range(n_col)
            for r in from_rows
        ]
        return lax.ppermute(buf, LANES, pairs)

    def to_mate(*bufs):
        return [send(buf, 1, 0) for buf in bufs]

    own = blocks[0, 0]
    near = send(own, 0, 1)
    inner = send(own, 0, 3, (1, 2))
    over_own = send(own, 2, 0)

    peers = [
        (across[core + 2 * y] * n_row + down[one ^ 3 * three])
        for core in range(2)
        for y in range(2)
        for one in range(2)
        for three in range(2)
    ]
    own_ids = jnp.pad(cols[0, 0], (0, orb - slots)).astype(vectors.dtype)
    keep, go = pl.pallas_call(
        split_kernel,
        out_shape=[jax.ShapeDtypeStruct((n_dev // 2, share, rows + orb), vectors.dtype)] * 2,
        in_specs=smem() + vmem(2),
        out_specs=vmem(2),
        scratch_shapes=[pltpu.VMEM((n_dev, share, rows), vectors.dtype)],
        compiler_params=pltpu.CompilerParams(vmem_limit_bytes=4 * 2**20),
    )(jnp.stack(peers), vectors, jnp.broadcast_to(own_ids, (share, orb)))
    parts = jnp.stack([keep, send(go, 1, 0)])

    def swap(parts, flip_col, flip_row, *others):
        count = parts.shape[1] // 2
        go = parts[:, count:]
        go = after(go, *others) if others else go
        return jnp.concatenate([parts[:, :count], send(go, flip_col, flip_row)])

    parts = swap(parts, 2, 0)

    near = after(near, over_own)
    outer = send(after(own, near), 0, 3, (0, 3))
    over_near = send(near, 2, 0)
    parts = swap(parts, 0, 1, near)
    mates = to_mate(own, near, over_own)
    inside = (lax.axis_index("row") == 1) | (lax.axis_index("row") == 2)
    far = pick(inside.astype(jnp.int32)[None], inner, outer, over_near, *mates)
    over_far = send(far, 2, 0)
    last = send(far, 0, 1)
    parts = swap(parts, 0, 3, far)[:, 0]
    mates += to_mate(far, over_near)
    last = after(last, over_far, *mates[3:])
    over_last = send(last[:half], 2, 0)
    side_last = send(over_far[half:], 0, 1)
    mates += to_mate(last, over_far, over_last, side_last)

    local = parts[:, 0, rows : rows + slots].astype(jnp.int32)
    at_row = {place(g, f): down[f] for g in range(n_col) for f in range(n_row)}
    at_row = jnp.stack([at_row[k] for k in range(n_dev)])[:, None]
    ids = (local // per_piece * n_row + at_row) * per_piece + local % per_piece

    bufs = [own, near, over_own, far, over_near, last, over_far, over_last, side_last]
    order = [(0, 0, 0), (0, 1, 0), (2, 0, 0), (0, 3, 0), (2, 1, 0), (0, 2, 0), (2, 3, 0), (2, 2, 0), (2, 2, half)]
    order += [(g ^ 1, f, slot) for g, f, slot in order]
    bufs += mates
    done = pl.pallas_call(
        functools.partial(filter_kernel, order, n_col, n_row),
        out_shape=jax.ShapeDtypeStruct((n_dev, 2, share, rows), jnp.bfloat16),
        in_specs=smem(3) + vmem() + anywhere(len(bufs)),
        out_specs=vmem()[0],
        scratch_shapes=[
            *[pltpu.VMEM((n_dev, slots, orb, orb), blocks.dtype)] * 2,
            pltpu.VMEM((n_blocks, share, orb), jnp.bfloat16),
            *[pltpu.VMEM((n_blocks, share, orb), jnp.float32)] * (3 + SPLIT),
            pltpu.SemaphoreType.DMA((len(bufs),)),
        ],
        compiler_params=pltpu.CompilerParams(vmem_limit_bytes=32 * 2**20),
    )(across, down, ids, parts, *bufs)
    back = lax.all_to_all(done, LANES, split_axis=0, concat_axis=0, tiled=True)
    outs = jnp.transpose(back, (1, 3, 0, 2)).reshape(2, rows, width).astype(jnp.float32)
    return outs[0], outs[1]


def per_device(vectors, blocks, cols):
    n_dev = lax.axis_size(LANES)
    line_of_four = lax.axis_size("col") == 4 and lax.axis_size("row") == 4
    if line_of_four and n_dev * blocks.size * blocks.dtype.itemsize <= GATHER_LIMIT:
        return gather_plan(vectors, blocks, cols)
    return spread_plan(vectors, blocks, cols)


def solution(mesh):
    return jax.shard_map(
        per_device,
        mesh=mesh,
        in_specs=(
            P(("col", "row"), "dom"),
            P(("dom", "col"), "row", None, None, None),
            P(("dom", "col"), "row", None),
        ),
        out_specs=(P(("col", "row"), "dom"), P(("col", "row"), "dom")),
        check_vma=False,
    )
```

```python
import functools

import jax
import jax.numpy as jnp
import numpy
from jax import lax
from jax.experimental import pallas as pl
from jax.experimental.pallas import tpu as pltpu
from jax.sharding import PartitionSpec as P

PER_ROW = 2
DEG = 4
SPLIT = 4
GATHER_LIMIT = 12 * 2**20
LANES = ("col", "row")


def onehot_sum(selected, high_part, low_part):
    first = jnp.einsum("su,sok->uok", selected, high_part, preferred_element_type=jnp.float32)
    second = jnp.einsum("su,sok->uok", selected, low_part, preferred_element_type=jnp.float32)
    return first + second


def apply_pair(send, grouped, col_ids, onehot):
    tile_rows, per_row, orb, _ = grouped.shape
    piece_rows, width = send.shape
    tile_cols = onehot.shape[1]
    wide = lax.all_gather(send, "col", axis=0, tiled=True).reshape(tile_cols, orb, width)
    picked = jnp.take(wide, col_ids, axis=0).reshape(tile_rows, per_row, orb, width)
    direct = jnp.einsum("tpio,tpok->tik", grouped, picked, preferred_element_type=jnp.float32)
    part_rows = lax.psum_scatter(
        direct.reshape(tile_rows * orb, width).astype(jnp.bfloat16),
        "row",
        scatter_dimension=0,
        tiled=True,
    ).astype(jnp.float32)
    tall = lax.all_gather(send, "row", axis=0, tiled=True).reshape(tile_rows, orb, width)
    mirrored = jnp.einsum("tpio,tik->tpok", grouped, tall, preferred_element_type=jnp.float32)
    mirrored = mirrored.reshape(tile_rows * per_row, orb, width)
    high_part = mirrored.astype(jnp.bfloat16)
    low_part = (mirrored - high_part.astype(jnp.float32)).astype(jnp.bfloat16)
    summed = onehot_sum(onehot, high_part, low_part)
    part_cols = lax.psum_scatter(
        summed.reshape(tile_cols * orb, width).astype(jnp.bfloat16),
        "col",
        scatter_dimension=0,
        tiled=True,
    ).astype(jnp.float32)
    return part_rows + part_cols


def spread_plan(vectors, blocks, cols):
    tiles = blocks[0, 0]
    col_ids = cols[0, 0]
    slots, orb, _ = tiles.shape
    tile_rows = slots // PER_ROW
    tile_cols = lax.axis_size("col") * (vectors.shape[0] // orb)
    grouped = tiles.reshape(tile_rows, PER_ROW, orb, orb)
    onehot = (col_ids[:, None] == jnp.arange(tile_cols, dtype=jnp.int32)[None, :]).astype(
        jnp.bfloat16
    )
    prev = vectors.astype(jnp.float32)
    now = apply_pair(vectors, grouped, col_ids, onehot)
    for step in range(DEG - 1):
        nxt = 2.0 * apply_pair(now.astype(jnp.bfloat16), grouped, col_ids, onehot) - prev
        prev, now = (now, nxt)
    return (now, prev)


def vmem(count=1):
    return [pl.BlockSpec(memory_space=pltpu.VMEM)] * count


def smem(count=1):
    return [pl.BlockSpec(memory_space=pltpu.SMEM)] * count


def anywhere(count=1):
    return [pl.BlockSpec(memory_space=pl.ANY)] * count


def nothing(*refs):
    pass


def after(value, *others):
    return pl.pallas_call(
        nothing,
        out_shape=jax.ShapeDtypeStruct(value.shape, value.dtype),
        in_specs=anywhere(1 + len(others)),
        out_specs=anywhere()[0],
        input_output_aliases={0: 0},
        compiler_params=pltpu.CompilerParams(vmem_limit_bytes=2**20),
    )(value, *others)


def copy_kernel(value_ref, *refs):
    out_ref, sem = refs[-2:]
    copy = pltpu.make_async_copy(value_ref, out_ref, sem)
    copy.start()
    copy.wait()


def copy_after(value, *others):
    return pl.pallas_call(
        copy_kernel,
        out_shape=jax.ShapeDtypeStruct(value.shape, value.dtype),
        in_specs=anywhere(1 + len(others)),
        out_specs=anywhere()[0],
        scratch_shapes=[pltpu.SemaphoreType.DMA(())],
        compiler_params=pltpu.CompilerParams(vmem_limit_bytes=2**20),
    )(value, *others)


def pick_kernel(first_ref, one_ref, other_ref, *refs):
    out_ref, sem = refs[-2:]

    @pl.when(first_ref[0] != 0)
    def _():
        copy = pltpu.make_async_copy(one_ref, out_ref, sem)
        copy.start()
        copy.wait()

    @pl.when(first_ref[0] == 0)
    def _():
        copy = pltpu.make_async_copy(other_ref, out_ref, sem)
        copy.start()
        copy.wait()


def pick(first, one, other, *others):
    return pl.pallas_call(
        pick_kernel,
        out_shape=jax.ShapeDtypeStruct(one.shape, one.dtype),
        in_specs=smem() + anywhere(2 + len(others)),
        out_specs=anywhere()[0],
        scratch_shapes=[pltpu.SemaphoreType.DMA(())],
        compiler_params=pltpu.CompilerParams(vmem_limit_bytes=2**20),
    )(first, one, other, *others)


def split_kernel(peers_ref, vectors_ref, ids_ref, keep_ref, go_ref, turned):
    count, share, rows = turned.shape
    whole = vectors_ref[...].T
    for d in range(count):
        turned[d] = whole[d * share : (d + 1) * share]
    for k in range(count):
        out_ref = (keep_ref, go_ref)[k // (count // 2)]
        out_ref[k % (count // 2), :, :rows] = turned[peers_ref[k]]
        out_ref[k % (count // 2), :, rows:] = ids_ref[...]


def place(g, f):
    return (f >> 1) * 8 + ((f & 1) ^ (f >> 1)) * 4 + g


def multiply(t, groups, across_ref, ids_ref, z, straight, scattered):
    tile_rows = z.shape[0] // len(groups)
    orb = z.shape[2]
    for g, group in enumerate(groups):
        if not group:
            continue
        here = across_ref[g] * tile_rows + t
        places = [(tile, t * PER_ROW + p) for tile in group for p in range(PER_ROW)]
        strip = jnp.concatenate([s[i, slot] for (_, s, _, i), slot in places], axis=1)
        turned = jnp.concatenate([st[i, slot] for (_, _, st, i), slot in places], axis=0)
        where = [ids_ref[place(g, f), slot] for (f, _, _, _), slot in places]
        wide = jnp.concatenate([z[u] for u in where], axis=1)
        straight[here] = jnp.dot(wide, turned, preferred_element_type=jnp.float32)
        mirrored = jnp.dot(z[here], strip, preferred_element_type=jnp.float32)
        for i, u in enumerate(where):
            scattered[i % len(scattered)][u] += mirrored[:, i * orb : (i + 1) * orb]


def clear(refs):
    for ref in refs:
        ref[...] = jnp.zeros_like(ref)


def turn(s_ref, st_ref, i, start, count):
    def four(k, carry):
        for m in range(4):
            st_ref[i, start + 4 * k + m] = s_ref[i, start + 4 * k + m].T
        return carry

    lax.fori_loop(0, count // 4, four, 0)


def load_kernel(count, *refs):
    bufs, (s_ref, st_ref, sems) = refs[:count], refs[count:]
    copies = [pltpu.make_async_copy(buf, s_ref.at[i], sems.at[i]) for i, buf in enumerate(bufs)]
    for copy in copies:
        copy.start()
    for i, copy in enumerate(copies):
        copy.wait()
        turn(s_ref, st_ref, i, 0, s_ref.shape[1])


def load(bufs):
    out = jax.ShapeDtypeStruct((len(bufs), *bufs[0].shape), bufs[0].dtype)
    size = len(bufs) * bufs[0].size
    return pl.pallas_call(
        functools.partial(load_kernel, len(bufs)),
        out_shape=[out, out],
        in_specs=anywhere(len(bufs)),
        out_specs=vmem(2),
        scratch_shapes=[pltpu.SemaphoreType.DMA((len(bufs),))],
        compiler_params=pltpu.CompilerParams(vmem_limit_bytes=2**20),
        cost_estimate=pl.CostEstimate(flops=0, bytes_accessed=6 * size, transcendentals=0),
    )(*bufs)


def filter_kernel(early, late, n_col, n_row, across_ref, down_ref, ids_ref, zt_ref, se_ref, ste_ref, *refs):
    bufs, (out_ref, s_ref, st_ref, z, now, prev, straight, *scattered, sems) = (
        refs[: len(late)],
        refs[len(late) :],
    )
    n_blocks, share, orb = z.shape
    slots = s_ref.shape[1]
    per_piece = n_blocks // (n_col * n_row)
    tile_rows = slots // PER_ROW
    rest = sorted({(g, f) for g, f, _ in late})

    copies = []
    for i, (buf, (g, f, start)) in enumerate(zip(bufs, late)):
        target = s_ref.at[rest.index((g, f)), pl.ds(start, buf.shape[0])]
        copies.append(pltpu.make_async_copy(buf, target, sems.at[i]))
        copies[-1].start()
    for g in range(n_col):
        for f in range(n_row):
            for b in range(per_piece):
                u = (across_ref[g] * n_row + down_ref[f]) * per_piece + b
                own = zt_ref[place(g, f), :, b * orb : (b + 1) * orb]
                z[u] = own
                now[u] = own.astype(jnp.float32)
    clear([prev])
    for copy, buf, (g, f, start) in zip(copies, bufs, late):
        copy.wait()
        turn(s_ref, st_ref, rest.index((g, f)), start, buf.shape[0])

    tiles = {at: (se_ref, ste_ref, i) for i, at in enumerate(early)}
    tiles.update({at: (s_ref, st_ref, i) for i, at in enumerate(rest)})
    groups = [[(f, *tiles[g, f]) for f in range(n_row)] for g in range(n_col)]

    def one_step(step, carry):
        clear(scattered)

        def block_row(t, carry):
            multiply(t, groups, across_ref, ids_ref, z, straight, scattered)
            return carry

        lax.fori_loop(0, tile_rows, block_row, 0)
        total = straight[...]
        for ref in scattered:
            total += ref[...]
        later = step > 0
        total = jnp.where(later, 2.0, 1.0) * total - jnp.where(later, 1.0, 0.0) * prev[...]
        prev[...] = now[...]
        now[...] = total
        z[...] = total.astype(z.dtype)
        return carry

    lax.fori_loop(0, DEG, one_step, 0)
    for p in range(n_col * n_row):
        for b in range(per_piece):
            u = p * per_piece + b
            out_ref[p, 0, :, b * orb : (b + 1) * orb] = now[u].astype(out_ref.dtype)
            out_ref[p, 1, :, b * orb : (b + 1) * orb] = prev[u].astype(out_ref.dtype)


def gather_plan(vectors, blocks, cols):
    n_dev = lax.axis_size(LANES)
    n_col, n_row = lax.axis_size("col"), lax.axis_size("row")
    rows, width = vectors.shape
    slots, orb = blocks.shape[2:4]
    share = width // n_dev
    per_piece = rows // orb
    n_blocks = n_dev * per_piece
    half = slots // 2
    across = lax.axis_index("col") ^ jnp.arange(n_col, dtype=jnp.int32)
    down = lax.axis_index("row") ^ jnp.arange(n_row, dtype=jnp.int32)

    def send(buf, flip_col, flip_row, from_rows=range(n_row)):
        pairs = [
            (c * n_row + r, (c ^ flip_col) * n_row + (r ^ flip_row))
            for c in range(n_col)
            for r in from_rows
        ]
        return lax.ppermute(buf, LANES, pairs)

    def to_mate(*bufs):
        return [send(buf, 1, 0) for buf in bufs]

    own = blocks[0, 0]
    near = send(own, 0, 1)
    inner = send(own, 0, 3, (1, 2))
    over_own = send(own, 2, 0)

    g_of = numpy.array([core + 2 * y for core in range(2) for y in range(2) for _ in range(4)])
    f_of = numpy.array([one ^ 3 * three for _ in range(4) for one in range(2) for three in range(2)])
    peers = (lax.axis_index("col") ^ g_of) * n_row + (lax.axis_index("row") ^ f_of)
    own_ids = jnp.pad(cols[0, 0], (0, orb - slots)).astype(vectors.dtype)
    keep, go = pl.pallas_call(
        split_kernel,
        out_shape=[jax.ShapeDtypeStruct((n_dev // 2, share, rows + orb), vectors.dtype)] * 2,
        in_specs=smem() + vmem(2),
        out_specs=vmem(2),
        scratch_shapes=[pltpu.VMEM((n_dev, share, rows), vectors.dtype)],
        compiler_params=pltpu.CompilerParams(vmem_limit_bytes=4 * 2**20),
    )(peers.astype(jnp.int32), vectors, jnp.broadcast_to(own_ids, (share, orb)))
    parts = jnp.stack([keep, send(go, 1, 0)])

    def swap(parts, flip_col, flip_row):
        count = parts.shape[1] // 2
        return jnp.concatenate([parts[:, :count], send(parts[:, count:], flip_col, flip_row)])

    parts = swap(parts, 2, 0)

    near = after(near, over_own, parts)
    outer = send(copy_after(own, near), 0, 3, (0, 3))
    over_near = send(near, 2, 0)
    parts = swap(parts, 0, 1)
    mates = to_mate(own, near, over_own)
    inside = (lax.axis_index("row") == 1) | (lax.axis_index("row") == 2)
    far = pick(inside.astype(jnp.int32)[None], inner, outer, over_near, parts, *mates)
    over_far = send(far, 2, 0)
    last = send(far, 0, 1)
    parts = swap(parts, 0, 3)[:, 0]
    mates += to_mate(far, over_near)
    last = after(last, over_far, parts, *mates[3:])
    over_last = send(last[:half], 2, 0)
    side_last = send(over_far[half:], 0, 1)
    mates += to_mate(last, over_far)
    early = [(0, 0), (0, 1), (2, 0), (0, 3), (2, 1), (0, 2), (2, 3)]
    early += [(g ^ 1, f) for g, f in early]
    se, ste = load([own, near, over_own, far, over_near, last, over_far, *mates])
    over_last, side_last = after(over_last, se), after(side_last, se)
    late_bufs = [over_last, side_last, *to_mate(over_last, side_last)]
    late = [(2, 2, 0), (2, 2, half), (3, 2, 0), (3, 2, half)]

    local = parts[:, 0, rows : rows + slots].astype(jnp.int32)
    f_at = {place(g, f): f for g in range(n_col) for f in range(n_row)}
    f_at = numpy.array([f_at[k] for k in range(n_dev)], numpy.int32)
    at_row = (lax.axis_index("row") ^ f_at)[:, None]
    ids = (local // per_piece * n_row + at_row) * per_piece + local % per_piece

    done = pl.pallas_call(
        functools.partial(filter_kernel, early, late, n_col, n_row),
        out_shape=jax.ShapeDtypeStruct((n_dev, 2, share, rows), jnp.bfloat16),
        in_specs=smem(3) + vmem(3) + anywhere(len(late)),
        out_specs=vmem()[0],
        scratch_shapes=[
            *[pltpu.VMEM((n_dev - len(early), slots, orb, orb), blocks.dtype)] * 2,
            pltpu.VMEM((n_blocks, share, orb), jnp.bfloat16),
            *[pltpu.VMEM((n_blocks, share, orb), jnp.float32)] * (3 + SPLIT),
            pltpu.SemaphoreType.DMA((len(late),)),
        ],
        compiler_params=pltpu.CompilerParams(vmem_limit_bytes=12 * 2**20),
    )(across, down, ids, parts, se, ste, *late_bufs)
    back = lax.all_to_all(done, LANES, split_axis=0, concat_axis=0, tiled=True)
    outs = jnp.transpose(back, (1, 3, 0, 2)).reshape(2, rows, width).astype(jnp.float32)
    return outs[0], outs[1]


def per_device(vectors, blocks, cols):
    n_dev = lax.axis_size(LANES)
    line_of_four = lax.axis_size("col") == 4 and lax.axis_size("row") == 4
    if line_of_four and n_dev * blocks.size * blocks.dtype.itemsize <= GATHER_LIMIT:
        return gather_plan(vectors, blocks, cols)
    return spread_plan(vectors, blocks, cols)


def solution(mesh):
    return jax.shard_map(
        per_device,
        mesh=mesh,
        in_specs=(
            P(("col", "row"), "dom"),
            P(("dom", "col"), "row", None, None, None),
            P(("dom", "col"), "row", None),
        ),
        out_specs=(P(("col", "row"), "dom"), P(("col", "row"), "dom")),
        check_vma=False,
    )
```

```python
import functools

import jax
import jax.numpy as jnp
from jax import lax
from jax.experimental import pallas as pl
from jax.experimental.pallas import tpu as pltpu
from jax.sharding import PartitionSpec as P

PER_ROW = 2
DEG = 4
SPLIT = 4
GATHER_LIMIT = 12 * 2**20
LANES = ("col", "row")


def onehot_sum(selected, high_part, low_part):
    first = jnp.einsum("su,sok->uok", selected, high_part, preferred_element_type=jnp.float32)
    second = jnp.einsum("su,sok->uok", selected, low_part, preferred_element_type=jnp.float32)
    return first + second


def apply_pair(send, grouped, col_ids, onehot):
    tile_rows, per_row, orb, _ = grouped.shape
    piece_rows, width = send.shape
    tile_cols = onehot.shape[1]
    wide = lax.all_gather(send, "col", axis=0, tiled=True).reshape(tile_cols, orb, width)
    picked = jnp.take(wide, col_ids, axis=0).reshape(tile_rows, per_row, orb, width)
    direct = jnp.einsum("tpio,tpok->tik", grouped, picked, preferred_element_type=jnp.float32)
    part_rows = lax.psum_scatter(
        direct.reshape(tile_rows * orb, width).astype(jnp.bfloat16),
        "row",
        scatter_dimension=0,
        tiled=True,
    ).astype(jnp.float32)
    tall = lax.all_gather(send, "row", axis=0, tiled=True).reshape(tile_rows, orb, width)
    mirrored = jnp.einsum("tpio,tik->tpok", grouped, tall, preferred_element_type=jnp.float32)
    mirrored = mirrored.reshape(tile_rows * per_row, orb, width)
    high_part = mirrored.astype(jnp.bfloat16)
    low_part = (mirrored - high_part.astype(jnp.float32)).astype(jnp.bfloat16)
    summed = onehot_sum(onehot, high_part, low_part)
    part_cols = lax.psum_scatter(
        summed.reshape(tile_cols * orb, width).astype(jnp.bfloat16),
        "col",
        scatter_dimension=0,
        tiled=True,
    ).astype(jnp.float32)
    return part_rows + part_cols


def spread_plan(vectors, blocks, cols):
    tiles = blocks[0, 0]
    col_ids = cols[0, 0]
    slots, orb, _ = tiles.shape
    tile_rows = slots // PER_ROW
    tile_cols = lax.axis_size("col") * (vectors.shape[0] // orb)
    grouped = tiles.reshape(tile_rows, PER_ROW, orb, orb)
    onehot = (col_ids[:, None] == jnp.arange(tile_cols, dtype=jnp.int32)[None, :]).astype(
        jnp.bfloat16
    )
    prev = vectors.astype(jnp.float32)
    now = apply_pair(vectors, grouped, col_ids, onehot)
    for step in range(DEG - 1):
        nxt = 2.0 * apply_pair(now.astype(jnp.bfloat16), grouped, col_ids, onehot) - prev
        prev, now = (now, nxt)
    return (now, prev)


def vmem(count=1):
    return [pl.BlockSpec(memory_space=pltpu.VMEM)] * count


def smem(count=1):
    return [pl.BlockSpec(memory_space=pltpu.SMEM)] * count


def anywhere(count=1):
    return [pl.BlockSpec(memory_space=pl.ANY)] * count


def nothing(*refs):
    pass


def after(value, *others):
    return pl.pallas_call(
        nothing,
        out_shape=jax.ShapeDtypeStruct(value.shape, value.dtype),
        in_specs=anywhere(1 + len(others)),
        out_specs=anywhere()[0],
        input_output_aliases={0: 0},
        compiler_params=pltpu.CompilerParams(vmem_limit_bytes=2**20),
    )(value, *others)


def copy_kernel(value_ref, *refs):
    out_ref, sem = refs[-2:]
    copy = pltpu.make_async_copy(value_ref, out_ref, sem)
    copy.start()
    copy.wait()


def copy_after(value, *others):
    return pl.pallas_call(
        copy_kernel,
        out_shape=jax.ShapeDtypeStruct(value.shape, value.dtype),
        in_specs=[pl.BlockSpec(memory_space=pltpu.HBM)] + anywhere(len(others)),
        out_specs=anywhere()[0],
        scratch_shapes=[pltpu.SemaphoreType.DMA(())],
        compiler_params=pltpu.CompilerParams(vmem_limit_bytes=2**20),
    )(value, *others)


def pick_kernel(rows, one_ref, other_ref, *refs):
    out_ref, sem = refs[-2:]
    row = lax.axis_index("row")
    first = (row == rows[0]) | (row == rows[1])

    @pl.when(first)
    def _():
        copy = pltpu.make_async_copy(one_ref, out_ref, sem)
        copy.start()
        copy.wait()

    @pl.when(jnp.logical_not(first))
    def _():
        copy = pltpu.make_async_copy(other_ref, out_ref, sem)
        copy.start()
        copy.wait()


def pick(rows, one, other, *others):
    return pl.pallas_call(
        functools.partial(pick_kernel, rows),
        out_shape=jax.ShapeDtypeStruct(one.shape, one.dtype),
        in_specs=anywhere(2 + len(others)),
        out_specs=anywhere()[0],
        scratch_shapes=[pltpu.SemaphoreType.DMA(())],
        compiler_params=pltpu.CompilerParams(vmem_limit_bytes=2**20),
    )(one, other, *others)


def split_kernel(n_col, n_row, vectors_ref, cols_ref, keep_ref, go_ref, known_ref, turned):
    col, row = lax.axis_index("col"), lax.axis_index("row")
    count, share, rows = turned.shape
    orb = keep_ref.shape[2]
    per_piece = rows // orb
    whole = vectors_ref[...].T
    for d in range(count):
        turned[d] = whole[d * share : (d + 1) * share]
    orders = [(y, one, three) for y in range(2) for one in range(2) for three in range(2)]
    for core, out_ref in enumerate((keep_ref, go_ref)):
        for k, (y, one, three) in enumerate(orders):
            peer = (col ^ (core + 2 * y)) * n_row + (row ^ one ^ 3 * three)
            for b in range(per_piece):
                out_ref[k * per_piece + b] = turned[peer, :, b * orb : (b + 1) * orb]
    ids = cols_ref[...]
    piece = jnp.zeros_like(ids)
    for c in range(1, n_col):
        piece += (ids >= c * per_piece).astype(jnp.int32)
    ids = ids - piece * per_piece + (piece * n_row + row) * per_piece
    known_ref[0] = ids.astype(jnp.float32).astype(known_ref.dtype)


def place(g, f):
    return (f >> 1) * 8 + ((f & 1) ^ (f >> 1)) * 4 + g


def multiply(t, groups, across, ids_ref, z, straight, scattered):
    tile_rows = z.shape[0] // len(groups)
    orb = z.shape[2]
    for g, group in enumerate(groups):
        if not group:
            continue
        here = across[g] * tile_rows + t
        places = [(tile, t * PER_ROW + p) for tile in group for p in range(PER_ROW)]
        strip = jnp.concatenate([s[i, slot] for (_, s, i, _, _), slot in places], axis=1)
        turned = jnp.concatenate([st[i, slot] for (_, _, _, st, i), slot in places], axis=0)
        where = [ids_ref[place(g, f), slot] for (f, *_), slot in places]
        wide = jnp.concatenate([z[u] for u in where], axis=1)
        straight[here] = jnp.dot(wide, turned, preferred_element_type=jnp.float32)
        mirrored = jnp.dot(z[here], strip, preferred_element_type=jnp.float32)
        for i, u in enumerate(where):
            scattered[i % len(scattered)][u] += mirrored[:, i * orb : (i + 1) * orb]


def clear(refs):
    for ref in refs:
        ref[...] = jnp.zeros_like(ref)


def turn(s_ref, st_ref, i, start, count):
    def four(k, carry):
        for m in range(4):
            st_ref[i, start + 4 * k + m] = s_ref[i, start + 4 * k + m].T
        return carry

    lax.fori_loop(0, count // 4, four, 0)


def load_kernel(count, *refs):
    bufs, (s_ref, st_ref, sems) = refs[:count], refs[count:]
    copies = [pltpu.make_async_copy(buf, s_ref.at[i], sems.at[i]) for i, buf in enumerate(bufs)]
    for copy in copies:
        copy.start()
    for i, copy in enumerate(copies):
        copy.wait()
        turn(s_ref, st_ref, i, 0, s_ref.shape[1])


def load(bufs):
    out = jax.ShapeDtypeStruct((len(bufs), *bufs[0].shape), bufs[0].dtype)
    size = len(bufs) * bufs[0].size
    return pl.pallas_call(
        functools.partial(load_kernel, len(bufs)),
        out_shape=[out, out],
        in_specs=anywhere(len(bufs)),
        out_specs=vmem(2),
        scratch_shapes=[pltpu.SemaphoreType.DMA((len(bufs),))],
        compiler_params=pltpu.CompilerParams(vmem_limit_bytes=2**20),
        cost_estimate=pl.CostEstimate(flops=0, bytes_accessed=6 * size, transcendentals=0),
    )(*bufs)


def filter_kernel(early, late, n_col, n_row, ids_ref, zt_ref, se_ref, ste_ref, *refs):
    bufs, (out_ref, s_ref, st_ref, z, now, prev, straight, *scattered, sems) = (
        refs[: len(late)],
        refs[len(late) :],
    )
    n_blocks, share, orb = z.shape
    slots = s_ref.shape[1]
    per_piece = n_blocks // (n_col * n_row)
    tile_rows = slots // PER_ROW
    across = [lax.axis_index("col") ^ g for g in range(n_col)]
    down = [lax.axis_index("row") ^ f for f in range(n_row)]
    rest = sorted({(g, f) for g, f, _ in late})

    copies = []
    for i, (buf, (g, f, start)) in enumerate(zip(bufs, late)):
        target = s_ref.at[rest.index((g, f)), pl.ds(start, buf.shape[0])]
        copies.append(pltpu.make_async_copy(buf, target, sems.at[i]))
        copies[-1].start()
    for g in range(n_col):
        for f in range(n_row):
            for b in range(per_piece):
                u = (across[g] * n_row + down[f]) * per_piece + b
                own = zt_ref[place(g, f), b]
                z[u] = own
                now[u] = own.astype(jnp.float32)
    clear([prev])
    for copy, buf, (g, f, start) in zip(copies, bufs, late):
        copy.wait()
        turn(s_ref, st_ref, rest.index((g, f)), start, buf.shape[0])

    tiles = {at: (se_ref, i, ste_ref, i) for i, at in enumerate(early)}
    tiles.update({at: (s_ref, i, st_ref, i) for i, at in enumerate(rest)})
    groups = [[(f, *tiles[g, f]) for f in range(n_row)] for g in range(n_col)]

    def one_step(step, carry):
        clear(scattered)

        def block_row(t, carry):
            multiply(t, groups, across, ids_ref, z, straight, scattered)
            return carry

        lax.fori_loop(0, tile_rows, block_row, 0)
        total = straight[...]
        for ref in scattered:
            total += ref[...]
        later = step > 0
        total = jnp.where(later, 2.0, 1.0) * total - jnp.where(later, 1.0, 0.0) * prev[...]
        prev[...] = now[...]
        now[...] = total
        z[...] = total.astype(z.dtype)
        return carry

    lax.fori_loop(0, DEG, one_step, 0)
    for p in range(n_col * n_row):
        for b in range(per_piece):
            u = p * per_piece + b
            out_ref[p, 0, :, b * orb : (b + 1) * orb] = now[u].astype(out_ref.dtype)
            out_ref[p, 1, :, b * orb : (b + 1) * orb] = prev[u].astype(out_ref.dtype)


def gather_plan(vectors, blocks, cols):
    n_dev = lax.axis_size(LANES)
    n_col, n_row = lax.axis_size("col"), lax.axis_size("row")
    rows, width = vectors.shape
    slots, orb = blocks.shape[2:4]
    share = width // n_dev
    per_piece = rows // orb
    n_blocks = n_dev * per_piece
    half = slots // 2

    def send(buf, flip_col, flip_row, from_rows=range(n_row)):
        pairs = [
            (c * n_row + r, (c ^ flip_col) * n_row + (r ^ flip_row))
            for c in range(n_col)
            for r in from_rows
        ]
        return lax.ppermute(buf, LANES, pairs)

    def to_mate(*bufs):
        return [send(buf, 1, 0) for buf in bufs]

    own = blocks[0, 0]
    near = send(own, 0, 1)
    inner = send(own, 0, 3, (1, 2))
    over_own = send(own, 2, 0)

    own_cols = jnp.broadcast_to(jnp.pad(cols[0, 0], (0, orb - slots)), (share, orb))
    shares = jax.ShapeDtypeStruct((n_dev // 2 * per_piece, share, orb), vectors.dtype)
    keep, go, known = pl.pallas_call(
        functools.partial(split_kernel, n_col, n_row),
        out_shape=[shares, shares, jax.ShapeDtypeStruct((1, share, orb), vectors.dtype)],
        in_specs=vmem(2),
        out_specs=vmem(3),
        scratch_shapes=[pltpu.VMEM((n_dev, share, rows), vectors.dtype)],
        compiler_params=pltpu.CompilerParams(vmem_limit_bytes=4 * 2**20),
    )(vectors, own_cols)

    def swap(keep, go, flip_col, flip_row):
        (keep, known), count = keep, go.shape[0]
        came = send(jnp.concatenate([go, known]), flip_col, flip_row)
        return jnp.concatenate([keep, came[:count]]), jnp.concatenate([known, came[count:]])

    parts = swap((keep, known), go, 1, 0)

    near = after(near, over_own, parts[0])
    outer = send(copy_after(own, near), 0, 3, (0, 3))
    over_near = send(near, 2, 0)
    mine, known = parts
    mine = mine.reshape(2, 2, -1, share, orb)
    parts = swap((mine[:, 0].reshape(-1, share, orb), known), mine[:, 1].reshape(-1, share, orb), 2, 0)
    mates = to_mate(own, near, over_own)
    far = pick((1, 2), inner, outer, over_near, parts[0], *mates)

    over_far = send(far, 2, 0)
    last = send(far, 0, 1)
    mine, known = parts
    mine = mine.reshape(n_col, n_row, -1, share, orb)
    parts = [(mine[:, 0].reshape(-1, share, orb), known)]
    for one, three in ((1, 0), (0, 1), (1, 1)):
        go = mine[:, 2 * one + three].reshape(-1, share, orb)
        came = send(jnp.concatenate([go, known]), 0, one ^ 3 * three)
        parts.append((came[: go.shape[0]], came[go.shape[0] :]))
    mine = jnp.concatenate([part for part, _ in parts])
    ids = jnp.concatenate([known[:, 0, :slots].astype(jnp.int32) for _, known in parts])
    mates += to_mate(far, over_near)
    last = after(last, over_far, mine, *mates[3:])

    over_last = send(last[:half], 2, 0)
    side_last = send(over_far[half:], 0, 1)
    mates += to_mate(last, over_far)
    se, ste = load([own, near, over_own, far, over_near, last, over_far, *mates])
    over_last, side_last = after(over_last, se), after(side_last, se)

    early = [(0, 0), (0, 1), (2, 0), (0, 3), (2, 1), (0, 2), (2, 3)]
    early += [(g ^ 1, f) for g, f in early]
    late = [(2, 2, 0), (2, 2, half), (3, 2, 0), (3, 2, half)]
    late_bufs = [over_last, side_last, *to_mate(over_last, side_last)]

    done = pl.pallas_call(
        functools.partial(filter_kernel, early, late, n_col, n_row),
        out_shape=jax.ShapeDtypeStruct((n_dev, 2, share, rows), jnp.bfloat16),
        in_specs=smem() + vmem(3) + anywhere(len(late)),
        out_specs=vmem()[0],
        scratch_shapes=[
            *[pltpu.VMEM((n_dev - len(early), slots, orb, orb), blocks.dtype)] * 2,
            pltpu.VMEM((n_blocks, share, orb), jnp.bfloat16),
            *[pltpu.VMEM((n_blocks, share, orb), jnp.float32)] * (3 + SPLIT),
            pltpu.SemaphoreType.DMA((len(late),)),
        ],
        compiler_params=pltpu.CompilerParams(vmem_limit_bytes=12 * 2**20),
    )(
        ids,
        mine.reshape(n_dev, per_piece, share, orb),
        se,
        ste,
        *late_bufs,
    )
    back = lax.all_to_all(done, LANES, split_axis=0, concat_axis=0, tiled=True)
    outs = jnp.transpose(back, (1, 3, 0, 2)).reshape(2, rows, width).astype(jnp.float32)
    return outs[0], outs[1]


def per_device(vectors, blocks, cols):
    n_dev = lax.axis_size(LANES)
    line_of_four = lax.axis_size("col") == 4 and lax.axis_size("row") == 4
    if line_of_four and n_dev * blocks.size * blocks.dtype.itemsize <= GATHER_LIMIT:
        return gather_plan(vectors, blocks, cols)
    return spread_plan(vectors, blocks, cols)


def solution(mesh):
    return jax.shard_map(
        per_device,
        mesh=mesh,
        in_specs=(
            P(("col", "row"), "dom"),
            P(("dom", "col"), "row", None, None, None),
            P(("dom", "col"), "row", None),
        ),
        out_specs=(P(("col", "row"), "dom"), P(("col", "row"), "dom")),
        check_vma=False,
    )
```

```python
import functools

import jax
import jax.numpy as jnp
from jax import lax
from jax.experimental import pallas as pl
from jax.experimental.pallas import tpu as pltpu
from jax.sharding import PartitionSpec as P

PER_ROW = 2
DEG = 4
SPLIT = 4
GATHER_LIMIT = 12 * 2**20
LANES = ("col", "row")


def onehot_sum(selected, high_part, low_part):
    first = jnp.einsum("su,sok->uok", selected, high_part, preferred_element_type=jnp.float32)
    second = jnp.einsum("su,sok->uok", selected, low_part, preferred_element_type=jnp.float32)
    return first + second


def apply_pair(send, grouped, col_ids, onehot):
    tile_rows, per_row, orb, _ = grouped.shape
    piece_rows, width = send.shape
    tile_cols = onehot.shape[1]
    wide = lax.all_gather(send, "col", axis=0, tiled=True).reshape(tile_cols, orb, width)
    picked = jnp.take(wide, col_ids, axis=0).reshape(tile_rows, per_row, orb, width)
    direct = jnp.einsum("tpio,tpok->tik", grouped, picked, preferred_element_type=jnp.float32)
    part_rows = lax.psum_scatter(
        direct.reshape(tile_rows * orb, width).astype(jnp.bfloat16),
        "row",
        scatter_dimension=0,
        tiled=True,
    ).astype(jnp.float32)
    tall = lax.all_gather(send, "row", axis=0, tiled=True).reshape(tile_rows, orb, width)
    mirrored = jnp.einsum("tpio,tik->tpok", grouped, tall, preferred_element_type=jnp.float32)
    mirrored = mirrored.reshape(tile_rows * per_row, orb, width)
    high_part = mirrored.astype(jnp.bfloat16)
    low_part = (mirrored - high_part.astype(jnp.float32)).astype(jnp.bfloat16)
    summed = onehot_sum(onehot, high_part, low_part)
    part_cols = lax.psum_scatter(
        summed.reshape(tile_cols * orb, width).astype(jnp.bfloat16),
        "col",
        scatter_dimension=0,
        tiled=True,
    ).astype(jnp.float32)
    return part_rows + part_cols


def spread_plan(vectors, blocks, cols):
    tiles = blocks[0, 0]
    col_ids = cols[0, 0]
    slots, orb, _ = tiles.shape
    tile_rows = slots // PER_ROW
    tile_cols = lax.axis_size("col") * (vectors.shape[0] // orb)
    grouped = tiles.reshape(tile_rows, PER_ROW, orb, orb)
    onehot = (col_ids[:, None] == jnp.arange(tile_cols, dtype=jnp.int32)[None, :]).astype(
        jnp.bfloat16
    )
    prev = vectors.astype(jnp.float32)
    now = apply_pair(vectors, grouped, col_ids, onehot)
    for step in range(DEG - 1):
        nxt = 2.0 * apply_pair(now.astype(jnp.bfloat16), grouped, col_ids, onehot) - prev
        prev, now = (now, nxt)
    return (now, prev)


def filter_kernel(per_piece, n_row, ids_ref, zt_ref, lower_ref, upper_ref, *refs):
    out_ref, s_ref, st_ref, z, now, prev, straight, *scattered, sems = refs
    tiles, slots = s_ref.shape[:2]
    orb = s_ref.shape[2]
    tile_rows = slots // PER_ROW
    pieces = zt_ref.shape[0]

    half = slots // 2
    for tile in range(tiles):
        other = tile % n_row * (tiles // n_row) + tile // n_row
        pltpu.make_async_copy(lower_ref.at[tile], s_ref.at[tile, pl.ds(0, half)], sems.at[tile]).start()
        pltpu.make_async_copy(upper_ref.at[other], s_ref.at[tile, pl.ds(half, half)], sems.at[tile]).start()

    for p in range(pieces):
        for b in range(per_piece):
            own = zt_ref[p, :, b * orb : (b + 1) * orb]
            z[p * per_piece + b] = own
            now[p * per_piece + b] = own.astype(jnp.float32)
    prev[...] = jnp.zeros_like(prev)

    def row_group(step, across, carry):
        group = [across * n_row + r for r in range(n_row)]

        @pl.when(step == 0)
        def _():
            for tile in group:
                pltpu.make_async_copy(s_ref.at[tile], s_ref.at[tile], sems.at[tile]).wait()
                for slot in range(slots):
                    st_ref[tile, slot] = s_ref[tile, slot].T

        for t in range(tile_rows):
            places = [(tile, t * PER_ROW + p) for tile in group for p in range(PER_ROW)]
            strip = jnp.concatenate([s_ref[tile, slot] for tile, slot in places], axis=1)
            turned_strip = jnp.concatenate([st_ref[tile, slot] for tile, slot in places], axis=0)
            where = [ids_ref[tile, slot] for tile, slot in places]
            wide = jnp.concatenate([z[g] for g in where], axis=1)
            tall = z[across * tile_rows + t]
            straight[across * tile_rows + t] = jnp.dot(
                wide, turned_strip, preferred_element_type=jnp.float32
            )
            turned = jnp.dot(tall, strip, preferred_element_type=jnp.float32)
            for i, g in enumerate(where):
                scattered[i % len(scattered)][g] += turned[:, i * orb : (i + 1) * orb]
        return carry

    def one_step(step, carry):
        for ref in scattered:
            ref[...] = jnp.zeros_like(ref)
        lax.fori_loop(0, tiles // n_row, functools.partial(row_group, step), 0)
        total = straight[...]
        for ref in scattered:
            total += ref[...]
        later = step > 0
        total = jnp.where(later, 2.0, 1.0) * total - jnp.where(later, 1.0, 0.0) * prev[...]
        prev[...] = now[...]
        now[...] = total
        z[...] = total.astype(z.dtype)
        return carry

    lax.fori_loop(0, DEG, one_step, 0)
    for p in range(pieces):
        for b in range(per_piece):
            g = p * per_piece + b
            out_ref[p, 0, :, b * orb : (b + 1) * orb] = now[g].astype(out_ref.dtype)
            out_ref[p, 1, :, b * orb : (b + 1) * orb] = prev[g].astype(out_ref.dtype)


def gather_plan(vectors, blocks, cols):
    n_dev = lax.axis_size(LANES)
    n_row = lax.axis_size("row")
    rows, width = vectors.shape
    slots, orb = blocks.shape[2:4]
    share = width // n_dev
    per_piece = rows // orb
    n_blocks = n_dev * per_piece
    half = slots // 2
    bufs = [
        lax.all_gather(blocks[0, 0, :half], LANES, axis=0),
        lax.all_gather(blocks[0, 0, half:], LANES[::-1], axis=0),
    ]

    turned = vectors.T.reshape(n_dev, share, rows)
    own_ids = jnp.pad(cols[0, 0].astype(jnp.bfloat16), (0, rows - slots))
    own_ids = jnp.broadcast_to(own_ids, (n_dev, share, rows))
    both = lax.all_to_all(
        jnp.concatenate([turned, own_ids], axis=1), LANES, split_axis=0, concat_axis=0, tiled=True
    )
    zt = both[:, :share]
    local = both[:, share, :slots].astype(jnp.int32)
    down = (jnp.arange(n_dev, dtype=jnp.int32) % n_row)[:, None]
    ids = (local // per_piece * n_row + down) * per_piece + local % per_piece

    done = pl.pallas_call(
        functools.partial(filter_kernel, per_piece, n_row),
        out_shape=jax.ShapeDtypeStruct((n_dev, 2, share, rows), jnp.bfloat16),
        in_specs=[
            pl.BlockSpec(memory_space=pltpu.SMEM),
            pl.BlockSpec(memory_space=pltpu.VMEM),
        ]
        + [pl.BlockSpec(memory_space=pl.ANY)] * len(bufs),
        out_specs=pl.BlockSpec(memory_space=pltpu.VMEM),
        scratch_shapes=[
            pltpu.VMEM((n_dev, slots, orb, orb), blocks.dtype),
            pltpu.VMEM((n_dev, slots, orb, orb), blocks.dtype),
            pltpu.VMEM((n_blocks, share, orb), jnp.bfloat16),
            *[pltpu.VMEM((n_blocks, share, orb), jnp.float32)] * (3 + SPLIT),
            pltpu.SemaphoreType.DMA((n_dev,)),
        ],
        compiler_params=pltpu.CompilerParams(vmem_limit_bytes=58 * 2**20),
    )(ids, zt, *bufs)
    back = lax.all_to_all(done, LANES, split_axis=0, concat_axis=0, tiled=True)
    outs = jnp.transpose(back, (1, 3, 0, 2)).reshape(2, rows, width).astype(jnp.float32)
    return outs[0], outs[1]


def per_device(vectors, blocks, cols):
    n_dev = lax.axis_size(LANES)
    line_of_four = lax.axis_size("col") == 4 and lax.axis_size("row") == 4
    if line_of_four and n_dev * blocks.size * blocks.dtype.itemsize <= GATHER_LIMIT:
        return gather_plan(vectors, blocks, cols)
    return spread_plan(vectors, blocks, cols)


def solution(mesh):
    return jax.shard_map(
        per_device,
        mesh=mesh,
        in_specs=(
            P(("col", "row"), "dom"),
            P(("dom", "col"), "row", None, None, None),
            P(("dom", "col"), "row", None),
        ),
        out_specs=(P(("col", "row"), "dom"), P(("col", "row"), "dom")),
        check_vma=False,
    )
```

```python
import functools

import jax
import jax.numpy as jnp
from jax import lax
from jax.experimental import pallas as pl
from jax.experimental.pallas import tpu as pltpu
from jax.sharding import PartitionSpec as P

PER_ROW = 2
DEG = 4
SPLIT = 4
GATHER_LIMIT = 12 * 2**20
LANES = ("col", "row")


def onehot_sum(selected, high_part, low_part):
    first = jnp.einsum("su,sok->uok", selected, high_part, preferred_element_type=jnp.float32)
    second = jnp.einsum("su,sok->uok", selected, low_part, preferred_element_type=jnp.float32)
    return first + second


def apply_pair(send, grouped, col_ids, onehot):
    tile_rows, per_row, orb, _ = grouped.shape
    piece_rows, width = send.shape
    tile_cols = onehot.shape[1]
    wide = lax.all_gather(send, "col", axis=0, tiled=True).reshape(tile_cols, orb, width)
    picked = jnp.take(wide, col_ids, axis=0).reshape(tile_rows, per_row, orb, width)
    direct = jnp.einsum("tpio,tpok->tik", grouped, picked, preferred_element_type=jnp.float32)
    part_rows = lax.psum_scatter(
        direct.reshape(tile_rows * orb, width).astype(jnp.bfloat16),
        "row",
        scatter_dimension=0,
        tiled=True,
    ).astype(jnp.float32)
    tall = lax.all_gather(send, "row", axis=0, tiled=True).reshape(tile_rows, orb, width)
    mirrored = jnp.einsum("tpio,tik->tpok", grouped, tall, preferred_element_type=jnp.float32)
    mirrored = mirrored.reshape(tile_rows * per_row, orb, width)
    high_part = mirrored.astype(jnp.bfloat16)
    low_part = (mirrored - high_part.astype(jnp.float32)).astype(jnp.bfloat16)
    summed = onehot_sum(onehot, high_part, low_part)
    part_cols = lax.psum_scatter(
        summed.reshape(tile_cols * orb, width).astype(jnp.bfloat16),
        "col",
        scatter_dimension=0,
        tiled=True,
    ).astype(jnp.float32)
    return part_rows + part_cols


def spread_plan(vectors, blocks, cols):
    tiles = blocks[0, 0]
    col_ids = cols[0, 0]
    slots, orb, _ = tiles.shape
    tile_rows = slots // PER_ROW
    tile_cols = lax.axis_size("col") * (vectors.shape[0] // orb)
    grouped = tiles.reshape(tile_rows, PER_ROW, orb, orb)
    onehot = (col_ids[:, None] == jnp.arange(tile_cols, dtype=jnp.int32)[None, :]).astype(
        jnp.bfloat16
    )
    prev = vectors.astype(jnp.float32)
    now = apply_pair(vectors, grouped, col_ids, onehot)
    for step in range(DEG - 1):
        nxt = 2.0 * apply_pair(now.astype(jnp.bfloat16), grouped, col_ids, onehot) - prev
        prev, now = (now, nxt)
    return (now, prev)


def vmem(count=1):
    return [pl.BlockSpec(memory_space=pltpu.VMEM)] * count


def smem(count=1):
    return [pl.BlockSpec(memory_space=pltpu.SMEM)] * count


def anywhere(count=1):
    return [pl.BlockSpec(memory_space=pl.ANY)] * count


def nothing(*refs):
    pass


def after(value, *others):
    return pl.pallas_call(
        nothing,
        out_shape=jax.ShapeDtypeStruct(value.shape, value.dtype),
        in_specs=anywhere(1 + len(others)),
        out_specs=anywhere()[0],
        input_output_aliases={0: 0},
        compiler_params=pltpu.CompilerParams(vmem_limit_bytes=2**20),
    )(value, *others)


def copy_kernel(value_ref, *refs):
    out_ref, sem = refs[-2:]
    copy = pltpu.make_async_copy(value_ref, out_ref, sem)
    copy.start()
    copy.wait()


def copy_after(value, *others):
    return pl.pallas_call(
        copy_kernel,
        out_shape=jax.ShapeDtypeStruct(value.shape, value.dtype),
        in_specs=[pl.BlockSpec(memory_space=pltpu.HBM)] + anywhere(len(others)),
        out_specs=anywhere()[0],
        scratch_shapes=[pltpu.SemaphoreType.DMA(())],
        compiler_params=pltpu.CompilerParams(vmem_limit_bytes=2**20),
    )(value, *others)


def pick_kernel(rows, one_ref, other_ref, *refs):
    out_ref, sem = refs[-2:]
    row = lax.axis_index("row")
    first = (row == rows[0]) | (row == rows[1])

    @pl.when(first)
    def _():
        copy = pltpu.make_async_copy(one_ref, out_ref, sem)
        copy.start()
        copy.wait()

    @pl.when(jnp.logical_not(first))
    def _():
        copy = pltpu.make_async_copy(other_ref, out_ref, sem)
        copy.start()
        copy.wait()


def pick(rows, one, other, *others):
    return pl.pallas_call(
        functools.partial(pick_kernel, rows),
        out_shape=jax.ShapeDtypeStruct(one.shape, one.dtype),
        in_specs=anywhere(2 + len(others)),
        out_specs=anywhere()[0],
        scratch_shapes=[pltpu.SemaphoreType.DMA(())],
        compiler_params=pltpu.CompilerParams(vmem_limit_bytes=2**20),
    )(one, other, *others)


def split_kernel(n_col, n_row, vectors_ref, cols_ref, stay_ref, go_ref, turned):
    col, row = lax.axis_index("col"), lax.axis_index("row")
    count, share, rows = turned.shape
    orb = stay_ref.shape[2]
    per_piece = rows // orb
    whole = vectors_ref[...].T
    for d in range(count):
        turned[d] = whole[d * share : (d + 1) * share]
    orders = [(y, one, three) for y in range(2) for one in range(2) for three in range(2)]
    ids = cols_ref[...]
    piece = jnp.zeros_like(ids)
    for c in range(1, n_col):
        piece += (ids >= c * per_piece).astype(jnp.int32)
    ids = ids - piece * per_piece + (piece * n_row + row) * per_piece
    for core, out_ref in enumerate((stay_ref, go_ref)):
        for k, (y, one, three) in enumerate(orders):
            peer = (col ^ (core + 2 * y)) * n_row + (row ^ one ^ 3 * three)
            for b in range(per_piece):
                out_ref[k * per_piece + b] = turned[peer, :, b * orb : (b + 1) * orb]
        out_ref[len(orders) * per_piece] = ids.astype(jnp.float32).astype(out_ref.dtype)


def regroup_kernel(sources, count, stay_ref, came_ref, *outs):
    per_piece = (stay_ref.shape[0] - sources) // (sources * count)
    kept = max(count // 2, 1)
    for h, out_ref in enumerate(outs):
        for s in range(2 * sources):
            ref = stay_ref if s < sources else came_ref
            ids = ref[sources * count * per_piece + s % sources]
            if h == 1 and count == 1:
                out_ref[s : s + 1] = ids.astype(jnp.float32)[:1].astype(jnp.int32)
                continue
            for k in range(kept * per_piece):
                out_ref[s * kept * per_piece + k] = ref[(s % sources * count + h * kept) * per_piece + k]
            if count > 1:
                out_ref[2 * sources * kept * per_piece + s] = ids


def regroup(stay, came, sources, per_piece):
    count = (stay.shape[0] // sources - 1) // per_piece
    _, share, orb = stay.shape
    if count > 1:
        out = jax.ShapeDtypeStruct((sources * count * per_piece + 2 * sources, share, orb), stay.dtype)
        outs = [out, out]
    else:
        outs = [
            jax.ShapeDtypeStruct((2 * sources * per_piece, share, orb), stay.dtype),
            jax.ShapeDtypeStruct((2 * sources, orb), jnp.int32),
        ]
    return pl.pallas_call(
        functools.partial(regroup_kernel, sources, count),
        out_shape=outs,
        in_specs=vmem(2),
        out_specs=vmem(2),
        compiler_params=pltpu.CompilerParams(vmem_limit_bytes=2**20),
    )(stay, came)


def place(g, f):
    return (f >> 1) * 8 + ((f & 1) ^ (f >> 1)) * 4 + g


def multiply(t, groups, across, ids_ref, z, straight, scattered):
    tile_rows = z.shape[0] // len(groups)
    orb = z.shape[2]
    for g, group in enumerate(groups):
        if not group:
            continue
        here = across[g] * tile_rows + t
        places = [(tile, t * PER_ROW + p) for tile in group for p in range(PER_ROW)]
        strip = jnp.concatenate([s[i, slot] for (_, s, i, _, _), slot in places], axis=1)
        turned = jnp.concatenate([st[i, slot] for (_, _, _, st, i), slot in places], axis=0)
        where = [ids_ref[place(g, f), slot] for (f, *_), slot in places]
        wide = jnp.concatenate([z[u] for u in where], axis=1)
        straight[here] = jnp.dot(wide, turned, preferred_element_type=jnp.float32)
        mirrored = jnp.dot(z[here], strip, preferred_element_type=jnp.float32)
        for i, u in enumerate(where):
            scattered[i % len(scattered)][u] += mirrored[:, i * orb : (i + 1) * orb]


def clear(refs):
    for ref in refs:
        ref[...] = jnp.zeros_like(ref)


def turn(s_ref, st_ref, i, start, count):
    def four(k, carry):
        for m in range(4):
            st_ref[i, start + 4 * k + m] = s_ref[i, start + 4 * k + m].T
        return carry

    lax.fori_loop(0, count // 4, four, 0)


def load_kernel(count, *refs):
    bufs, (s_ref, st_ref, sems) = refs[:count], refs[count:]
    copies = [pltpu.make_async_copy(buf, s_ref.at[i], sems.at[i]) for i, buf in enumerate(bufs)]
    for copy in copies:
        copy.start()
    for i, copy in enumerate(copies):
        copy.wait()
        turn(s_ref, st_ref, i, 0, s_ref.shape[1])


def load(bufs):
    out = jax.ShapeDtypeStruct((len(bufs), *bufs[0].shape), bufs[0].dtype)
    size = len(bufs) * bufs[0].size
    return pl.pallas_call(
        functools.partial(load_kernel, len(bufs)),
        out_shape=[out, out],
        in_specs=anywhere(len(bufs)),
        out_specs=vmem(2),
        scratch_shapes=[pltpu.SemaphoreType.DMA((len(bufs),))],
        compiler_params=pltpu.CompilerParams(vmem_limit_bytes=2**20),
        cost_estimate=pl.CostEstimate(flops=0, bytes_accessed=6 * size, transcendentals=0),
    )(*bufs)


def filter_kernel(early, late, n_col, n_row, ids_ref, zt_ref, se_ref, ste_ref, *refs):
    bufs, (out_ref, s_ref, st_ref, z, now, prev, straight, *scattered, sems) = (
        refs[: len(late)],
        refs[len(late) :],
    )
    n_blocks, share, orb = z.shape
    slots = s_ref.shape[1]
    per_piece = n_blocks // (n_col * n_row)
    tile_rows = slots // PER_ROW
    across = [lax.axis_index("col") ^ g for g in range(n_col)]
    down = [lax.axis_index("row") ^ f for f in range(n_row)]
    rest = sorted({(g, f) for g, f, _ in late})

    copies = []
    for i, (buf, (g, f, start)) in enumerate(zip(bufs, late)):
        target = s_ref.at[rest.index((g, f)), pl.ds(start, buf.shape[0])]
        copies.append(pltpu.make_async_copy(buf, target, sems.at[i]))
        copies[-1].start()
    for g in range(n_col):
        for f in range(n_row):
            for b in range(per_piece):
                u = (across[g] * n_row + down[f]) * per_piece + b
                own = zt_ref[place(g, f), b]
                z[u] = own
                now[u] = own.astype(jnp.float32)
    clear([prev])
    for copy, buf, (g, f, start) in zip(copies, bufs, late):
        copy.wait()
        turn(s_ref, st_ref, rest.index((g, f)), start, buf.shape[0])

    tiles = {at: (se_ref, i, ste_ref, i) for i, at in enumerate(early)}
    tiles.update({at: (s_ref, i, st_ref, i) for i, at in enumerate(rest)})
    groups = [[(f, *tiles[g, f]) for f in range(n_row)] for g in range(n_col)]

    def one_step(step, carry):
        clear(scattered)

        def block_row(t, carry):
            multiply(t, groups, across, ids_ref, z, straight, scattered)
            return carry

        lax.fori_loop(0, tile_rows, block_row, 0)
        total = straight[...]
        for ref in scattered:
            total += ref[...]
        later = step > 0
        total = jnp.where(later, 2.0, 1.0) * total - jnp.where(later, 1.0, 0.0) * prev[...]
        prev[...] = now[...]
        now[...] = total
        z[...] = total.astype(z.dtype)
        return carry

    lax.fori_loop(0, DEG, one_step, 0)
    for p in range(n_col * n_row):
        for b in range(per_piece):
            u = p * per_piece + b
            out_ref[p, 0, :, b * orb : (b + 1) * orb] = now[u].astype(out_ref.dtype)
            out_ref[p, 1, :, b * orb : (b + 1) * orb] = prev[u].astype(out_ref.dtype)


def result_kernel(back_ref, last_ref, before_ref):
    count, _, share, rows = back_ref.shape
    for i, out_ref in enumerate((last_ref, before_ref)):
        whole = jnp.concatenate([back_ref[d, i] for d in range(count)], axis=0)
        out_ref[...] = whole.astype(jnp.float32).T


def gather_plan(vectors, blocks, cols):
    n_dev = lax.axis_size(LANES)
    n_col, n_row = lax.axis_size("col"), lax.axis_size("row")
    rows, width = vectors.shape
    slots, orb = blocks.shape[2:4]
    share = width // n_dev
    per_piece = rows // orb
    n_blocks = n_dev * per_piece
    half = slots // 2

    def send(buf, flip_col, flip_row, from_rows=range(n_row)):
        pairs = [
            (c * n_row + r, (c ^ flip_col) * n_row + (r ^ flip_row))
            for c in range(n_col)
            for r in from_rows
        ]
        return lax.ppermute(buf, LANES, pairs)

    def to_mate(*bufs):
        return [send(buf, 1, 0) for buf in bufs]

    own = blocks[0, 0]
    near = send(own, 0, 1)
    inner = send(own, 0, 3, (1, 2))
    over_own = send(own, 2, 0)

    own_cols = jnp.broadcast_to(jnp.pad(cols[0, 0], (0, orb - slots)), (share, orb))
    shares = jax.ShapeDtypeStruct((n_dev // 2 * per_piece + 1, share, orb), vectors.dtype)
    stay, go = pl.pallas_call(
        functools.partial(split_kernel, n_col, n_row),
        out_shape=[shares, shares],
        in_specs=vmem(2),
        out_specs=vmem(2),
        scratch_shapes=[pltpu.VMEM((n_dev, share, rows), vectors.dtype)],
        compiler_params=pltpu.CompilerParams(vmem_limit_bytes=4 * 2**20),
    )(vectors, own_cols)
    stay, go = regroup(stay, send(go, 1, 0), 1, per_piece)

    near = after(near, over_own)
    outer = send(copy_after(own, near), 0, 3, (0, 3))
    over_near = send(near, 2, 0)
    stay, go = regroup(stay, send(go, 2, 0), 2, per_piece)
    stay, go = regroup(stay, send(go, 0, 1), 4, per_piece)
    mates = to_mate(own, near, over_own)
    far = pick((1, 2), inner, outer, over_near, go, *mates)

    over_far = send(far, 2, 0)
    last = send(far, 0, 1)
    mates += to_mate(far, over_near)
    mine, ids = regroup(stay, send(go, 0, 3), 8, per_piece)
    last = after(last, over_far, mine, *mates[3:])

    over_last = send(last[:half], 2, 0)
    side_last = send(over_far[half:], 0, 1)
    mates += to_mate(last, over_far)
    se, ste = load([own, near, over_own, far, over_near, last, over_far, *mates])
    over_last, side_last = after(over_last, se), after(side_last, se)

    early = [(0, 0), (0, 1), (2, 0), (0, 3), (2, 1), (0, 2), (2, 3)]
    early += [(g ^ 1, f) for g, f in early]
    late = [(2, 2, 0), (2, 2, half), (3, 2, 0), (3, 2, half)]
    late_bufs = [over_last, side_last, *to_mate(over_last, side_last)]

    done = pl.pallas_call(
        functools.partial(filter_kernel, early, late, n_col, n_row),
        out_shape=jax.ShapeDtypeStruct((n_dev, 2, share, rows), jnp.bfloat16),
        in_specs=smem() + vmem(3) + anywhere(len(late)),
        out_specs=vmem()[0],
        scratch_shapes=[
            *[pltpu.VMEM((n_dev - len(early), slots, orb, orb), blocks.dtype)] * 2,
            pltpu.VMEM((n_blocks, share, orb), jnp.bfloat16),
            *[pltpu.VMEM((n_blocks, share, orb), jnp.float32)] * (3 + SPLIT),
            pltpu.SemaphoreType.DMA((len(late),)),
        ],
        compiler_params=pltpu.CompilerParams(vmem_limit_bytes=12 * 2**20),
    )(
        ids,
        mine.reshape(n_dev, per_piece, share, orb),
        se,
        ste,
        *late_bufs,
    )
    back = lax.all_to_all(done, LANES, split_axis=0, concat_axis=0, tiled=True)
    whole = jax.ShapeDtypeStruct((rows, width), jnp.float32)
    return pl.pallas_call(
        result_kernel,
        out_shape=[whole, whole],
        in_specs=vmem(),
        out_specs=vmem(2),
        compiler_params=pltpu.CompilerParams(vmem_limit_bytes=4 * 2**20),
    )(back)


def per_device(vectors, blocks, cols):
    n_dev = lax.axis_size(LANES)
    line_of_four = lax.axis_size("col") == 4 and lax.axis_size("row") == 4
    if line_of_four and n_dev * blocks.size * blocks.dtype.itemsize <= GATHER_LIMIT:
        return gather_plan(vectors, blocks, cols)
    return spread_plan(vectors, blocks, cols)


def solution(mesh):
    return jax.shard_map(
        per_device,
        mesh=mesh,
        in_specs=(
            P(("col", "row"), "dom"),
            P(("dom", "col"), "row", None, None, None),
            P(("dom", "col"), "row", None),
        ),
        out_specs=(P(("col", "row"), "dom"), P(("col", "row"), "dom")),
        check_vma=False,
    )
```

```python
import functools

import jax
import jax.numpy as jnp
from jax import lax
from jax.experimental import pallas as pl
from jax.experimental.pallas import tpu as pltpu
from jax.sharding import PartitionSpec as P

PER_ROW = 2
DEG = 4
SPLIT = 4
GATHER_LIMIT = 12 * 2**20
LANES = ("col", "row")
INNER = (1, 2)


def onehot_sum(selected, high_part, low_part):
    first = jnp.einsum("su,sok->uok", selected, high_part, preferred_element_type=jnp.float32)
    second = jnp.einsum("su,sok->uok", selected, low_part, preferred_element_type=jnp.float32)
    return first + second


def apply_pair(send, grouped, col_ids, onehot):
    tile_rows, per_row, orb, _ = grouped.shape
    piece_rows, width = send.shape
    tile_cols = onehot.shape[1]
    wide = lax.all_gather(send, "col", axis=0, tiled=True).reshape(tile_cols, orb, width)
    picked = jnp.take(wide, col_ids, axis=0).reshape(tile_rows, per_row, orb, width)
    direct = jnp.einsum("tpio,tpok->tik", grouped, picked, preferred_element_type=jnp.float32)
    part_rows = lax.psum_scatter(
        direct.reshape(tile_rows * orb, width).astype(jnp.bfloat16),
        "row",
        scatter_dimension=0,
        tiled=True,
    ).astype(jnp.float32)
    tall = lax.all_gather(send, "row", axis=0, tiled=True).reshape(tile_rows, orb, width)
    mirrored = jnp.einsum("tpio,tik->tpok", grouped, tall, preferred_element_type=jnp.float32)
    mirrored = mirrored.reshape(tile_rows * per_row, orb, width)
    high_part = mirrored.astype(jnp.bfloat16)
    low_part = (mirrored - high_part.astype(jnp.float32)).astype(jnp.bfloat16)
    summed = onehot_sum(onehot, high_part, low_part)
    part_cols = lax.psum_scatter(
        summed.reshape(tile_cols * orb, width).astype(jnp.bfloat16),
        "col",
        scatter_dimension=0,
        tiled=True,
    ).astype(jnp.float32)
    return part_rows + part_cols


def spread_plan(vectors, blocks, cols):
    tiles = blocks[0, 0]
    col_ids = cols[0, 0]
    slots, orb, _ = tiles.shape
    tile_rows = slots // PER_ROW
    tile_cols = lax.axis_size("col") * (vectors.shape[0] // orb)
    grouped = tiles.reshape(tile_rows, PER_ROW, orb, orb)
    onehot = (col_ids[:, None] == jnp.arange(tile_cols, dtype=jnp.int32)[None, :]).astype(
        jnp.bfloat16
    )
    prev = vectors.astype(jnp.float32)
    now = apply_pair(vectors, grouped, col_ids, onehot)
    for step in range(DEG - 1):
        nxt = 2.0 * apply_pair(now.astype(jnp.bfloat16), grouped, col_ids, onehot) - prev
        prev, now = (now, nxt)
    return (now, prev)


def vmem(count=1):
    return [pl.BlockSpec(memory_space=pltpu.VMEM)] * count


def smem(count=1):
    return [pl.BlockSpec(memory_space=pltpu.SMEM)] * count


def anywhere(count=1):
    return [pl.BlockSpec(memory_space=pl.ANY)] * count


def nothing(*refs):
    pass


def after(value, *others):
    return pl.pallas_call(
        nothing,
        out_shape=jax.ShapeDtypeStruct(value.shape, value.dtype),
        in_specs=anywhere(1 + len(others)),
        out_specs=anywhere()[0],
        input_output_aliases={0: 0},
        compiler_params=pltpu.CompilerParams(vmem_limit_bytes=2**20),
    )(value, *others)


def pick_kernel(rows, one_ref, other_ref, *refs):
    out_ref, sem = refs[-2:]
    row = lax.axis_index("row")
    first = (row == rows[0]) | (row == rows[1])

    @pl.when(first)
    def _():
        copy = pltpu.make_async_copy(one_ref, out_ref, sem)
        copy.start()
        copy.wait()

    @pl.when(jnp.logical_not(first))
    def _():
        copy = pltpu.make_async_copy(other_ref, out_ref, sem)
        copy.start()
        copy.wait()


def pick(rows, one, other, *others):
    return pl.pallas_call(
        functools.partial(pick_kernel, rows),
        out_shape=jax.ShapeDtypeStruct(one.shape, one.dtype),
        in_specs=anywhere(2 + len(others)),
        out_specs=anywhere()[0],
        scratch_shapes=[pltpu.SemaphoreType.DMA(())],
        compiler_params=pltpu.CompilerParams(vmem_limit_bytes=2**20),
    )(one, other, *others)


def split_kernel(n_col, n_row, vectors_ref, cols_ref, stay_ref, go_ref, turned):
    col, row = lax.axis_index("col"), lax.axis_index("row")
    count, share, rows = turned.shape
    orb = stay_ref.shape[2]
    per_piece = rows // orb
    whole = vectors_ref[...].T
    for d in range(count):
        turned[d] = whole[d * share : (d + 1) * share]
    orders = [(y, one, three) for y in range(2) for one in range(2) for three in range(2)]
    ids = cols_ref[...]
    piece = jnp.zeros_like(ids)
    for c in range(1, n_col):
        piece += (ids >= c * per_piece).astype(jnp.int32)
    ids = ids - piece * per_piece + (piece * n_row + row) * per_piece
    for core, out_ref in enumerate((stay_ref, go_ref)):
        for k, (y, one, three) in enumerate(orders):
            peer = (col ^ (core + 2 * y)) * n_row + (row ^ one ^ 3 * three)
            for b in range(per_piece):
                out_ref[k * per_piece + b] = turned[peer, :, b * orb : (b + 1) * orb]
        out_ref[len(orders) * per_piece] = ids.astype(jnp.float32).astype(out_ref.dtype)


def regroup_kernel(sources, count, stay_ref, came_ref, *outs):
    per_piece = (stay_ref.shape[0] - sources) // (sources * count)
    kept = max(count // 2, 1)
    for h, out_ref in enumerate(outs):
        for s in range(2 * sources):
            ref = stay_ref if s < sources else came_ref
            ids = ref[sources * count * per_piece + s % sources]
            if h == 1 and count == 1:
                out_ref[s : s + 1] = ids.astype(jnp.float32)[:1].astype(jnp.int32)
                continue
            for k in range(kept * per_piece):
                out_ref[s * kept * per_piece + k] = ref[(s % sources * count + h * kept) * per_piece + k]
            if count > 1:
                out_ref[2 * sources * kept * per_piece + s] = ids


def regroup(stay, came, sources, per_piece):
    count = (stay.shape[0] // sources - 1) // per_piece
    _, share, orb = stay.shape
    if count > 1:
        out = jax.ShapeDtypeStruct((sources * count * per_piece + 2 * sources, share, orb), stay.dtype)
        outs = [out, out]
    else:
        outs = [
            jax.ShapeDtypeStruct((2 * sources * per_piece, share, orb), stay.dtype),
            jax.ShapeDtypeStruct((2 * sources, orb), jnp.int32),
        ]
    return pl.pallas_call(
        functools.partial(regroup_kernel, sources, count),
        out_shape=outs,
        in_specs=vmem(2),
        out_specs=vmem(2),
        compiler_params=pltpu.CompilerParams(vmem_limit_bytes=2**20),
    )(stay, came)


def place(g, f):
    return (f >> 1) * 8 + ((f & 1) ^ (f >> 1)) * 4 + g


def multiply(t, groups, across, ids_ref, z, straight, scattered):
    tile_rows = z.shape[0] // len(groups)
    orb = z.shape[2]
    for g, group in enumerate(groups):
        if not group:
            continue
        here = across[g] * tile_rows + t
        places = [(tile, t * PER_ROW + p) for tile in group for p in range(PER_ROW)]
        strip = jnp.concatenate([s[i, slot] for (_, s, i, _, _), slot in places], axis=1)
        turned = jnp.concatenate([st[i, slot] for (_, _, _, st, i), slot in places], axis=0)
        where = [ids_ref[place(g, f), slot] for (f, *_), slot in places]
        wide = jnp.concatenate([z[u] for u in where], axis=1)
        straight[here] = jnp.dot(wide, turned, preferred_element_type=jnp.float32)
        mirrored = jnp.dot(z[here], strip, preferred_element_type=jnp.float32)
        for i, u in enumerate(where):
            scattered[i % len(scattered)][u] += mirrored[:, i * orb : (i + 1) * orb]


def clear(refs):
    for ref in refs:
        ref[...] = jnp.zeros_like(ref)


def turn(s_ref, st_ref, i, start, count):
    def four(k, carry):
        for m in range(4):
            st_ref[i, start + 4 * k + m] = s_ref[i, start + 4 * k + m].T
        return carry

    lax.fori_loop(0, count // 4, four, 0)


def load_kernel(count, *refs):
    bufs, (s_ref, st_ref, sems) = refs[:count], refs[count:]
    copies = [pltpu.make_async_copy(buf, s_ref.at[i], sems.at[i]) for i, buf in enumerate(bufs)]
    for copy in copies:
        copy.start()
    for i, copy in enumerate(copies):
        copy.wait()
        turn(s_ref, st_ref, i, 0, s_ref.shape[1])


def load(bufs):
    out = jax.ShapeDtypeStruct((len(bufs), *bufs[0].shape), bufs[0].dtype)
    size = len(bufs) * bufs[0].size
    return pl.pallas_call(
        functools.partial(load_kernel, len(bufs)),
        out_shape=[out, out],
        in_specs=anywhere(len(bufs)),
        out_specs=vmem(2),
        scratch_shapes=[pltpu.SemaphoreType.DMA((len(bufs),))],
        compiler_params=pltpu.CompilerParams(vmem_limit_bytes=2**20),
        cost_estimate=pl.CostEstimate(flops=0, bytes_accessed=6 * size, transcendentals=0),
    )(*bufs)


def filter_kernel(early, late, n_col, n_row, ids_ref, zt_ref, se_ref, ste_ref, *refs):
    bufs, (out_ref, s_ref, st_ref, z, now, prev, straight, *scattered, sems) = (
        refs[: len(late)],
        refs[len(late) :],
    )
    n_blocks, share, orb = z.shape
    slots = s_ref.shape[1]
    per_piece = n_blocks // (n_col * n_row)
    tile_rows = slots // PER_ROW
    across = [lax.axis_index("col") ^ g for g in range(n_col)]
    down = [lax.axis_index("row") ^ f for f in range(n_row)]
    rest = sorted({(g, f) for g, f, _ in late})

    copies = []
    for i, (buf, (g, f, start)) in enumerate(zip(bufs, late)):
        target = s_ref.at[rest.index((g, f)), pl.ds(start, buf.shape[0])]
        copies.append(pltpu.make_async_copy(buf, target, sems.at[i]))
        copies[-1].start()
    for g in range(n_col):
        for f in range(n_row):
            for b in range(per_piece):
                u = (across[g] * n_row + down[f]) * per_piece + b
                own = zt_ref[place(g, f), b]
                z[u] = own
                now[u] = own.astype(jnp.float32)
    clear([prev])
    for copy, buf, (g, f, start) in zip(copies, bufs, late):
        copy.wait()
        turn(s_ref, st_ref, rest.index((g, f)), start, buf.shape[0])

    tiles = {at: (se_ref, i, ste_ref, i) for i, at in enumerate(early)}
    tiles.update({at: (s_ref, i, st_ref, i) for i, at in enumerate(rest)})
    groups = [[(f, *tiles[g, f]) for f in range(n_row)] for g in range(n_col)]

    def one_step(step, carry):
        clear(scattered)

        def block_row(t, carry):
            multiply(t, groups, across, ids_ref, z, straight, scattered)
            return carry

        lax.fori_loop(0, tile_rows, block_row, 0)
        total = straight[...]
        for ref in scattered:
            total += ref[...]
        later = step > 0
        total = jnp.where(later, 2.0, 1.0) * total - jnp.where(later, 1.0, 0.0) * prev[...]
        prev[...] = now[...]
        now[...] = total
        z[...] = total.astype(z.dtype)
        return carry

    lax.fori_loop(0, DEG, one_step, 0)
    for p in range(n_col * n_row):
        for b in range(per_piece):
            u = p * per_piece + b
            out_ref[p, 0, :, b * orb : (b + 1) * orb] = now[u].astype(out_ref.dtype)
            out_ref[p, 1, :, b * orb : (b + 1) * orb] = prev[u].astype(out_ref.dtype)


def result_kernel(back_ref, last_ref, before_ref):
    count, _, share, rows = back_ref.shape
    for i, out_ref in enumerate((last_ref, before_ref)):
        whole = jnp.concatenate([back_ref[d, i] for d in range(count)], axis=0)
        out_ref[...] = whole.astype(jnp.float32).T


def gather_plan(vectors, blocks, cols):
    n_dev = lax.axis_size(LANES)
    n_col, n_row = lax.axis_size("col"), lax.axis_size("row")
    rows, width = vectors.shape
    slots, orb = blocks.shape[2:4]
    share = width // n_dev
    per_piece = rows // orb
    n_blocks = n_dev * per_piece
    half = slots // 2

    def send(buf, flip_col, flip_row, from_rows=range(n_row)):
        pairs = [
            (c * n_row + r, (c ^ flip_col) * n_row + (r ^ flip_row))
            for c in range(n_col)
            for r in from_rows
        ]
        return lax.ppermute(buf, LANES, pairs)

    def to_mate(*bufs):
        return [send(buf, 1, 0) for buf in bufs]

    own = blocks[0, 0]
    near = send(own, 0, 1)
    inner = send(own, 0, 3, INNER)
    over_own = send(own, 2, 0)

    own_cols = jnp.broadcast_to(jnp.pad(cols[0, 0], (0, orb - slots)), (share, orb))
    shares = jax.ShapeDtypeStruct((n_dev // 2 * per_piece + 1, share, orb), vectors.dtype)
    stay, go = pl.pallas_call(
        functools.partial(split_kernel, n_col, n_row),
        out_shape=[shares, shares],
        in_specs=vmem(2),
        out_specs=vmem(2),
        scratch_shapes=[pltpu.VMEM((n_dev, share, rows), vectors.dtype)],
        compiler_params=pltpu.CompilerParams(vmem_limit_bytes=4 * 2**20),
    )(vectors, own_cols)
    stay, go = regroup(stay, send(go, 1, 0), 1, per_piece)

    near = after(near, over_own)
    over_near = send(near, 2, 0)
    crossed = send(near, 0, 3, INNER)
    outward = send(inner, 0, 1, INNER)
    stay, go = regroup(stay, send(go, 2, 0), 2, per_piece)
    stay, go = regroup(stay, send(go, 0, 1), 4, per_piece)
    mates = to_mate(own, near, over_own)
    two = pick(INNER, crossed, outward, over_near, go, *mates)

    over_two = send(two, 2, 0)
    outer = send(crossed, 0, 1, INNER)
    mates += to_mate(two, over_near)
    mine, ids = regroup(stay, send(go, 0, 3), 8, per_piece)
    three = pick(INNER, inner, outer, over_two, mine, *mates[3:])

    over_three = send(three[:half], 2, 0)
    side_three = send(over_two[half:], 0, 1)
    mates += to_mate(three, over_two)
    se, ste = load([own, near, over_own, two, over_near, three, over_two, *mates])
    over_three, side_three = after(over_three, se), after(side_three, se)

    early = [(0, 0), (0, 1), (2, 0), (0, 2), (2, 1), (0, 3), (2, 2)]
    early += [(g ^ 1, f) for g, f in early]
    late = [(2, 3, 0), (2, 3, half), (3, 3, 0), (3, 3, half)]
    late_bufs = [over_three, side_three, *to_mate(over_three, side_three)]

    done = pl.pallas_call(
        functools.partial(filter_kernel, early, late, n_col, n_row),
        out_shape=jax.ShapeDtypeStruct((n_dev, 2, share, rows), jnp.bfloat16),
        in_specs=smem() + vmem(3) + anywhere(len(late)),
        out_specs=vmem()[0],
        scratch_shapes=[
            *[pltpu.VMEM((n_dev - len(early), slots, orb, orb), blocks.dtype)] * 2,
            pltpu.VMEM((n_blocks, share, orb), jnp.bfloat16),
            *[pltpu.VMEM((n_blocks, share, orb), jnp.float32)] * (3 + SPLIT),
            pltpu.SemaphoreType.DMA((len(late),)),
        ],
        compiler_params=pltpu.CompilerParams(vmem_limit_bytes=12 * 2**20),
    )(
        ids,
        mine.reshape(n_dev, per_piece, share, orb),
        se,
        ste,
        *late_bufs,
    )
    back = lax.all_to_all(done, LANES, split_axis=0, concat_axis=0, tiled=True)
    whole = jax.ShapeDtypeStruct((rows, width), jnp.float32)
    return pl.pallas_call(
        result_kernel,
        out_shape=[whole, whole],
        in_specs=vmem(),
        out_specs=vmem(2),
        compiler_params=pltpu.CompilerParams(vmem_limit_bytes=4 * 2**20),
    )(back)


def per_device(vectors, blocks, cols):
    n_dev = lax.axis_size(LANES)
    line_of_four = lax.axis_size("col") == 4 and lax.axis_size("row") == 4
    if line_of_four and n_dev * blocks.size * blocks.dtype.itemsize <= GATHER_LIMIT:
        return gather_plan(vectors, blocks, cols)
    return spread_plan(vectors, blocks, cols)


def solution(mesh):
    return jax.shard_map(
        per_device,
        mesh=mesh,
        in_specs=(
            P(("col", "row"), "dom"),
            P(("dom", "col"), "row", None, None, None),
            P(("dom", "col"), "row", None),
        ),
        out_specs=(P(("col", "row"), "dom"), P(("col", "row"), "dom")),
        check_vma=False,
    )
```

```python
import functools

import jax
import jax.numpy as jnp
from jax import lax
from jax.experimental import pallas as pl
from jax.experimental.pallas import tpu as pltpu
from jax.sharding import PartitionSpec as P

PER_ROW = 2
DEG = 4
SPLIT = 4
GATHER_LIMIT = 12 * 2**20
LANES = ("col", "row")
INNER = (1, 2)


def onehot_sum(selected, high_part, low_part):
    first = jnp.einsum("su,sok->uok", selected, high_part, preferred_element_type=jnp.float32)
    second = jnp.einsum("su,sok->uok", selected, low_part, preferred_element_type=jnp.float32)
    return first + second


def apply_pair(send, grouped, col_ids, onehot):
    tile_rows, per_row, orb, _ = grouped.shape
    piece_rows, width = send.shape
    tile_cols = onehot.shape[1]
    wide = lax.all_gather(send, "col", axis=0, tiled=True).reshape(tile_cols, orb, width)
    picked = jnp.take(wide, col_ids, axis=0).reshape(tile_rows, per_row, orb, width)
    direct = jnp.einsum("tpio,tpok->tik", grouped, picked, preferred_element_type=jnp.float32)
    part_rows = lax.psum_scatter(
        direct.reshape(tile_rows * orb, width).astype(jnp.bfloat16),
        "row",
        scatter_dimension=0,
        tiled=True,
    ).astype(jnp.float32)
    tall = lax.all_gather(send, "row", axis=0, tiled=True).reshape(tile_rows, orb, width)
    mirrored = jnp.einsum("tpio,tik->tpok", grouped, tall, preferred_element_type=jnp.float32)
    mirrored = mirrored.reshape(tile_rows * per_row, orb, width)
    high_part = mirrored.astype(jnp.bfloat16)
    low_part = (mirrored - high_part.astype(jnp.float32)).astype(jnp.bfloat16)
    summed = onehot_sum(onehot, high_part, low_part)
    part_cols = lax.psum_scatter(
        summed.reshape(tile_cols * orb, width).astype(jnp.bfloat16),
        "col",
        scatter_dimension=0,
        tiled=True,
    ).astype(jnp.float32)
    return part_rows + part_cols


def spread_plan(vectors, blocks, cols):
    tiles = blocks[0, 0]
    col_ids = cols[0, 0]
    slots, orb, _ = tiles.shape
    tile_rows = slots // PER_ROW
    tile_cols = lax.axis_size("col") * (vectors.shape[0] // orb)
    grouped = tiles.reshape(tile_rows, PER_ROW, orb, orb)
    onehot = (col_ids[:, None] == jnp.arange(tile_cols, dtype=jnp.int32)[None, :]).astype(
        jnp.bfloat16
    )
    prev = vectors.astype(jnp.float32)
    now = apply_pair(vectors, grouped, col_ids, onehot)
    for step in range(DEG - 1):
        nxt = 2.0 * apply_pair(now.astype(jnp.bfloat16), grouped, col_ids, onehot) - prev
        prev, now = (now, nxt)
    return (now, prev)


def vmem(count=1):
    return [pl.BlockSpec(memory_space=pltpu.VMEM)] * count


def smem(count=1):
    return [pl.BlockSpec(memory_space=pltpu.SMEM)] * count


def anywhere(count=1):
    return [pl.BlockSpec(memory_space=pl.ANY)] * count


def nothing(*refs):
    pass


def after(value, *others, rank=0):
    return pl.pallas_call(
        nothing,
        out_shape=jax.ShapeDtypeStruct(value.shape, value.dtype),
        in_specs=anywhere(1 + len(others)),
        out_specs=anywhere()[0],
        input_output_aliases={0: 0},
        compiler_params=pltpu.CompilerParams(vmem_limit_bytes=2**20),
        cost_estimate=pl.CostEstimate(flops=0, bytes_accessed=rank * 2**23, transcendentals=0),
    )(value, *others)


def pick_kernel(rows, one_ref, other_ref, *refs):
    out_ref, sem = refs[-2:]
    row = lax.axis_index("row")
    first = (row == rows[0]) | (row == rows[1])

    @pl.when(first)
    def _():
        copy = pltpu.make_async_copy(one_ref, out_ref, sem)
        copy.start()
        copy.wait()

    @pl.when(jnp.logical_not(first))
    def _():
        copy = pltpu.make_async_copy(other_ref, out_ref, sem)
        copy.start()
        copy.wait()


def pick(rows, one, other, *others):
    return pl.pallas_call(
        functools.partial(pick_kernel, rows),
        out_shape=jax.ShapeDtypeStruct(one.shape, one.dtype),
        in_specs=anywhere(2 + len(others)),
        out_specs=anywhere()[0],
        scratch_shapes=[pltpu.SemaphoreType.DMA(())],
        compiler_params=pltpu.CompilerParams(vmem_limit_bytes=2**20),
    )(one, other, *others)


def split_kernel(n_col, n_row, vectors_ref, cols_ref, stay_ref, go_ref, turned):
    col, row = lax.axis_index("col"), lax.axis_index("row")
    count, share, rows = turned.shape
    orb = stay_ref.shape[2]
    per_piece = rows // orb
    whole = vectors_ref[...].T
    for d in range(count):
        turned[d] = whole[d * share : (d + 1) * share]
    orders = [(y, one, three) for y in range(2) for one in range(2) for three in range(2)]
    ids = cols_ref[...]
    piece = jnp.zeros_like(ids)
    for c in range(1, n_col):
        piece += (ids >= c * per_piece).astype(jnp.int32)
    ids = ids - piece * per_piece + (piece * n_row + row) * per_piece
    for core, out_ref in enumerate((stay_ref, go_ref)):
        for k, (y, one, three) in enumerate(orders):
            peer = (col ^ (core + 2 * y)) * n_row + (row ^ one ^ 3 * three)
            for b in range(per_piece):
                out_ref[k * per_piece + b] = turned[peer, :, b * orb : (b + 1) * orb]
        out_ref[len(orders) * per_piece] = ids.astype(jnp.float32).astype(out_ref.dtype)


def regroup_kernel(sources, count, stay_ref, came_ref, *outs):
    per_piece = (stay_ref.shape[0] - sources) // (sources * count)
    kept = max(count // 2, 1)
    for h, out_ref in enumerate(outs):
        for s in range(2 * sources):
            ref = stay_ref if s < sources else came_ref
            ids = ref[sources * count * per_piece + s % sources]
            if h == 1 and count == 1:
                out_ref[s : s + 1] = ids.astype(jnp.float32)[:1].astype(jnp.int32)
                continue
            for k in range(kept * per_piece):
                out_ref[s * kept * per_piece + k] = ref[(s % sources * count + h * kept) * per_piece + k]
            if count > 1:
                out_ref[2 * sources * kept * per_piece + s] = ids


def regroup(stay, came, sources, per_piece):
    count = (stay.shape[0] // sources - 1) // per_piece
    _, share, orb = stay.shape
    if count > 1:
        out = jax.ShapeDtypeStruct((sources * count * per_piece + 2 * sources, share, orb), stay.dtype)
        outs = [out, out]
    else:
        outs = [
            jax.ShapeDtypeStruct((2 * sources * per_piece, share, orb), stay.dtype),
            jax.ShapeDtypeStruct((2 * sources, orb), jnp.int32),
        ]
    return pl.pallas_call(
        functools.partial(regroup_kernel, sources, count),
        out_shape=outs,
        in_specs=vmem(2),
        out_specs=vmem(2),
        compiler_params=pltpu.CompilerParams(vmem_limit_bytes=2**20),
    )(stay, came)


def place(g, f):
    return (f >> 1) * 8 + ((f & 1) ^ (f >> 1)) * 4 + g


def multiply(t, groups, across, ids_ref, z, straight, scattered):
    tile_rows = z.shape[0] // len(groups)
    orb = z.shape[2]
    for g, group in enumerate(groups):
        if not group:
            continue
        here = across[g] * tile_rows + t
        places = [(tile, t * PER_ROW + p) for tile in group for p in range(PER_ROW)]
        strip = jnp.concatenate([s[i, slot] for (_, s, i, _, _), slot in places], axis=1)
        turned = jnp.concatenate([st[i, slot] for (_, _, _, st, i), slot in places], axis=0)
        where = [ids_ref[place(g, f), slot] for (f, *_), slot in places]
        wide = jnp.concatenate([z[u] for u in where], axis=1)
        straight[here] = jnp.dot(wide, turned, preferred_element_type=jnp.float32)
        mirrored = jnp.dot(z[here], strip, preferred_element_type=jnp.float32)
        for i, u in enumerate(where):
            scattered[i % len(scattered)][u] += mirrored[:, i * orb : (i + 1) * orb]


def clear(refs):
    for ref in refs:
        ref[...] = jnp.zeros_like(ref)


def turn(s_ref, st_ref, i, start, count):
    def four(k, carry):
        for m in range(4):
            st_ref[i, start + 4 * k + m] = s_ref[i, start + 4 * k + m].T
        return carry

    lax.fori_loop(0, count // 4, four, 0)


def fill(bufs, s_ref, st_ref, sems):
    copies = [pltpu.make_async_copy(buf, s_ref.at[i], sems.at[i]) for i, buf in enumerate(bufs)]
    for copy in copies:
        copy.start()
    for i, copy in enumerate(copies):
        copy.wait()
        turn(s_ref, st_ref, i, 0, s_ref.shape[1])


def grouped(tiles, n_col, n_row):
    return [[(f, *tiles[g, f]) for f in range(n_row) if (g, f) in tiles] for g in range(n_col)]


def spread_vectors(parts_ref, z, n_col, n_row, now=None):
    per_piece = z.shape[0] // (n_col * n_row)
    across = [lax.axis_index("col") ^ g for g in range(n_col)]
    down = [lax.axis_index("row") ^ f for f in range(n_row)]
    for g in range(n_col):
        for f in range(n_row):
            for b in range(per_piece):
                u = (across[g] * n_row + down[f]) * per_piece + b
                own = parts_ref[place(g, f) * per_piece + b]
                z[u] = own
                if now is not None:
                    now[u] = own.astype(jnp.float32)


def sum_products(groups, n_col, ids_ref, z, straight, scattered):
    across = [lax.axis_index("col") ^ g for g in range(n_col)]
    clear(scattered)

    def block_row(t, carry):
        multiply(t, groups, across, ids_ref, z, straight, scattered)
        return carry

    lax.fori_loop(0, z.shape[0] // n_col, block_row, 0)
    total = straight[...]
    for ref in scattered:
        total += ref[...]
    return total


def first_kernel(early, n_col, n_row, ids_ref, parts_ref, *refs):
    bufs, (s_ref, st_ref, sum_ref, z, straight, *scattered, sems) = refs[: len(early)], refs[len(early) :]
    spread_vectors(parts_ref, z, n_col, n_row)
    fill(bufs, s_ref, st_ref, sems)
    tiles = {at: (s_ref, i, st_ref, i) for i, at in enumerate(early)}
    clear([straight])
    sum_ref[...] = sum_products(grouped(tiles, n_col, n_row), n_col, ids_ref, z, straight, scattered)


def filter_kernel(early, late, n_col, n_row, ids_ref, parts_ref, sum_ref, se_ref, ste_ref, *refs):
    bufs, (out_ref, s_ref, st_ref, z, now, prev, straight, *scattered, sems) = (
        refs[: len(late)],
        refs[len(late) :],
    )
    n_blocks, share, orb = z.shape
    per_piece = n_blocks // (n_col * n_row)
    rest = sorted({(g, f) for g, f, _ in late})

    copies = []
    for i, (buf, (g, f, start)) in enumerate(zip(bufs, late)):
        target = s_ref.at[rest.index((g, f)), pl.ds(start, buf.shape[0])]
        copies.append(pltpu.make_async_copy(buf, target, sems.at[i]))
        copies[-1].start()
    spread_vectors(parts_ref, z, n_col, n_row, prev)
    for copy, buf, (g, f, start) in zip(copies, bufs, late):
        copy.wait()
        turn(s_ref, st_ref, rest.index((g, f)), start, buf.shape[0])

    tiles = {at: (s_ref, i, st_ref, i) for i, at in enumerate(rest)}
    clear([straight])
    total = sum_products(grouped(tiles, n_col, n_row), n_col, ids_ref, z, straight, scattered)
    total += sum_ref[...]
    now[...] = total
    z[...] = total.astype(z.dtype)

    tiles.update({at: (se_ref, i, ste_ref, i) for i, at in enumerate(early)})
    groups = grouped(tiles, n_col, n_row)

    def one_step(step, carry):
        total = sum_products(groups, n_col, ids_ref, z, straight, scattered)
        total = 2.0 * total - prev[...]
        prev[...] = now[...]
        now[...] = total
        z[...] = total.astype(z.dtype)
        return carry

    lax.fori_loop(1, DEG, one_step, 0)
    for p in range(n_col * n_row):
        for b in range(per_piece):
            u = p * per_piece + b
            out_ref[p, 0, :, b * orb : (b + 1) * orb] = now[u].astype(out_ref.dtype)
            out_ref[p, 1, :, b * orb : (b + 1) * orb] = prev[u].astype(out_ref.dtype)


def result_kernel(back_ref, last_ref, before_ref):
    count, _, share, rows = back_ref.shape
    for i, out_ref in enumerate((last_ref, before_ref)):
        whole = jnp.concatenate([back_ref[d, i] for d in range(count)], axis=0)
        out_ref[...] = whole.astype(jnp.float32).T


def gather_plan(vectors, blocks, cols):
    n_dev = lax.axis_size(LANES)
    n_col, n_row = lax.axis_size("col"), lax.axis_size("row")
    rows, width = vectors.shape
    slots, orb = blocks.shape[2:4]
    share = width // n_dev
    per_piece = rows // orb
    n_blocks = n_dev * per_piece
    half = slots // 2

    def send(buf, flip_col, flip_row, from_rows=range(n_row)):
        pairs = [
            (c * n_row + r, (c ^ flip_col) * n_row + (r ^ flip_row))
            for c in range(n_col)
            for r in from_rows
        ]
        return lax.ppermute(buf, LANES, pairs)

    def to_mate(*bufs):
        return [send(buf, 1, 0) for buf in bufs]

    own = blocks[0, 0]
    near = send(own, 0, 1)
    inner = send(own, 0, 3, INNER)
    over_own = send(own, 2, 0)

    own_cols = jnp.broadcast_to(jnp.pad(cols[0, 0], (0, orb - slots)), (share, orb))
    shares = jax.ShapeDtypeStruct((n_dev // 2 * per_piece + 1, share, orb), vectors.dtype)
    stay, go = pl.pallas_call(
        functools.partial(split_kernel, n_col, n_row),
        out_shape=[shares, shares],
        in_specs=vmem(2),
        out_specs=vmem(2),
        scratch_shapes=[pltpu.VMEM((n_dev, share, rows), vectors.dtype)],
        compiler_params=pltpu.CompilerParams(vmem_limit_bytes=4 * 2**20),
    )(vectors, own_cols)
    stay, go = regroup(stay, send(go, 1, 0), 1, per_piece)

    stay, go = regroup(stay, send(go, 2, 0), 2, per_piece)
    mates = to_mate(own)
    near = after(near, over_own, go, *mates)
    over_near = after(send(near, 2, 0), rank=3)
    crossed = after(send(near, 0, 3, INNER), rank=1)
    inner = after(inner, near)
    outward = after(send(inner, 0, 1, INNER), rank=1)
    stay, go = regroup(stay, send(go, 0, 1), 4, per_piece)
    mates += to_mate(near, over_own)
    two = pick(INNER, crossed, outward, over_near, go, *mates)

    over_two = send(two, 2, 0)
    outer = after(send(crossed, 0, 1, INNER), rank=1)
    mates += to_mate(two, over_near)
    mine, ids = regroup(stay, send(go, 0, 3), 8, per_piece)
    three = pick(INNER, inner, outer, over_two, mine, *mates[3:])

    over_three = send(three[:half], 2, 0)
    side_three = send(over_two[half:], 0, 1)
    mates += to_mate(three, over_two)
    early = [(0, 0), (0, 1), (2, 0), (0, 2), (2, 1), (0, 3), (2, 2)]
    early += [(g ^ 1, f) for g, f in early]
    tiles_of = jax.ShapeDtypeStruct((len(early), slots, orb, orb), blocks.dtype)
    sums = jax.ShapeDtypeStruct((n_blocks, share, orb), jnp.float32)
    se, ste, total = pl.pallas_call(
        functools.partial(first_kernel, early, n_col, n_row),
        out_shape=[tiles_of, tiles_of, sums],
        in_specs=smem() + vmem() + anywhere(len(early)),
        out_specs=vmem(3),
        scratch_shapes=[
            pltpu.VMEM((n_blocks, share, orb), jnp.bfloat16),
            *[pltpu.VMEM((n_blocks, share, orb), jnp.float32)] * (1 + SPLIT),
            pltpu.SemaphoreType.DMA((len(early),)),
        ],
        compiler_params=pltpu.CompilerParams(vmem_limit_bytes=6 * 2**20),
        cost_estimate=pl.CostEstimate(
            flops=4 * len(early) * slots * orb * orb * share,
            bytes_accessed=6 * len(early) * own.size,
            transcendentals=0,
        ),
    )(ids, mine, own, near, over_own, two, over_near, three, over_two, *mates)
    over_three, side_three = after(over_three, se), after(side_three, se)
    late = [(2, 3, 0), (2, 3, half), (3, 3, 0), (3, 3, half)]
    late_bufs = [over_three, side_three, *to_mate(over_three, side_three)]

    done = pl.pallas_call(
        functools.partial(filter_kernel, early, late, n_col, n_row),
        out_shape=jax.ShapeDtypeStruct((n_dev, 2, share, rows), jnp.bfloat16),
        in_specs=smem() + vmem(4) + anywhere(len(late)),
        out_specs=vmem()[0],
        scratch_shapes=[
            *[pltpu.VMEM((2, slots, orb, orb), blocks.dtype)] * 2,
            pltpu.VMEM((n_blocks, share, orb), jnp.bfloat16),
            *[pltpu.VMEM((n_blocks, share, orb), jnp.float32)] * (3 + SPLIT),
            pltpu.SemaphoreType.DMA((len(late),)),
        ],
        compiler_params=pltpu.CompilerParams(vmem_limit_bytes=12 * 2**20),
    )(ids, mine, total, se, ste, *late_bufs)
    back = lax.all_to_all(done, LANES, split_axis=0, concat_axis=0, tiled=True)
    whole = jax.ShapeDtypeStruct((rows, width), jnp.float32)
    return pl.pallas_call(
        result_kernel,
        out_shape=[whole, whole],
        in_specs=vmem(),
        out_specs=vmem(2),
        compiler_params=pltpu.CompilerParams(vmem_limit_bytes=4 * 2**20),
    )(back)


def per_device(vectors, blocks, cols):
    n_dev = lax.axis_size(LANES)
    line_of_four = lax.axis_size("col") == 4 and lax.axis_size("row") == 4
    if line_of_four and n_dev * blocks.size * blocks.dtype.itemsize <= GATHER_LIMIT:
        return gather_plan(vectors, blocks, cols)
    return spread_plan(vectors, blocks, cols)


def solution(mesh):
    return jax.shard_map(
        per_device,
        mesh=mesh,
        in_specs=(
            P(("col", "row"), "dom"),
            P(("dom", "col"), "row", None, None, None),
            P(("dom", "col"), "row", None),
        ),
        out_specs=(P(("col", "row"), "dom"), P(("col", "row"), "dom")),
        check_vma=False,
    )
```

```python
import functools

import jax
import jax.numpy as jnp
from jax import lax
from jax.experimental import pallas as pl
from jax.experimental.pallas import tpu as pltpu
from jax.sharding import PartitionSpec as P

PER_ROW = 2
DEG = 4
SPLIT = 4
GATHER_LIMIT = 12 * 2**20
LANES = ("col", "row")
INNER = (1, 2)


def onehot_sum(selected, high_part, low_part):
    first = jnp.einsum("su,sok->uok", selected, high_part, preferred_element_type=jnp.float32)
    second = jnp.einsum("su,sok->uok", selected, low_part, preferred_element_type=jnp.float32)
    return first + second


def apply_pair(send, grouped, col_ids, onehot):
    tile_rows, per_row, orb, _ = grouped.shape
    piece_rows, width = send.shape
    tile_cols = onehot.shape[1]
    wide = lax.all_gather(send, "col", axis=0, tiled=True).reshape(tile_cols, orb, width)
    picked = jnp.take(wide, col_ids, axis=0).reshape(tile_rows, per_row, orb, width)
    direct = jnp.einsum("tpio,tpok->tik", grouped, picked, preferred_element_type=jnp.float32)
    part_rows = lax.psum_scatter(
        direct.reshape(tile_rows * orb, width).astype(jnp.bfloat16),
        "row",
        scatter_dimension=0,
        tiled=True,
    ).astype(jnp.float32)
    tall = lax.all_gather(send, "row", axis=0, tiled=True).reshape(tile_rows, orb, width)
    mirrored = jnp.einsum("tpio,tik->tpok", grouped, tall, preferred_element_type=jnp.float32)
    mirrored = mirrored.reshape(tile_rows * per_row, orb, width)
    high_part = mirrored.astype(jnp.bfloat16)
    low_part = (mirrored - high_part.astype(jnp.float32)).astype(jnp.bfloat16)
    summed = onehot_sum(onehot, high_part, low_part)
    part_cols = lax.psum_scatter(
        summed.reshape(tile_cols * orb, width).astype(jnp.bfloat16),
        "col",
        scatter_dimension=0,
        tiled=True,
    ).astype(jnp.float32)
    return part_rows + part_cols


def spread_plan(vectors, blocks, cols):
    tiles = blocks[0, 0]
    col_ids = cols[0, 0]
    slots, orb, _ = tiles.shape
    tile_rows = slots // PER_ROW
    tile_cols = lax.axis_size("col") * (vectors.shape[0] // orb)
    grouped = tiles.reshape(tile_rows, PER_ROW, orb, orb)
    onehot = (col_ids[:, None] == jnp.arange(tile_cols, dtype=jnp.int32)[None, :]).astype(
        jnp.bfloat16
    )
    prev = vectors.astype(jnp.float32)
    now = apply_pair(vectors, grouped, col_ids, onehot)
    for step in range(DEG - 1):
        nxt = 2.0 * apply_pair(now.astype(jnp.bfloat16), grouped, col_ids, onehot) - prev
        prev, now = (now, nxt)
    return (now, prev)


def vmem(count=1):
    return [pl.BlockSpec(memory_space=pltpu.VMEM)] * count


def smem(count=1):
    return [pl.BlockSpec(memory_space=pltpu.SMEM)] * count


def anywhere(count=1):
    return [pl.BlockSpec(memory_space=pl.ANY)] * count


def nothing(*refs):
    pass


def after(value, *others, rank=0):
    return pl.pallas_call(
        nothing,
        out_shape=jax.ShapeDtypeStruct(value.shape, value.dtype),
        in_specs=anywhere(1 + len(others)),
        out_specs=anywhere()[0],
        input_output_aliases={0: 0},
        compiler_params=pltpu.CompilerParams(vmem_limit_bytes=2**20),
        cost_estimate=pl.CostEstimate(flops=0, bytes_accessed=rank * 2**23, transcendentals=0),
    )(value, *others)


def pick_kernel(rows, one_ref, other_ref, *refs):
    out_ref, sem = refs[-2:]
    row = lax.axis_index("row")
    first = (row == rows[0]) | (row == rows[1])

    @pl.when(first)
    def _():
        copy = pltpu.make_async_copy(one_ref, out_ref, sem)
        copy.start()
        copy.wait()

    @pl.when(jnp.logical_not(first))
    def _():
        copy = pltpu.make_async_copy(other_ref, out_ref, sem)
        copy.start()
        copy.wait()


def pick(rows, one, other, *others):
    return pl.pallas_call(
        functools.partial(pick_kernel, rows),
        out_shape=jax.ShapeDtypeStruct(one.shape, one.dtype),
        in_specs=anywhere(2 + len(others)),
        out_specs=anywhere()[0],
        scratch_shapes=[pltpu.SemaphoreType.DMA(())],
        compiler_params=pltpu.CompilerParams(vmem_limit_bytes=2**20),
    )(one, other, *others)


def split_kernel(n_col, n_row, vectors_ref, cols_ref, stay_ref, go_ref, turned):
    col, row = lax.axis_index("col"), lax.axis_index("row")
    count, share, rows = turned.shape
    orb = stay_ref.shape[2]
    per_piece = rows // orb
    whole = vectors_ref[...].T
    for d in range(count):
        turned[d] = whole[d * share : (d + 1) * share]
    orders = [(y, one, three) for y in range(2) for one in range(2) for three in range(2)]
    ids = cols_ref[...]
    piece = jnp.zeros_like(ids)
    for c in range(1, n_col):
        piece += (ids >= c * per_piece).astype(jnp.int32)
    ids = ids - piece * per_piece + (piece * n_row + row) * per_piece
    for core, out_ref in enumerate((stay_ref, go_ref)):
        for k, (y, one, three) in enumerate(orders):
            peer = (col ^ (core + 2 * y)) * n_row + (row ^ one ^ 3 * three)
            for b in range(per_piece):
                out_ref[k * per_piece + b] = turned[peer, :, b * orb : (b + 1) * orb]
        out_ref[len(orders) * per_piece] = ids.astype(jnp.float32).astype(out_ref.dtype)


def regroup_kernel(sources, count, stay_ref, came_ref, *outs):
    per_piece = (stay_ref.shape[0] - sources) // (sources * count)
    kept = max(count // 2, 1)
    for h, out_ref in enumerate(outs):
        for s in range(2 * sources):
            ref = stay_ref if s < sources else came_ref
            ids = ref[sources * count * per_piece + s % sources]
            if h == 1 and count == 1:
                out_ref[s : s + 1] = ids.astype(jnp.float32)[:1].astype(jnp.int32)
                continue
            for k in range(kept * per_piece):
                out_ref[s * kept * per_piece + k] = ref[(s % sources * count + h * kept) * per_piece + k]
            if count > 1:
                out_ref[2 * sources * kept * per_piece + s] = ids


def regroup(stay, came, sources, per_piece):
    count = (stay.shape[0] // sources - 1) // per_piece
    _, share, orb = stay.shape
    if count > 1:
        out = jax.ShapeDtypeStruct((sources * count * per_piece + 2 * sources, share, orb), stay.dtype)
        outs = [out, out]
    else:
        outs = [
            jax.ShapeDtypeStruct((2 * sources * per_piece, share, orb), stay.dtype),
            jax.ShapeDtypeStruct((2 * sources, orb), jnp.int32),
        ]
    return pl.pallas_call(
        functools.partial(regroup_kernel, sources, count),
        out_shape=outs,
        in_specs=vmem(2),
        out_specs=vmem(2),
        compiler_params=pltpu.CompilerParams(vmem_limit_bytes=2**20),
    )(stay, came)


def place(g, f):
    return (f >> 1) * 8 + ((f & 1) ^ (f >> 1)) * 4 + g


def multiply(t, groups, across, ids_ref, z, straight, scattered):
    tile_rows = z.shape[0] // len(groups)
    orb = z.shape[2]
    for g, group in enumerate(groups):
        if not group:
            continue
        here = across[g] * tile_rows + t
        places = [(tile, t * PER_ROW + p) for tile in group for p in range(PER_ROW)]
        strip = jnp.concatenate([s[i, slot] for (_, s, i, _, _), slot in places], axis=1)
        turned = jnp.concatenate([st[i, slot] for (_, _, _, st, i), slot in places], axis=0)
        where = [ids_ref[place(g, f), slot] for (f, *_), slot in places]
        wide = jnp.concatenate([z[u] for u in where], axis=1)
        straight[here] = jnp.dot(wide, turned, preferred_element_type=jnp.float32)
        mirrored = jnp.dot(z[here], strip, preferred_element_type=jnp.float32)
        for i, u in enumerate(where):
            scattered[i % len(scattered)][u] += mirrored[:, i * orb : (i + 1) * orb]


def clear(refs):
    for ref in refs:
        ref[...] = jnp.zeros_like(ref)


def turn(s_ref, st_ref, i, start, count):
    def four(k, carry):
        for m in range(4):
            st_ref[i, start + 4 * k + m] = s_ref[i, start + 4 * k + m].T
        return carry

    lax.fori_loop(0, count // 4, four, 0)


def fill(bufs, s_ref, st_ref, sems):
    copies = [pltpu.make_async_copy(buf, s_ref.at[i], sems.at[i]) for i, buf in enumerate(bufs)]
    for copy in copies:
        copy.start()
    for i, copy in enumerate(copies):
        copy.wait()
        turn(s_ref, st_ref, i, 0, s_ref.shape[1])


def grouped(tiles, n_col, n_row):
    return [[(f, *tiles[g, f]) for f in range(n_row) if (g, f) in tiles] for g in range(n_col)]


def spread_vectors(parts_ref, z, n_col, n_row, now=None):
    per_piece = z.shape[0] // (n_col * n_row)
    across = [lax.axis_index("col") ^ g for g in range(n_col)]
    down = [lax.axis_index("row") ^ f for f in range(n_row)]
    for g in range(n_col):
        for f in range(n_row):
            for b in range(per_piece):
                u = (across[g] * n_row + down[f]) * per_piece + b
                own = parts_ref[place(g, f) * per_piece + b]
                z[u] = own
                if now is not None:
                    now[u] = own.astype(jnp.float32)


def sum_products(groups, n_col, ids_ref, z, straight, scattered):
    across = [lax.axis_index("col") ^ g for g in range(n_col)]
    clear(scattered)

    def block_row(t, carry):
        multiply(t, groups, across, ids_ref, z, straight, scattered)
        return carry

    lax.fori_loop(0, z.shape[0] // n_col, block_row, 0)
    total = straight[...]
    for ref in scattered:
        total += ref[...]
    return total


def load_kernel(count, *refs):
    bufs, (s_ref, st_ref, sems) = refs[:count], refs[count:]
    fill(bufs, s_ref, st_ref, sems)


def load(*bufs):
    out = jax.ShapeDtypeStruct((len(bufs), *bufs[0].shape), bufs[0].dtype)
    return pl.pallas_call(
        functools.partial(load_kernel, len(bufs)),
        out_shape=[out, out],
        in_specs=anywhere(len(bufs)),
        out_specs=vmem(2),
        scratch_shapes=[pltpu.SemaphoreType.DMA((len(bufs),))],
        compiler_params=pltpu.CompilerParams(vmem_limit_bytes=2**20),
        cost_estimate=pl.CostEstimate(flops=0, bytes_accessed=6 * out.size, transcendentals=0),
    )(*bufs)


def first_kernel(early, later, n_col, n_row, ids_ref, parts_ref, sa_ref, sta_ref, *refs):
    bufs, (s_ref, st_ref, sum_ref, z, straight, *scattered, sems) = refs[: len(later)], refs[len(later) :]
    spread_vectors(parts_ref, z, n_col, n_row)
    fill(bufs, s_ref, st_ref, sems)
    tiles = {at: (sa_ref, i, sta_ref, i) for i, at in enumerate(early)}
    tiles.update({at: (s_ref, i, st_ref, i) for i, at in enumerate(later)})
    clear([straight])
    sum_ref[...] = sum_products(grouped(tiles, n_col, n_row), n_col, ids_ref, z, straight, scattered)


def filter_kernel(early, later, late, n_col, n_row, ids_ref, parts_ref, sum_ref, *refs):
    (sa_ref, sta_ref, sb_ref, stb_ref), refs = refs[:4], refs[4:]
    bufs, (out_ref, s_ref, st_ref, z, now, prev, straight, *scattered, sems) = (
        refs[: len(late)],
        refs[len(late) :],
    )
    n_blocks, share, orb = z.shape
    per_piece = n_blocks // (n_col * n_row)
    rest = sorted({(g, f) for g, f, _ in late})

    copies = []
    for i, (buf, (g, f, start)) in enumerate(zip(bufs, late)):
        target = s_ref.at[rest.index((g, f)), pl.ds(start, buf.shape[0])]
        copies.append(pltpu.make_async_copy(buf, target, sems.at[i]))
        copies[-1].start()
    spread_vectors(parts_ref, z, n_col, n_row, prev)
    for copy, buf, (g, f, start) in zip(copies, bufs, late):
        copy.wait()
        turn(s_ref, st_ref, rest.index((g, f)), start, buf.shape[0])

    tiles = {at: (s_ref, i, st_ref, i) for i, at in enumerate(rest)}
    clear([straight])
    total = sum_products(grouped(tiles, n_col, n_row), n_col, ids_ref, z, straight, scattered)
    total += sum_ref[...]
    now[...] = total
    z[...] = total.astype(z.dtype)

    tiles.update({at: (sa_ref, i, sta_ref, i) for i, at in enumerate(early)})
    tiles.update({at: (sb_ref, i, stb_ref, i) for i, at in enumerate(later)})
    groups = grouped(tiles, n_col, n_row)

    def one_step(step, carry):
        total = sum_products(groups, n_col, ids_ref, z, straight, scattered)
        total = 2.0 * total - prev[...]
        prev[...] = now[...]
        now[...] = total
        z[...] = total.astype(z.dtype)
        return carry

    lax.fori_loop(1, DEG, one_step, 0)
    for p in range(n_col * n_row):
        for b in range(per_piece):
            u = p * per_piece + b
            out_ref[p, 0, :, b * orb : (b + 1) * orb] = now[u].astype(out_ref.dtype)
            out_ref[p, 1, :, b * orb : (b + 1) * orb] = prev[u].astype(out_ref.dtype)


def result_kernel(back_ref, last_ref, before_ref):
    count, _, share, rows = back_ref.shape
    for i, out_ref in enumerate((last_ref, before_ref)):
        whole = jnp.concatenate([back_ref[d, i] for d in range(count)], axis=0)
        out_ref[...] = whole.astype(jnp.float32).T


def gather_plan(vectors, blocks, cols):
    n_dev = lax.axis_size(LANES)
    n_col, n_row = lax.axis_size("col"), lax.axis_size("row")
    rows, width = vectors.shape
    slots, orb = blocks.shape[2:4]
    share = width // n_dev
    per_piece = rows // orb
    n_blocks = n_dev * per_piece
    half = slots // 2

    def send(buf, flip_col, flip_row, from_rows=range(n_row)):
        pairs = [
            (c * n_row + r, (c ^ flip_col) * n_row + (r ^ flip_row))
            for c in range(n_col)
            for r in from_rows
        ]
        return lax.ppermute(buf, LANES, pairs)

    def to_mate(*bufs):
        return [send(buf, 1, 0) for buf in bufs]

    own = blocks[0, 0]
    near = send(own, 0, 1)
    inner = send(own, 0, 3, INNER)
    over_own = send(own, 2, 0)

    own_cols = jnp.broadcast_to(jnp.pad(cols[0, 0], (0, orb - slots)), (share, orb))
    shares = jax.ShapeDtypeStruct((n_dev // 2 * per_piece + 1, share, orb), vectors.dtype)
    stay, go = pl.pallas_call(
        functools.partial(split_kernel, n_col, n_row),
        out_shape=[shares, shares],
        in_specs=vmem(2),
        out_specs=vmem(2),
        scratch_shapes=[pltpu.VMEM((n_dev, share, rows), vectors.dtype)],
        compiler_params=pltpu.CompilerParams(vmem_limit_bytes=4 * 2**20),
    )(vectors, own_cols)
    stay, go = regroup(stay, send(go, 1, 0), 1, per_piece)

    stay, go = regroup(stay, send(go, 2, 0), 2, per_piece)
    mates = to_mate(own)
    near = after(near, over_own, go, *mates)
    over_near = after(send(near, 2, 0), rank=3)
    crossed = after(send(near, 0, 3, INNER), rank=1)
    inner = after(inner, near)
    outward = after(send(inner, 0, 1, INNER), rank=1)
    stay, go = regroup(stay, send(go, 0, 1), 4, per_piece)
    mates += to_mate(near, over_own)
    two = pick(INNER, crossed, outward, over_near, go, *mates)

    over_two = send(two, 2, 0)
    outer = after(send(crossed, 0, 1, INNER), rank=1)
    mates += to_mate(two, over_near)
    mine, ids = regroup(stay, send(go, 0, 3), 8, per_piece)
    sa, sta = load(own, near, over_own, over_near, *mates[:3])
    three = pick(INNER, inner, outer, over_two, mine, sa, *mates[3:])

    over_three = send(three[:half], 2, 0)
    side_three = send(over_two[half:], 0, 1)
    mates += to_mate(three, over_two)
    early = [(0, 0), (0, 1), (2, 0), (2, 1), (1, 0), (1, 1), (3, 0)]
    later = [(0, 2), (2, 2), (0, 3), (1, 2), (3, 1), (1, 3), (3, 2)]
    tiles_of = jax.ShapeDtypeStruct((len(later), slots, orb, orb), blocks.dtype)
    sums = jax.ShapeDtypeStruct((n_blocks, share, orb), jnp.float32)
    sb, stb, total = pl.pallas_call(
        functools.partial(first_kernel, early, later, n_col, n_row),
        out_shape=[tiles_of, tiles_of, sums],
        in_specs=smem() + vmem(3) + anywhere(len(later)),
        out_specs=vmem(3),
        scratch_shapes=[
            pltpu.VMEM((n_blocks, share, orb), jnp.bfloat16),
            *[pltpu.VMEM((n_blocks, share, orb), jnp.float32)] * (1 + SPLIT),
            pltpu.SemaphoreType.DMA((len(later),)),
        ],
        compiler_params=pltpu.CompilerParams(vmem_limit_bytes=6 * 2**20),
        cost_estimate=pl.CostEstimate(
            flops=4 * len(early + later) * slots * orb * orb * share,
            bytes_accessed=6 * len(later) * own.size,
            transcendentals=0,
        ),
    )(ids, mine, sa, sta, two, over_two, three, *mates[3:])
    over_three, side_three = after(over_three, sb), after(side_three, sb)
    late = [(2, 3, 0), (2, 3, half), (3, 3, 0), (3, 3, half)]
    late_bufs = [over_three, side_three, *to_mate(over_three, side_three)]

    done = pl.pallas_call(
        functools.partial(filter_kernel, early, later, late, n_col, n_row),
        out_shape=jax.ShapeDtypeStruct((n_dev, 2, share, rows), jnp.bfloat16),
        in_specs=smem() + vmem(6) + anywhere(len(late)),
        out_specs=vmem()[0],
        scratch_shapes=[
            *[pltpu.VMEM((2, slots, orb, orb), blocks.dtype)] * 2,
            pltpu.VMEM((n_blocks, share, orb), jnp.bfloat16),
            *[pltpu.VMEM((n_blocks, share, orb), jnp.float32)] * (3 + SPLIT),
            pltpu.SemaphoreType.DMA((len(late),)),
        ],
        compiler_params=pltpu.CompilerParams(vmem_limit_bytes=12 * 2**20),
    )(ids, mine, total, sa, sta, sb, stb, *late_bufs)
    back = lax.all_to_all(done, LANES, split_axis=0, concat_axis=0, tiled=True)
    whole = jax.ShapeDtypeStruct((rows, width), jnp.float32)
    return pl.pallas_call(
        result_kernel,
        out_shape=[whole, whole],
        in_specs=vmem(),
        out_specs=vmem(2),
        compiler_params=pltpu.CompilerParams(vmem_limit_bytes=4 * 2**20),
    )(back)


def per_device(vectors, blocks, cols):
    n_dev = lax.axis_size(LANES)
    line_of_four = lax.axis_size("col") == 4 and lax.axis_size("row") == 4
    if line_of_four and n_dev * blocks.size * blocks.dtype.itemsize <= GATHER_LIMIT:
        return gather_plan(vectors, blocks, cols)
    return spread_plan(vectors, blocks, cols)


def solution(mesh):
    return jax.shard_map(
        per_device,
        mesh=mesh,
        in_specs=(
            P(("col", "row"), "dom"),
            P(("dom", "col"), "row", None, None, None),
            P(("dom", "col"), "row", None),
        ),
        out_specs=(P(("col", "row"), "dom"), P(("col", "row"), "dom")),
        check_vma=False,
    )
```

```python
import functools

import jax
import jax.numpy as jnp
from jax import lax
from jax.experimental import pallas as pl
from jax.experimental.pallas import tpu as pltpu
from jax.sharding import PartitionSpec as P

PER_ROW = 2
DEG = 4
SPLIT = 4
UNROLL = 2
GATHER_LIMIT = 12 * 2**20
LANES = ("col", "row")
INNER = (1, 2)


def onehot_sum(selected, high_part, low_part):
    first = jnp.einsum("su,sok->uok", selected, high_part, preferred_element_type=jnp.float32)
    second = jnp.einsum("su,sok->uok", selected, low_part, preferred_element_type=jnp.float32)
    return first + second


def apply_pair(send, grouped, col_ids, onehot):
    tile_rows, per_row, orb, _ = grouped.shape
    piece_rows, width = send.shape
    tile_cols = onehot.shape[1]
    wide = lax.all_gather(send, "col", axis=0, tiled=True).reshape(tile_cols, orb, width)
    picked = jnp.take(wide, col_ids, axis=0).reshape(tile_rows, per_row, orb, width)
    direct = jnp.einsum("tpio,tpok->tik", grouped, picked, preferred_element_type=jnp.float32)
    part_rows = lax.psum_scatter(
        direct.reshape(tile_rows * orb, width).astype(jnp.bfloat16),
        "row",
        scatter_dimension=0,
        tiled=True,
    ).astype(jnp.float32)
    tall = lax.all_gather(send, "row", axis=0, tiled=True).reshape(tile_rows, orb, width)
    mirrored = jnp.einsum("tpio,tik->tpok", grouped, tall, preferred_element_type=jnp.float32)
    mirrored = mirrored.reshape(tile_rows * per_row, orb, width)
    high_part = mirrored.astype(jnp.bfloat16)
    low_part = (mirrored - high_part.astype(jnp.float32)).astype(jnp.bfloat16)
    summed = onehot_sum(onehot, high_part, low_part)
    part_cols = lax.psum_scatter(
        summed.reshape(tile_cols * orb, width).astype(jnp.bfloat16),
        "col",
        scatter_dimension=0,
        tiled=True,
    ).astype(jnp.float32)
    return part_rows + part_cols


def spread_plan(vectors, blocks, cols):
    tiles = blocks[0, 0]
    col_ids = cols[0, 0]
    slots, orb, _ = tiles.shape
    tile_rows = slots // PER_ROW
    tile_cols = lax.axis_size("col") * (vectors.shape[0] // orb)
    grouped = tiles.reshape(tile_rows, PER_ROW, orb, orb)
    onehot = (col_ids[:, None] == jnp.arange(tile_cols, dtype=jnp.int32)[None, :]).astype(
        jnp.bfloat16
    )
    prev = vectors.astype(jnp.float32)
    now = apply_pair(vectors, grouped, col_ids, onehot)
    for step in range(DEG - 1):
        nxt = 2.0 * apply_pair(now.astype(jnp.bfloat16), grouped, col_ids, onehot) - prev
        prev, now = (now, nxt)
    return (now, prev)


def vmem(count=1):
    return [pl.BlockSpec(memory_space=pltpu.VMEM)] * count


def smem(count=1):
    return [pl.BlockSpec(memory_space=pltpu.SMEM)] * count


def anywhere(count=1):
    return [pl.BlockSpec(memory_space=pl.ANY)] * count


def nothing(*refs):
    pass


def after(value, *others, rank=0):
    return pl.pallas_call(
        nothing,
        out_shape=jax.ShapeDtypeStruct(value.shape, value.dtype),
        in_specs=anywhere(1 + len(others)),
        out_specs=anywhere()[0],
        input_output_aliases={0: 0},
        compiler_params=pltpu.CompilerParams(vmem_limit_bytes=2**20),
        cost_estimate=pl.CostEstimate(flops=0, bytes_accessed=rank * 2**23, transcendentals=0),
    )(value, *others)


def pick_kernel(rows, one_ref, other_ref, *refs):
    out_ref, sem = refs[-2:]
    row = lax.axis_index("row")
    first = (row == rows[0]) | (row == rows[1])

    @pl.when(first)
    def _():
        copy = pltpu.make_async_copy(one_ref, out_ref, sem)
        copy.start()
        copy.wait()

    @pl.when(jnp.logical_not(first))
    def _():
        copy = pltpu.make_async_copy(other_ref, out_ref, sem)
        copy.start()
        copy.wait()


def pick(rows, one, other, *others):
    return pl.pallas_call(
        functools.partial(pick_kernel, rows),
        out_shape=jax.ShapeDtypeStruct(one.shape, one.dtype),
        in_specs=anywhere(2 + len(others)),
        out_specs=anywhere()[0],
        scratch_shapes=[pltpu.SemaphoreType.DMA(())],
        compiler_params=pltpu.CompilerParams(vmem_limit_bytes=2**20),
    )(one, other, *others)


def split_kernel(n_col, n_row, vectors_ref, cols_ref, stay_ref, go_ref, turned):
    col, row = lax.axis_index("col"), lax.axis_index("row")
    count, share, rows = turned.shape
    orb = stay_ref.shape[2]
    per_piece = rows // orb
    whole = vectors_ref[...].T
    for d in range(count):
        turned[d] = whole[d * share : (d + 1) * share]
    orders = [(y, one, three) for y in range(2) for one in range(2) for three in range(2)]
    ids = cols_ref[...]
    piece = jnp.zeros_like(ids)
    for c in range(1, n_col):
        piece += (ids >= c * per_piece).astype(jnp.int32)
    ids = ids - piece * per_piece + (piece * n_row + row) * per_piece
    for core, out_ref in enumerate((stay_ref, go_ref)):
        for k, (y, one, three) in enumerate(orders):
            peer = (col ^ (core + 2 * y)) * n_row + (row ^ one ^ 3 * three)
            for b in range(per_piece):
                out_ref[k * per_piece + b] = turned[peer, :, b * orb : (b + 1) * orb]
        out_ref[len(orders) * per_piece] = ids.astype(jnp.float32).astype(out_ref.dtype)


def regroup_kernel(sources, count, stay_ref, came_ref, *outs):
    per_piece = (stay_ref.shape[0] - sources) // (sources * count)
    kept = max(count // 2, 1)
    for h, out_ref in enumerate(outs):
        for s in range(2 * sources):
            ref = stay_ref if s < sources else came_ref
            ids = ref[sources * count * per_piece + s % sources]
            if h == 1 and count == 1:
                out_ref[s : s + 1] = ids.astype(jnp.float32)[:1].astype(jnp.int32)
                continue
            for k in range(kept * per_piece):
                out_ref[s * kept * per_piece + k] = ref[(s % sources * count + h * kept) * per_piece + k]
            if count > 1:
                out_ref[2 * sources * kept * per_piece + s] = ids


def regroup(stay, came, sources, per_piece):
    count = (stay.shape[0] // sources - 1) // per_piece
    _, share, orb = stay.shape
    if count > 1:
        out = jax.ShapeDtypeStruct((sources * count * per_piece + 2 * sources, share, orb), stay.dtype)
        outs = [out, out]
    else:
        outs = [
            jax.ShapeDtypeStruct((2 * sources * per_piece, share, orb), stay.dtype),
            jax.ShapeDtypeStruct((2 * sources, orb), jnp.int32),
        ]
    return pl.pallas_call(
        functools.partial(regroup_kernel, sources, count),
        out_shape=outs,
        in_specs=vmem(2),
        out_specs=vmem(2),
        compiler_params=pltpu.CompilerParams(vmem_limit_bytes=2**20),
    )(stay, came)


def place(g, f):
    return (f >> 1) * 8 + ((f & 1) ^ (f >> 1)) * 4 + g


def multiply(t, groups, across, ids_ref, z, straight, scattered):
    tile_rows = z.shape[0] // len(groups)
    orb = z.shape[2]
    for g, group in enumerate(groups):
        if not group:
            continue
        here = across[g] * tile_rows + t
        places = [(tile, t * PER_ROW + p) for tile in group for p in range(PER_ROW)]
        strip = jnp.concatenate([s[slot] for (_, s, _, _), slot in places], axis=1)
        turned = jnp.concatenate([st[i, slot] for (_, _, st, i), slot in places], axis=0)
        where = [ids_ref[place(g, f), slot] for (f, *_), slot in places]
        wide = jnp.concatenate([z[u] for u in where], axis=1)
        straight[here] = jnp.dot(wide, turned, preferred_element_type=jnp.float32)
        mirrored = jnp.dot(z[here], strip, preferred_element_type=jnp.float32)
        for i, u in enumerate(where):
            scattered[i % len(scattered)][u] += mirrored[:, i * orb : (i + 1) * orb]


def clear(refs):
    for ref in refs:
        ref[...] = jnp.zeros_like(ref)


def turn(s_ref, st_ref, i, start, count):
    def four(k, carry):
        for m in range(4):
            st_ref[i, start + 4 * k + m] = s_ref[i, start + 4 * k + m].T
        return carry

    lax.fori_loop(0, count // 4, four, 0)


def turn_all(bufs, st_ref):
    def four(k, carry):
        for i, buf in enumerate(bufs):
            for m in range(4):
                st_ref[i, 4 * k + m] = buf[4 * k + m].T
        return carry

    lax.fori_loop(0, st_ref.shape[1] // 4, four, 0)


def grouped(tiles, n_col, n_row):
    return [[(f, *tiles[g, f]) for f in range(n_row) if (g, f) in tiles] for g in range(n_col)]


def spread_vectors(parts_ref, z, n_col, n_row, now=None):
    per_piece = z.shape[0] // (n_col * n_row)
    across = [lax.axis_index("col") ^ g for g in range(n_col)]
    down = [lax.axis_index("row") ^ f for f in range(n_row)]
    for g in range(n_col):
        for f in range(n_row):
            for b in range(per_piece):
                u = (across[g] * n_row + down[f]) * per_piece + b
                own = parts_ref[place(g, f) * per_piece + b]
                z[u] = own
                if now is not None:
                    now[u] = own.astype(jnp.float32)


def sum_products(groups, n_col, ids_ref, z, straight, scattered):
    across = [lax.axis_index("col") ^ g for g in range(n_col)]
    clear(scattered)

    def block_rows(k, carry):
        for t in range(UNROLL):
            multiply(k * UNROLL + t, groups, across, ids_ref, z, straight, scattered)
        return carry

    lax.fori_loop(0, z.shape[0] // n_col // UNROLL, block_rows, 0)
    total = straight[...]
    for ref in scattered:
        total += ref[...]
    return total


def turned_kernel(*refs):
    turn_all(refs[:-1], refs[-1])


def turned_tiles(*bufs):
    size = len(bufs) * bufs[0].size
    return pl.pallas_call(
        turned_kernel,
        out_shape=jax.ShapeDtypeStruct((len(bufs), *bufs[0].shape), bufs[0].dtype),
        in_specs=vmem(len(bufs)),
        out_specs=vmem()[0],
        compiler_params=pltpu.CompilerParams(vmem_limit_bytes=2**20),
        cost_estimate=pl.CostEstimate(flops=0, bytes_accessed=6 * size, transcendentals=0),
    )(*bufs)


def first_kernel(early, later, n_col, n_row, ids_ref, parts_ref, sta_ref, *refs):
    sa, refs = refs[: len(early)], refs[len(early) :]
    sb, (stb_ref, sum_ref, z, straight, *scattered) = refs[: len(later)], refs[len(later) :]
    spread_vectors(parts_ref, z, n_col, n_row)
    turn_all(sb, stb_ref)
    tiles = {at: (s, sta_ref, i) for i, (at, s) in enumerate(zip(early, sa))}
    tiles.update({at: (s, stb_ref, i) for i, (at, s) in enumerate(zip(later, sb))})
    clear([straight])
    sum_ref[...] = sum_products(grouped(tiles, n_col, n_row), n_col, ids_ref, z, straight, scattered)


def filter_kernel(early, later, late, n_col, n_row, ids_ref, parts_ref, sum_ref, *refs):
    (sta_ref, stb_ref), refs = refs[:2], refs[2:]
    sa, refs = refs[: len(early)], refs[len(early) :]
    sb, refs = refs[: len(later)], refs[len(later) :]
    bufs, (out_ref, s_ref, st_ref, z, now, prev, straight, *scattered, sems) = (
        refs[: len(late)],
        refs[len(late) :],
    )
    n_blocks, share, orb = z.shape
    per_piece = n_blocks // (n_col * n_row)
    rest = sorted({(g, f) for g, f, _ in late})

    copies = []
    for i, (buf, (g, f, start)) in enumerate(zip(bufs, late)):
        target = s_ref.at[rest.index((g, f)), pl.ds(start, buf.shape[0])]
        copies.append(pltpu.make_async_copy(buf, target, sems.at[i]))
        copies[-1].start()
    spread_vectors(parts_ref, z, n_col, n_row, prev)
    for copy, buf, (g, f, start) in zip(copies, bufs, late):
        copy.wait()
        turn(s_ref, st_ref, rest.index((g, f)), start, buf.shape[0])

    tiles = {at: (s_ref.at[i], st_ref, i) for i, at in enumerate(rest)}
    clear([straight])
    total = sum_products(grouped(tiles, n_col, n_row), n_col, ids_ref, z, straight, scattered)
    total += sum_ref[...]
    now[...] = total
    z[...] = total.astype(z.dtype)

    tiles.update({at: (s, sta_ref, i) for i, (at, s) in enumerate(zip(early, sa))})
    tiles.update({at: (s, stb_ref, i) for i, (at, s) in enumerate(zip(later, sb))})
    groups = grouped(tiles, n_col, n_row)

    def one_step(step, carry):
        total = sum_products(groups, n_col, ids_ref, z, straight, scattered)
        total = 2.0 * total - prev[...]
        prev[...] = now[...]
        now[...] = total
        z[...] = total.astype(z.dtype)
        return carry

    lax.fori_loop(1, DEG, one_step, 0)
    for p in range(n_col * n_row):
        for b in range(per_piece):
            u = p * per_piece + b
            out_ref[p, 0, :, b * orb : (b + 1) * orb] = now[u].astype(out_ref.dtype)
            out_ref[p, 1, :, b * orb : (b + 1) * orb] = prev[u].astype(out_ref.dtype)


def result_kernel(back_ref, last_ref, before_ref):
    count, _, share, rows = back_ref.shape
    for i, out_ref in enumerate((last_ref, before_ref)):
        whole = jnp.concatenate([back_ref[d, i] for d in range(count)], axis=0)
        out_ref[...] = whole.astype(jnp.float32).T


def gather_plan(vectors, blocks, cols):
    n_dev = lax.axis_size(LANES)
    n_col, n_row = lax.axis_size("col"), lax.axis_size("row")
    rows, width = vectors.shape
    slots, orb = blocks.shape[2:4]
    share = width // n_dev
    per_piece = rows // orb
    n_blocks = n_dev * per_piece
    half = slots // 2

    def send(buf, flip_col, flip_row, from_rows=range(n_row)):
        pairs = [
            (c * n_row + r, (c ^ flip_col) * n_row + (r ^ flip_row))
            for c in range(n_col)
            for r in from_rows
        ]
        return lax.ppermute(buf, LANES, pairs)

    def to_mate(*bufs):
        return [send(buf, 1, 0) for buf in bufs]

    own = blocks[0, 0]
    near = send(own, 0, 1)
    inner = send(own, 0, 3, INNER)
    over_own = send(own, 2, 0)

    own_cols = jnp.broadcast_to(jnp.pad(cols[0, 0], (0, orb - slots)), (share, orb))
    shares = jax.ShapeDtypeStruct((n_dev // 2 * per_piece + 1, share, orb), vectors.dtype)
    stay, go = pl.pallas_call(
        functools.partial(split_kernel, n_col, n_row),
        out_shape=[shares, shares],
        in_specs=vmem(2),
        out_specs=vmem(2),
        scratch_shapes=[pltpu.VMEM((n_dev, share, rows), vectors.dtype)],
        compiler_params=pltpu.CompilerParams(vmem_limit_bytes=4 * 2**20),
    )(vectors, own_cols)
    stay, go = regroup(stay, send(go, 1, 0), 1, per_piece)

    stay, go = regroup(stay, send(go, 2, 0), 2, per_piece)
    mates = to_mate(own)
    near = after(near, over_own, go, *mates)
    over_near = after(send(near, 2, 0), rank=3)
    crossed = after(send(near, 0, 3, INNER), rank=1)
    inner = after(inner, near)
    outward = after(send(inner, 0, 1, INNER), rank=1)
    stay, go = regroup(stay, send(go, 0, 1), 4, per_piece)
    mates += to_mate(near, over_own)
    two = pick(INNER, crossed, outward, over_near, go, *mates)

    over_two = send(two, 2, 0)
    outer = after(send(crossed, 0, 1, INNER), rank=1)
    mates += to_mate(two, over_near)
    mine, ids = regroup(stay, send(go, 0, 3), 8, per_piece)
    sa = [own, near, over_own, over_near, *mates[:3]]
    sta = turned_tiles(*sa)
    three = pick(INNER, inner, outer, over_two, mine, sta, *mates[3:])

    over_three = send(three[:half], 2, 0)
    side_three = send(over_two[half:], 0, 1)
    mates += to_mate(three, over_two)
    early = [(0, 0), (0, 1), (2, 0), (2, 1), (1, 0), (1, 1), (3, 0)]
    later = [(0, 2), (2, 2), (0, 3), (1, 2), (3, 1), (1, 3), (3, 2)]
    tiles_of = jax.ShapeDtypeStruct((len(later), slots, orb, orb), blocks.dtype)
    sums = jax.ShapeDtypeStruct((n_blocks, share, orb), jnp.float32)
    sb = [two, over_two, three, *mates[3:]]
    stb, total = pl.pallas_call(
        functools.partial(first_kernel, early, later, n_col, n_row),
        out_shape=[tiles_of, sums],
        in_specs=smem() + vmem(2 + len(early + later)),
        out_specs=vmem(2),
        scratch_shapes=[
            pltpu.VMEM((n_blocks, share, orb), jnp.bfloat16),
            *[pltpu.VMEM((n_blocks, share, orb), jnp.float32)] * (1 + SPLIT),
        ],
        compiler_params=pltpu.CompilerParams(vmem_limit_bytes=6 * 2**20),
        cost_estimate=pl.CostEstimate(
            flops=4 * len(early + later) * slots * orb * orb * share,
            bytes_accessed=6 * len(later) * own.size,
            transcendentals=0,
        ),
    )(ids, mine, sta, *sa, *sb)
    over_three, side_three = after(over_three, stb), after(side_three, stb)
    late = [(2, 3, 0), (2, 3, half), (3, 3, 0), (3, 3, half)]
    late_bufs = [over_three, side_three, *to_mate(over_three, side_three)]

    done = pl.pallas_call(
        functools.partial(filter_kernel, early, later, late, n_col, n_row),
        out_shape=jax.ShapeDtypeStruct((n_dev, 2, share, rows), jnp.bfloat16),
        in_specs=smem() + vmem(4 + len(early + later)) + anywhere(len(late)),
        out_specs=vmem()[0],
        scratch_shapes=[
            *[pltpu.VMEM((2, slots, orb, orb), blocks.dtype)] * 2,
            pltpu.VMEM((n_blocks, share, orb), jnp.bfloat16),
            *[pltpu.VMEM((n_blocks, share, orb), jnp.float32)] * (3 + SPLIT),
            pltpu.SemaphoreType.DMA((len(late),)),
        ],
        compiler_params=pltpu.CompilerParams(vmem_limit_bytes=12 * 2**20),
    )(ids, mine, total, sta, stb, *sa, *sb, *late_bufs)
    back = lax.all_to_all(done, LANES, split_axis=0, concat_axis=0, tiled=True)
    whole = jax.ShapeDtypeStruct((rows, width), jnp.float32)
    return pl.pallas_call(
        result_kernel,
        out_shape=[whole, whole],
        in_specs=vmem(),
        out_specs=vmem(2),
        compiler_params=pltpu.CompilerParams(vmem_limit_bytes=4 * 2**20),
    )(back)


def per_device(vectors, blocks, cols):
    n_dev = lax.axis_size(LANES)
    line_of_four = lax.axis_size("col") == 4 and lax.axis_size("row") == 4
    if line_of_four and n_dev * blocks.size * blocks.dtype.itemsize <= GATHER_LIMIT:
        return gather_plan(vectors, blocks, cols)
    return spread_plan(vectors, blocks, cols)


def solution(mesh):
    return jax.shard_map(
        per_device,
        mesh=mesh,
        in_specs=(
            P(("col", "row"), "dom"),
            P(("dom", "col"), "row", None, None, None),
            P(("dom", "col"), "row", None),
        ),
        out_specs=(P(("col", "row"), "dom"), P(("col", "row"), "dom")),
        check_vma=False,
    )
```

```python
import functools

import jax
import jax.numpy as jnp
from jax import lax
from jax.experimental import pallas as pl
from jax.experimental.pallas import tpu as pltpu
from jax.sharding import PartitionSpec as P

PER_ROW = 2
DEG = 4
SPLIT = 4
UNROLL = 4
GATHER_LIMIT = 12 * 2**20
LANES = ("col", "row")
INNER = (1, 2)


def onehot_sum(selected, high_part, low_part):
    first = jnp.einsum("su,sok->uok", selected, high_part, preferred_element_type=jnp.float32)
    second = jnp.einsum("su,sok->uok", selected, low_part, preferred_element_type=jnp.float32)
    return first + second


def apply_pair(send, grouped, col_ids, onehot):
    tile_rows, per_row, orb, _ = grouped.shape
    piece_rows, width = send.shape
    tile_cols = onehot.shape[1]
    wide = lax.all_gather(send, "col", axis=0, tiled=True).reshape(tile_cols, orb, width)
    picked = jnp.take(wide, col_ids, axis=0).reshape(tile_rows, per_row, orb, width)
    direct = jnp.einsum("tpio,tpok->tik", grouped, picked, preferred_element_type=jnp.float32)
    part_rows = lax.psum_scatter(
        direct.reshape(tile_rows * orb, width).astype(jnp.bfloat16),
        "row",
        scatter_dimension=0,
        tiled=True,
    ).astype(jnp.float32)
    tall = lax.all_gather(send, "row", axis=0, tiled=True).reshape(tile_rows, orb, width)
    mirrored = jnp.einsum("tpio,tik->tpok", grouped, tall, preferred_element_type=jnp.float32)
    mirrored = mirrored.reshape(tile_rows * per_row, orb, width)
    high_part = mirrored.astype(jnp.bfloat16)
    low_part = (mirrored - high_part.astype(jnp.float32)).astype(jnp.bfloat16)
    summed = onehot_sum(onehot, high_part, low_part)
    part_cols = lax.psum_scatter(
        summed.reshape(tile_cols * orb, width).astype(jnp.bfloat16),
        "col",
        scatter_dimension=0,
        tiled=True,
    ).astype(jnp.float32)
    return part_rows + part_cols


def spread_plan(vectors, blocks, cols):
    tiles = blocks[0, 0]
    col_ids = cols[0, 0]
    slots, orb, _ = tiles.shape
    tile_rows = slots // PER_ROW
    tile_cols = lax.axis_size("col") * (vectors.shape[0] // orb)
    grouped = tiles.reshape(tile_rows, PER_ROW, orb, orb)
    onehot = (col_ids[:, None] == jnp.arange(tile_cols, dtype=jnp.int32)[None, :]).astype(
        jnp.bfloat16
    )
    prev = vectors.astype(jnp.float32)
    now = apply_pair(vectors, grouped, col_ids, onehot)
    for step in range(DEG - 1):
        nxt = 2.0 * apply_pair(now.astype(jnp.bfloat16), grouped, col_ids, onehot) - prev
        prev, now = (now, nxt)
    return (now, prev)


def vmem(count=1):
    return [pl.BlockSpec(memory_space=pltpu.VMEM)] * count


def smem(count=1):
    return [pl.BlockSpec(memory_space=pltpu.SMEM)] * count


def anywhere(count=1):
    return [pl.BlockSpec(memory_space=pl.ANY)] * count


def nothing(*refs):
    pass


def after(value, *others, rank=0):
    return pl.pallas_call(
        nothing,
        out_shape=jax.ShapeDtypeStruct(value.shape, value.dtype),
        in_specs=anywhere(1 + len(others)),
        out_specs=anywhere()[0],
        input_output_aliases={0: 0},
        compiler_params=pltpu.CompilerParams(vmem_limit_bytes=2**20),
        cost_estimate=pl.CostEstimate(flops=0, bytes_accessed=rank * 2**23, transcendentals=0),
    )(value, *others)


def pick_kernel(rows, one_ref, other_ref, *refs):
    out_ref, sem = refs[-2:]
    row = lax.axis_index("row")
    first = (row == rows[0]) | (row == rows[1])

    @pl.when(first)
    def _():
        copy = pltpu.make_async_copy(one_ref, out_ref, sem)
        copy.start()
        copy.wait()

    @pl.when(jnp.logical_not(first))
    def _():
        copy = pltpu.make_async_copy(other_ref, out_ref, sem)
        copy.start()
        copy.wait()


def pick(rows, one, other, *others):
    return pl.pallas_call(
        functools.partial(pick_kernel, rows),
        out_shape=jax.ShapeDtypeStruct(one.shape, one.dtype),
        in_specs=anywhere(2 + len(others)),
        out_specs=anywhere()[0],
        scratch_shapes=[pltpu.SemaphoreType.DMA(())],
        compiler_params=pltpu.CompilerParams(vmem_limit_bytes=2**20),
    )(one, other, *others)


def split_kernel(n_col, n_row, vectors_ref, cols_ref, stay_ref, go_ref, turned):
    col, row = lax.axis_index("col"), lax.axis_index("row")
    count, share, rows = turned.shape
    orb = stay_ref.shape[2]
    per_piece = rows // orb
    whole = vectors_ref[...].T
    for d in range(count):
        turned[d] = whole[d * share : (d + 1) * share]
    orders = [(y, one, three) for y in range(2) for one in range(2) for three in range(2)]
    ids = cols_ref[...]
    piece = jnp.zeros_like(ids)
    for c in range(1, n_col):
        piece += (ids >= c * per_piece).astype(jnp.int32)
    ids = ids - piece * per_piece + (piece * n_row + row) * per_piece
    for core, out_ref in enumerate((stay_ref, go_ref)):
        for k, (y, one, three) in enumerate(orders):
            peer = (col ^ (core + 2 * y)) * n_row + (row ^ one ^ 3 * three)
            for b in range(per_piece):
                out_ref[k * per_piece + b] = turned[peer, :, b * orb : (b + 1) * orb]
        out_ref[len(orders) * per_piece] = ids.astype(jnp.float32).astype(out_ref.dtype)


def regroup_kernel(sources, count, stay_ref, came_ref, *outs):
    per_piece = (stay_ref.shape[0] - sources) // (sources * count)
    kept = max(count // 2, 1)
    for h, out_ref in enumerate(outs):
        for s in range(2 * sources):
            ref = stay_ref if s < sources else came_ref
            ids = ref[sources * count * per_piece + s % sources]
            if h == 1 and count == 1:
                out_ref[s : s + 1] = ids.astype(jnp.float32)[:1].astype(jnp.int32)
                continue
            for k in range(kept * per_piece):
                out_ref[s * kept * per_piece + k] = ref[(s % sources * count + h * kept) * per_piece + k]
            if count > 1:
                out_ref[2 * sources * kept * per_piece + s] = ids


def regroup(stay, came, sources, per_piece):
    count = (stay.shape[0] // sources - 1) // per_piece
    _, share, orb = stay.shape
    if count > 1:
        out = jax.ShapeDtypeStruct((sources * count * per_piece + 2 * sources, share, orb), stay.dtype)
        outs = [out, out]
    else:
        outs = [
            jax.ShapeDtypeStruct((2 * sources * per_piece, share, orb), stay.dtype),
            jax.ShapeDtypeStruct((2 * sources, orb), jnp.int32),
        ]
    return pl.pallas_call(
        functools.partial(regroup_kernel, sources, count),
        out_shape=outs,
        in_specs=vmem(2),
        out_specs=vmem(2),
        compiler_params=pltpu.CompilerParams(vmem_limit_bytes=2**20),
    )(stay, came)


def place(g, f):
    return (f >> 1) * 8 + ((f & 1) ^ (f >> 1)) * 4 + g


def multiply(t, groups, across, ids_ref, z, straight, scattered):
    tile_rows = z.shape[0] // len(groups)
    orb = z.shape[2]
    for g, group in enumerate(groups):
        if not group:
            continue
        here = across[g] * tile_rows + t
        places = [(tile, t * PER_ROW + p) for tile in group for p in range(PER_ROW)]
        strip = jnp.concatenate([s[slot] for (_, s, _, _), slot in places], axis=1)
        turned = jnp.concatenate([st[i, slot] for (_, _, st, i), slot in places], axis=0)
        where = [ids_ref[place(g, f), slot] for (f, *_), slot in places]
        wide = jnp.concatenate([z[u] for u in where], axis=1)
        straight[here] = jnp.dot(wide, turned, preferred_element_type=jnp.float32)
        mirrored = jnp.dot(z[here], strip, preferred_element_type=jnp.float32)
        for i, u in enumerate(where):
            scattered[i % len(scattered)][u] += mirrored[:, i * orb : (i + 1) * orb]


def clear(refs):
    for ref in refs:
        ref[...] = jnp.zeros_like(ref)


def turn(s_ref, st_ref, i, start, count):
    def four(k, carry):
        for m in range(4):
            st_ref[i, start + 4 * k + m] = s_ref[i, start + 4 * k + m].T
        return carry

    lax.fori_loop(0, count // 4, four, 0)


def turn_all(bufs, st_ref):
    def four(k, carry):
        for i, buf in enumerate(bufs):
            for m in range(4):
                st_ref[i, 4 * k + m] = buf[4 * k + m].T
        return carry

    lax.fori_loop(0, st_ref.shape[1] // 4, four, 0)


def grouped(tiles, n_col, n_row):
    return [[(f, *tiles[g, f]) for f in range(n_row) if (g, f) in tiles] for g in range(n_col)]


def spread_vectors(parts_ref, z, n_col, n_row, now=None):
    per_piece = z.shape[0] // (n_col * n_row)
    across = [lax.axis_index("col") ^ g for g in range(n_col)]
    down = [lax.axis_index("row") ^ f for f in range(n_row)]
    for g in range(n_col):
        for f in range(n_row):
            for b in range(per_piece):
                u = (across[g] * n_row + down[f]) * per_piece + b
                own = parts_ref[place(g, f) * per_piece + b]
                z[u] = own
                if now is not None:
                    now[u] = own.astype(jnp.float32)


def sum_products(groups, n_col, ids_ref, z, straight, scattered):
    across = [lax.axis_index("col") ^ g for g in range(n_col)]
    clear(scattered)

    def block_rows(k, carry):
        for t in range(UNROLL):
            multiply(k * UNROLL + t, groups, across, ids_ref, z, straight, scattered)
        return carry

    lax.fori_loop(0, z.shape[0] // n_col // UNROLL, block_rows, 0)
    total = straight[...]
    for ref in scattered:
        total += ref[...]
    return total


def turned_kernel(*refs):
    turn_all(refs[:-1], refs[-1])


def turned_tiles(*bufs):
    size = len(bufs) * bufs[0].size
    return pl.pallas_call(
        turned_kernel,
        out_shape=jax.ShapeDtypeStruct((len(bufs), *bufs[0].shape), bufs[0].dtype),
        in_specs=vmem(len(bufs)),
        out_specs=vmem()[0],
        compiler_params=pltpu.CompilerParams(vmem_limit_bytes=2**20),
        cost_estimate=pl.CostEstimate(flops=0, bytes_accessed=6 * size, transcendentals=0),
    )(*bufs)


def first_kernel(early, later, n_col, n_row, ids_ref, parts_ref, sta_ref, *refs):
    sa, refs = refs[: len(early)], refs[len(early) :]
    sb, (stb_ref, sum_ref, z, straight, *scattered) = refs[: len(later)], refs[len(later) :]
    spread_vectors(parts_ref, z, n_col, n_row)
    turn_all(sb, stb_ref)
    tiles = {at: (s, sta_ref, i) for i, (at, s) in enumerate(zip(early, sa))}
    tiles.update({at: (s, stb_ref, i) for i, (at, s) in enumerate(zip(later, sb))})
    clear([straight])
    sum_ref[...] = sum_products(grouped(tiles, n_col, n_row), n_col, ids_ref, z, straight, scattered)


def filter_kernel(early, later, late, n_col, n_row, ids_ref, parts_ref, sum_ref, *refs):
    (sta_ref, stb_ref), refs = refs[:2], refs[2:]
    sa, refs = refs[: len(early)], refs[len(early) :]
    sb, refs = refs[: len(later)], refs[len(later) :]
    bufs, (out_ref, s_ref, st_ref, z, now, prev, straight, *scattered, sems) = (
        refs[: len(late)],
        refs[len(late) :],
    )
    n_blocks, share, orb = z.shape
    per_piece = n_blocks // (n_col * n_row)
    rest = sorted({(g, f) for g, f, _ in late})

    copies = []
    for i, (buf, (g, f, start)) in enumerate(zip(bufs, late)):
        target = s_ref.at[rest.index((g, f)), pl.ds(start, buf.shape[0])]
        copies.append(pltpu.make_async_copy(buf, target, sems.at[i]))
        copies[-1].start()
    spread_vectors(parts_ref, z, n_col, n_row, prev)
    for copy, buf, (g, f, start) in zip(copies, bufs, late):
        copy.wait()
        turn(s_ref, st_ref, rest.index((g, f)), start, buf.shape[0])

    tiles = {at: (s_ref.at[i], st_ref, i) for i, at in enumerate(rest)}
    clear([straight])
    total = sum_products(grouped(tiles, n_col, n_row), n_col, ids_ref, z, straight, scattered)
    total += sum_ref[...]
    now[...] = total
    z[...] = total.astype(z.dtype)

    tiles.update({at: (s, sta_ref, i) for i, (at, s) in enumerate(zip(early, sa))})
    tiles.update({at: (s, stb_ref, i) for i, (at, s) in enumerate(zip(later, sb))})
    groups = grouped(tiles, n_col, n_row)

    def one_step(step, carry):
        total = sum_products(groups, n_col, ids_ref, z, straight, scattered)
        total = 2.0 * total - prev[...]
        prev[...] = now[...]
        now[...] = total
        z[...] = total.astype(z.dtype)
        return carry

    lax.fori_loop(1, DEG, one_step, 0)
    for p in range(n_col * n_row):
        for b in range(per_piece):
            u = p * per_piece + b
            out_ref[p, 0, :, b * orb : (b + 1) * orb] = now[u].astype(out_ref.dtype)
            out_ref[p, 1, :, b * orb : (b + 1) * orb] = prev[u].astype(out_ref.dtype)


def result_kernel(back_ref, last_ref, before_ref):
    count, _, share, rows = back_ref.shape
    for i, out_ref in enumerate((last_ref, before_ref)):
        whole = jnp.concatenate([back_ref[d, i] for d in range(count)], axis=0)
        out_ref[...] = whole.astype(jnp.float32).T


def gather_plan(vectors, blocks, cols):
    n_dev = lax.axis_size(LANES)
    n_col, n_row = lax.axis_size("col"), lax.axis_size("row")
    rows, width = vectors.shape
    slots, orb = blocks.shape[2:4]
    share = width // n_dev
    per_piece = rows // orb
    n_blocks = n_dev * per_piece
    half = slots // 2

    def send(buf, flip_col, flip_row, from_rows=range(n_row)):
        pairs = [
            (c * n_row + r, (c ^ flip_col) * n_row + (r ^ flip_row))
            for c in range(n_col)
            for r in from_rows
        ]
        return lax.ppermute(buf, LANES, pairs)

    def to_mate(*bufs):
        return [send(buf, 1, 0) for buf in bufs]

    own = blocks[0, 0]
    near = send(own, 0, 1)
    inner = send(own, 0, 3, INNER)
    over_own = after(send(own, 2, 0), rank=1)

    own_cols = jnp.broadcast_to(jnp.pad(cols[0, 0], (0, orb - slots)), (share, orb))
    shares = jax.ShapeDtypeStruct((n_dev // 2 * per_piece + 1, share, orb), vectors.dtype)
    stay, go = pl.pallas_call(
        functools.partial(split_kernel, n_col, n_row),
        out_shape=[shares, shares],
        in_specs=vmem(2),
        out_specs=vmem(2),
        scratch_shapes=[pltpu.VMEM((n_dev, share, rows), vectors.dtype)],
        compiler_params=pltpu.CompilerParams(vmem_limit_bytes=4 * 2**20),
    )(vectors, own_cols)
    stay, go = regroup(stay, send(go, 1, 0), 1, per_piece)

    stay, go = regroup(stay, send(go, 2, 0), 2, per_piece)
    mates = to_mate(own)
    near = after(near, over_own, go, *mates)
    over_near = after(send(near, 2, 0), rank=3)
    crossed = after(send(near, 0, 3, INNER), rank=1)
    inner = after(inner, near)
    outward = after(send(inner, 0, 1, INNER), rank=1)
    stay, go = regroup(stay, send(go, 0, 1), 4, per_piece)
    mates += to_mate(near, over_own)
    two = pick(INNER, crossed, outward, over_near, go, *mates)

    over_two = send(two, 2, 0)
    outer = after(send(crossed, 0, 1, INNER), rank=1)
    mates += to_mate(two, over_near)
    mine, ids = regroup(stay, send(go, 0, 3), 8, per_piece)
    sa = [own, near, over_own, over_near, *mates[:3]]
    sta = turned_tiles(*sa)
    three = pick(INNER, inner, outer, over_two, mine, sta, *mates[3:])

    over_three = send(three[:half], 2, 0)
    side_three = send(over_two[half:], 0, 1)
    mates += to_mate(three, over_two)
    early = [(0, 0), (0, 1), (2, 0), (2, 1), (1, 0), (1, 1), (3, 0)]
    later = [(0, 2), (2, 2), (0, 3), (1, 2), (3, 1), (1, 3), (3, 2)]
    tiles_of = jax.ShapeDtypeStruct((len(later), slots, orb, orb), blocks.dtype)
    sums = jax.ShapeDtypeStruct((n_blocks, share, orb), jnp.float32)
    sb = [two, over_two, three, *mates[3:]]
    stb, total = pl.pallas_call(
        functools.partial(first_kernel, early, later, n_col, n_row),
        out_shape=[tiles_of, sums],
        in_specs=smem() + vmem(2 + len(early + later)),
        out_specs=vmem(2),
        scratch_shapes=[
            pltpu.VMEM((n_blocks, share, orb), jnp.bfloat16),
            *[pltpu.VMEM((n_blocks, share, orb), jnp.float32)] * (1 + SPLIT),
        ],
        compiler_params=pltpu.CompilerParams(vmem_limit_bytes=6 * 2**20),
        cost_estimate=pl.CostEstimate(
            flops=4 * len(early + later) * slots * orb * orb * share,
            bytes_accessed=6 * len(later) * own.size,
            transcendentals=0,
        ),
    )(ids, mine, sta, *sa, *sb)
    over_three, side_three = after(over_three, stb), after(side_three, stb)
    late = [(2, 3, 0), (2, 3, half), (3, 3, 0), (3, 3, half)]
    late_bufs = [over_three, side_three, *to_mate(over_three, side_three)]

    done = pl.pallas_call(
        functools.partial(filter_kernel, early, later, late, n_col, n_row),
        out_shape=jax.ShapeDtypeStruct((n_dev, 2, share, rows), jnp.bfloat16),
        in_specs=smem() + vmem(4 + len(early + later)) + anywhere(len(late)),
        out_specs=vmem()[0],
        scratch_shapes=[
            *[pltpu.VMEM((2, slots, orb, orb), blocks.dtype)] * 2,
            pltpu.VMEM((n_blocks, share, orb), jnp.bfloat16),
            *[pltpu.VMEM((n_blocks, share, orb), jnp.float32)] * (3 + SPLIT),
            pltpu.SemaphoreType.DMA((len(late),)),
        ],
        compiler_params=pltpu.CompilerParams(vmem_limit_bytes=12 * 2**20),
    )(ids, mine, total, sta, stb, *sa, *sb, *late_bufs)
    back = lax.all_to_all(done, LANES, split_axis=0, concat_axis=0, tiled=True)
    whole = jax.ShapeDtypeStruct((rows, width), jnp.float32)
    return pl.pallas_call(
        result_kernel,
        out_shape=[whole, whole],
        in_specs=vmem(),
        out_specs=vmem(2),
        compiler_params=pltpu.CompilerParams(vmem_limit_bytes=4 * 2**20),
    )(back)


def per_device(vectors, blocks, cols):
    n_dev = lax.axis_size(LANES)
    line_of_four = lax.axis_size("col") == 4 and lax.axis_size("row") == 4
    if line_of_four and n_dev * blocks.size * blocks.dtype.itemsize <= GATHER_LIMIT:
        return gather_plan(vectors, blocks, cols)
    return spread_plan(vectors, blocks, cols)


def solution(mesh):
    return jax.shard_map(
        per_device,
        mesh=mesh,
        in_specs=(
            P(("col", "row"), "dom"),
            P(("dom", "col"), "row", None, None, None),
            P(("dom", "col"), "row", None),
        ),
        out_specs=(P(("col", "row"), "dom"), P(("col", "row"), "dom")),
        check_vma=False,
    )
```

```python
import functools

import jax
import jax.numpy as jnp
from jax import lax
from jax.experimental import pallas as pl
from jax.experimental.pallas import tpu as pltpu
from jax.sharding import PartitionSpec as P

PER_ROW = 2
DEG = 4
SPLIT = 4
UNROLL = 8
GATHER_LIMIT = 12 * 2**20
LANES = ("col", "row")
INNER = (1, 2)


def onehot_sum(selected, high_part, low_part):
    first = jnp.einsum("su,sok->uok", selected, high_part, preferred_element_type=jnp.float32)
    second = jnp.einsum("su,sok->uok", selected, low_part, preferred_element_type=jnp.float32)
    return first + second


def apply_pair(send, grouped, col_ids, onehot):
    tile_rows, per_row, orb, _ = grouped.shape
    piece_rows, width = send.shape
    tile_cols = onehot.shape[1]
    wide = lax.all_gather(send, "col", axis=0, tiled=True).reshape(tile_cols, orb, width)
    picked = jnp.take(wide, col_ids, axis=0).reshape(tile_rows, per_row, orb, width)
    direct = jnp.einsum("tpio,tpok->tik", grouped, picked, preferred_element_type=jnp.float32)
    part_rows = lax.psum_scatter(
        direct.reshape(tile_rows * orb, width).astype(jnp.bfloat16),
        "row",
        scatter_dimension=0,
        tiled=True,
    ).astype(jnp.float32)
    tall = lax.all_gather(send, "row", axis=0, tiled=True).reshape(tile_rows, orb, width)
    mirrored = jnp.einsum("tpio,tik->tpok", grouped, tall, preferred_element_type=jnp.float32)
    mirrored = mirrored.reshape(tile_rows * per_row, orb, width)
    high_part = mirrored.astype(jnp.bfloat16)
    low_part = (mirrored - high_part.astype(jnp.float32)).astype(jnp.bfloat16)
    summed = onehot_sum(onehot, high_part, low_part)
    part_cols = lax.psum_scatter(
        summed.reshape(tile_cols * orb, width).astype(jnp.bfloat16),
        "col",
        scatter_dimension=0,
        tiled=True,
    ).astype(jnp.float32)
    return part_rows + part_cols


def spread_plan(vectors, blocks, cols):
    tiles = blocks[0, 0]
    col_ids = cols[0, 0]
    slots, orb, _ = tiles.shape
    tile_rows = slots // PER_ROW
    tile_cols = lax.axis_size("col") * (vectors.shape[0] // orb)
    grouped = tiles.reshape(tile_rows, PER_ROW, orb, orb)
    onehot = (col_ids[:, None] == jnp.arange(tile_cols, dtype=jnp.int32)[None, :]).astype(
        jnp.bfloat16
    )
    prev = vectors.astype(jnp.float32)
    now = apply_pair(vectors, grouped, col_ids, onehot)
    for step in range(DEG - 1):
        nxt = 2.0 * apply_pair(now.astype(jnp.bfloat16), grouped, col_ids, onehot) - prev
        prev, now = (now, nxt)
    return (now, prev)


def vmem(count=1):
    return [pl.BlockSpec(memory_space=pltpu.VMEM)] * count


def smem(count=1):
    return [pl.BlockSpec(memory_space=pltpu.SMEM)] * count


def anywhere(count=1):
    return [pl.BlockSpec(memory_space=pl.ANY)] * count


def nothing(*refs):
    pass


def after(value, *others, rank=0):
    return pl.pallas_call(
        nothing,
        out_shape=jax.ShapeDtypeStruct(value.shape, value.dtype),
        in_specs=anywhere(1 + len(others)),
        out_specs=anywhere()[0],
        input_output_aliases={0: 0},
        compiler_params=pltpu.CompilerParams(vmem_limit_bytes=2**20),
        cost_estimate=pl.CostEstimate(flops=0, bytes_accessed=rank * 2**23, transcendentals=0),
    )(value, *others)


def pick_kernel(rows, one_ref, other_ref, *refs):
    out_ref, sem = refs[-2:]
    row = lax.axis_index("row")
    first = (row == rows[0]) | (row == rows[1])

    @pl.when(first)
    def _():
        copy = pltpu.make_async_copy(one_ref, out_ref, sem)
        copy.start()
        copy.wait()

    @pl.when(jnp.logical_not(first))
    def _():
        copy = pltpu.make_async_copy(other_ref, out_ref, sem)
        copy.start()
        copy.wait()


def pick(rows, one, other, *others):
    return pl.pallas_call(
        functools.partial(pick_kernel, rows),
        out_shape=jax.ShapeDtypeStruct(one.shape, one.dtype),
        in_specs=anywhere(2 + len(others)),
        out_specs=anywhere()[0],
        scratch_shapes=[pltpu.SemaphoreType.DMA(())],
        compiler_params=pltpu.CompilerParams(vmem_limit_bytes=2**20),
    )(one, other, *others)


def split_kernel(n_col, n_row, vectors_ref, cols_ref, stay_ref, go_ref, turned):
    col, row = lax.axis_index("col"), lax.axis_index("row")
    count, share, rows = turned.shape
    orb = stay_ref.shape[2]
    per_piece = rows // orb
    whole = vectors_ref[...].T
    for d in range(count):
        turned[d] = whole[d * share : (d + 1) * share]
    orders = [(y, one, three) for y in range(2) for one in range(2) for three in range(2)]
    ids = cols_ref[...]
    piece = jnp.zeros_like(ids)
    for c in range(1, n_col):
        piece += (ids >= c * per_piece).astype(jnp.int32)
    ids = ids - piece * per_piece + (piece * n_row + row) * per_piece
    for core, out_ref in enumerate((stay_ref, go_ref)):
        for k, (y, one, three) in enumerate(orders):
            peer = (col ^ (core + 2 * y)) * n_row + (row ^ one ^ 3 * three)
            for b in range(per_piece):
                out_ref[k * per_piece + b] = turned[peer, :, b * orb : (b + 1) * orb]
        out_ref[len(orders) * per_piece] = ids.astype(jnp.float32).astype(out_ref.dtype)


def regroup_kernel(sources, count, stay_ref, came_ref, *outs):
    per_piece = (stay_ref.shape[0] - sources) // (sources * count)
    kept = max(count // 2, 1)
    for h, out_ref in enumerate(outs):
        for s in range(2 * sources):
            ref = stay_ref if s < sources else came_ref
            ids = ref[sources * count * per_piece + s % sources]
            if h == 1 and count == 1:
                out_ref[s : s + 1] = ids.astype(jnp.float32)[:1].astype(jnp.int32)
                continue
            for k in range(kept * per_piece):
                out_ref[s * kept * per_piece + k] = ref[(s % sources * count + h * kept) * per_piece + k]
            if count > 1:
                out_ref[2 * sources * kept * per_piece + s] = ids


def regroup(stay, came, sources, per_piece):
    count = (stay.shape[0] // sources - 1) // per_piece
    _, share, orb = stay.shape
    if count > 1:
        out = jax.ShapeDtypeStruct((sources * count * per_piece + 2 * sources, share, orb), stay.dtype)
        outs = [out, out]
    else:
        outs = [
            jax.ShapeDtypeStruct((2 * sources * per_piece, share, orb), stay.dtype),
            jax.ShapeDtypeStruct((2 * sources, orb), jnp.int32),
        ]
    return pl.pallas_call(
        functools.partial(regroup_kernel, sources, count),
        out_shape=outs,
        in_specs=vmem(2),
        out_specs=vmem(2),
        compiler_params=pltpu.CompilerParams(vmem_limit_bytes=2**20),
    )(stay, came)


def place(g, f):
    return (f >> 1) * 8 + ((f & 1) ^ (f >> 1)) * 4 + g


def multiply(t, groups, across, ids_ref, z, straight, scattered):
    tile_rows = z.shape[0] // len(groups)
    orb = z.shape[2]
    for g, group in enumerate(groups):
        if not group:
            continue
        here = across[g] * tile_rows + t
        places = [(tile, t * PER_ROW + p) for tile in group for p in range(PER_ROW)]
        strip = jnp.concatenate([s[slot] for (_, s, _, _), slot in places], axis=1)
        turned = jnp.concatenate([st[i, slot] for (_, _, st, i), slot in places], axis=0)
        where = [ids_ref[place(g, f), slot] for (f, *_), slot in places]
        wide = jnp.concatenate([z[u] for u in where], axis=1)
        straight[here] = jnp.dot(wide, turned, preferred_element_type=jnp.float32)
        mirrored = jnp.dot(z[here], strip, preferred_element_type=jnp.float32)
        for i, u in enumerate(where):
            scattered[i % len(scattered)][u] += mirrored[:, i * orb : (i + 1) * orb]


def clear(refs):
    for ref in refs:
        ref[...] = jnp.zeros_like(ref)


def turn(s_ref, st_ref, i, start, count):
    def four(k, carry):
        for m in range(4):
            st_ref[i, start + 4 * k + m] = s_ref[i, start + 4 * k + m].T
        return carry

    lax.fori_loop(0, count // 4, four, 0)


def turn_all(bufs, st_ref):
    def four(k, carry):
        for i, buf in enumerate(bufs):
            for m in range(4):
                st_ref[i, 4 * k + m] = buf[4 * k + m].T
        return carry

    lax.fori_loop(0, st_ref.shape[1] // 4, four, 0)


def grouped(tiles, n_col, n_row):
    return [[(f, *tiles[g, f]) for f in range(n_row) if (g, f) in tiles] for g in range(n_col)]


def spread_vectors(parts_ref, z, n_col, n_row, now=None):
    per_piece = z.shape[0] // (n_col * n_row)
    across = [lax.axis_index("col") ^ g for g in range(n_col)]
    down = [lax.axis_index("row") ^ f for f in range(n_row)]
    for g in range(n_col):
        for f in range(n_row):
            for b in range(per_piece):
                u = (across[g] * n_row + down[f]) * per_piece + b
                own = parts_ref[place(g, f) * per_piece + b]
                z[u] = own
                if now is not None:
                    now[u] = own.astype(jnp.float32)


def sum_products(groups, n_col, ids_ref, z, straight, scattered):
    across = [lax.axis_index("col") ^ g for g in range(n_col)]
    clear(scattered)

    def block_rows(k, carry):
        for t in range(UNROLL):
            multiply(k * UNROLL + t, groups, across, ids_ref, z, straight, scattered)
        return carry

    lax.fori_loop(0, z.shape[0] // n_col // UNROLL, block_rows, 0)
    total = straight[...]
    for ref in scattered:
        total += ref[...]
    return total


def turned_kernel(*refs):
    turn_all(refs[:-1], refs[-1])


def turned_tiles(*bufs):
    size = len(bufs) * bufs[0].size
    return pl.pallas_call(
        turned_kernel,
        out_shape=jax.ShapeDtypeStruct((len(bufs), *bufs[0].shape), bufs[0].dtype),
        in_specs=vmem(len(bufs)),
        out_specs=vmem()[0],
        compiler_params=pltpu.CompilerParams(vmem_limit_bytes=2**20),
        cost_estimate=pl.CostEstimate(flops=0, bytes_accessed=6 * size, transcendentals=0),
    )(*bufs)


def first_kernel(early, later, n_col, n_row, ids_ref, parts_ref, sta_ref, *refs):
    sa, refs = refs[: len(early)], refs[len(early) :]
    sb, (stb_ref, sum_ref, z, straight, *scattered) = refs[: len(later)], refs[len(later) :]
    spread_vectors(parts_ref, z, n_col, n_row)
    turn_all(sb, stb_ref)
    tiles = {at: (s, sta_ref, i) for i, (at, s) in enumerate(zip(early, sa))}
    tiles.update({at: (s, stb_ref, i) for i, (at, s) in enumerate(zip(later, sb))})
    clear([straight])
    sum_ref[...] = sum_products(grouped(tiles, n_col, n_row), n_col, ids_ref, z, straight, scattered)


def filter_kernel(early, later, late, n_col, n_row, ids_ref, parts_ref, sum_ref, *refs):
    (sta_ref, stb_ref), refs = refs[:2], refs[2:]
    sa, refs = refs[: len(early)], refs[len(early) :]
    sb, refs = refs[: len(later)], refs[len(later) :]
    bufs, (out_ref, s_ref, st_ref, z, now, prev, straight, *scattered, sems) = (
        refs[: len(late)],
        refs[len(late) :],
    )
    n_blocks, share, orb = z.shape
    per_piece = n_blocks // (n_col * n_row)
    rest = sorted({(g, f) for g, f, _ in late})

    copies = []
    for i, (buf, (g, f, start)) in enumerate(zip(bufs, late)):
        target = s_ref.at[rest.index((g, f)), pl.ds(start, buf.shape[0])]
        copies.append(pltpu.make_async_copy(buf, target, sems.at[i]))
        copies[-1].start()
    spread_vectors(parts_ref, z, n_col, n_row, prev)
    for copy, buf, (g, f, start) in zip(copies, bufs, late):
        copy.wait()
        turn(s_ref, st_ref, rest.index((g, f)), start, buf.shape[0])

    tiles = {at: (s_ref.at[i], st_ref, i) for i, at in enumerate(rest)}
    clear([straight])
    total = sum_products(grouped(tiles, n_col, n_row), n_col, ids_ref, z, straight, scattered)
    total += sum_ref[...]
    now[...] = total
    z[...] = total.astype(z.dtype)

    tiles.update({at: (s, sta_ref, i) for i, (at, s) in enumerate(zip(early, sa))})
    tiles.update({at: (s, stb_ref, i) for i, (at, s) in enumerate(zip(later, sb))})
    groups = grouped(tiles, n_col, n_row)

    def one_step(step, carry):
        total = sum_products(groups, n_col, ids_ref, z, straight, scattered)
        total = 2.0 * total - prev[...]
        prev[...] = now[...]
        now[...] = total
        z[...] = total.astype(z.dtype)
        return carry

    lax.fori_loop(1, DEG, one_step, 0)
    for p in range(n_col * n_row):
        for b in range(per_piece):
            u = p * per_piece + b
            out_ref[p, 0, :, b * orb : (b + 1) * orb] = now[u].astype(out_ref.dtype)
            out_ref[p, 1, :, b * orb : (b + 1) * orb] = prev[u].astype(out_ref.dtype)


def result_kernel(back_ref, marker_ref, last_ref, before_ref):
    count, _, share, rows = back_ref.shape
    for i, out_ref in enumerate((last_ref, before_ref)):
        whole = jnp.concatenate([back_ref[d, i] for d in range(count)], axis=0)
        out_ref[...] = whole.astype(jnp.float32).T


def gather_plan(vectors, blocks, cols):
    n_dev = lax.axis_size(LANES)
    n_col, n_row = lax.axis_size("col"), lax.axis_size("row")
    rows, width = vectors.shape
    slots, orb = blocks.shape[2:4]
    share = width // n_dev
    per_piece = rows // orb
    n_blocks = n_dev * per_piece
    half = slots // 2

    def send(buf, flip_col, flip_row, from_rows=range(n_row)):
        pairs = [
            (c * n_row + r, (c ^ flip_col) * n_row + (r ^ flip_row))
            for c in range(n_col)
            for r in from_rows
        ]
        return lax.ppermute(buf, LANES, pairs)

    def to_mate(*bufs):
        return [send(buf, 1, 0) for buf in bufs]

    own = blocks[0, 0]
    near = send(own, 0, 1)
    inner = send(own, 0, 3, INNER)
    over_own = after(send(own, 2, 0), rank=1)

    own_cols = jnp.broadcast_to(jnp.pad(cols[0, 0], (0, orb - slots)), (share, orb))
    shares = jax.ShapeDtypeStruct((n_dev // 2 * per_piece + 1, share, orb), vectors.dtype)
    stay, go = pl.pallas_call(
        functools.partial(split_kernel, n_col, n_row),
        out_shape=[shares, shares],
        in_specs=vmem(2),
        out_specs=vmem(2),
        scratch_shapes=[pltpu.VMEM((n_dev, share, rows), vectors.dtype)],
        compiler_params=pltpu.CompilerParams(vmem_limit_bytes=4 * 2**20),
    )(vectors, own_cols)
    stay, go = regroup(stay, send(go, 1, 0), 1, per_piece)

    stay, go = regroup(stay, send(go, 2, 0), 2, per_piece)
    mates = to_mate(own)
    near = after(near, over_own, go, *mates)
    over_near = after(send(near, 2, 0), rank=3)
    crossed = after(send(near, 0, 3, INNER), rank=1)
    inner = after(inner, near)
    outward = after(send(inner, 0, 1, INNER), rank=1)
    stay, go = regroup(stay, send(go, 0, 1), 4, per_piece)
    mates += to_mate(near, over_own)
    two = pick(INNER, crossed, outward, over_near, go, *mates)

    over_two = send(two, 2, 0)
    outer = after(send(crossed, 0, 1, INNER), rank=1)
    mates += to_mate(two, over_near)
    mine, ids = regroup(stay, send(go, 0, 3), 8, per_piece)
    sa = [own, near, over_own, over_near, *mates[:3]]
    sta = turned_tiles(*sa)
    three = pick(INNER, inner, outer, over_two, mine, sta, *mates[3:])

    over_three = send(three[:half], 2, 0)
    side_three = send(over_two[half:], 0, 1)
    mates += to_mate(three, over_two)
    early = [(0, 0), (0, 1), (2, 0), (2, 1), (1, 0), (1, 1), (3, 0)]
    later = [(0, 2), (2, 2), (0, 3), (1, 2), (3, 1), (1, 3), (3, 2)]
    tiles_of = jax.ShapeDtypeStruct((len(later), slots, orb, orb), blocks.dtype)
    sums = jax.ShapeDtypeStruct((n_blocks, share, orb), jnp.float32)
    sb = [two, over_two, three, *mates[3:]]
    stb, total = pl.pallas_call(
        functools.partial(first_kernel, early, later, n_col, n_row),
        out_shape=[tiles_of, sums],
        in_specs=smem() + vmem(2 + len(early + later)),
        out_specs=vmem(2),
        scratch_shapes=[
            pltpu.VMEM((n_blocks, share, orb), jnp.bfloat16),
            *[pltpu.VMEM((n_blocks, share, orb), jnp.float32)] * (1 + SPLIT),
        ],
        compiler_params=pltpu.CompilerParams(vmem_limit_bytes=6 * 2**20),
        cost_estimate=pl.CostEstimate(
            flops=4 * len(early + later) * slots * orb * orb * share,
            bytes_accessed=6 * len(later) * own.size,
            transcendentals=0,
        ),
    )(ids, mine, sta, *sa, *sb)
    over_three, side_three = after(over_three, stb), after(side_three, stb)
    late = [(2, 3, 0), (2, 3, half), (3, 3, 0), (3, 3, half)]
    late_bufs = [over_three, side_three, *to_mate(over_three, side_three)]

    done = pl.pallas_call(
        functools.partial(filter_kernel, early, later, late, n_col, n_row),
        out_shape=jax.ShapeDtypeStruct((n_dev, 2, share, rows), jnp.bfloat16),
        in_specs=smem() + vmem(4 + len(early + later)) + anywhere(len(late)),
        out_specs=vmem()[0],
        scratch_shapes=[
            *[pltpu.VMEM((2, slots, orb, orb), blocks.dtype)] * 2,
            pltpu.VMEM((n_blocks, share, orb), jnp.bfloat16),
            *[pltpu.VMEM((n_blocks, share, orb), jnp.float32)] * (3 + SPLIT),
            pltpu.SemaphoreType.DMA((len(late),)),
        ],
        compiler_params=pltpu.CompilerParams(vmem_limit_bytes=12 * 2**20),
    )(ids, mine, total, sta, stb, *sa, *sb, *late_bufs)
    back = lax.all_to_all(done, LANES, split_axis=0, concat_axis=0, tiled=True)
    whole = jax.ShapeDtypeStruct((rows, width), jnp.float32)
    return pl.pallas_call(
        result_kernel,
        out_shape=[whole, whole],
        in_specs=vmem() + anywhere(),
        out_specs=vmem(2),
        compiler_params=pltpu.CompilerParams(vmem_limit_bytes=4 * 2**20),
    )(back, after(ids, done, rank=8))


def per_device(vectors, blocks, cols):
    n_dev = lax.axis_size(LANES)
    line_of_four = lax.axis_size("col") == 4 and lax.axis_size("row") == 4
    if line_of_four and n_dev * blocks.size * blocks.dtype.itemsize <= GATHER_LIMIT:
        return gather_plan(vectors, blocks, cols)
    return spread_plan(vectors, blocks, cols)


def solution(mesh):
    return jax.shard_map(
        per_device,
        mesh=mesh,
        in_specs=(
            P(("col", "row"), "dom"),
            P(("dom", "col"), "row", None, None, None),
            P(("dom", "col"), "row", None),
        ),
        out_specs=(P(("col", "row"), "dom"), P(("col", "row"), "dom")),
        check_vma=False,
    )
```

```python
import functools

import jax
import jax.numpy as jnp
from jax import lax
from jax.experimental import pallas as pl
from jax.experimental.pallas import tpu as pltpu
from jax.sharding import PartitionSpec as P

PER_ROW = 2
DEG = 4
SPLIT = 4
UNROLL = 8
GATHER_LIMIT = 12 * 2**20
LANES = ("col", "row")
INNER = (1, 2)


def onehot_sum(selected, high_part, low_part):
    first = jnp.einsum("su,sok->uok", selected, high_part, preferred_element_type=jnp.float32)
    second = jnp.einsum("su,sok->uok", selected, low_part, preferred_element_type=jnp.float32)
    return first + second


def apply_pair(send, grouped, col_ids, onehot):
    tile_rows, per_row, orb, _ = grouped.shape
    piece_rows, width = send.shape
    tile_cols = onehot.shape[1]
    wide = lax.all_gather(send, "col", axis=0, tiled=True).reshape(tile_cols, orb, width)
    picked = jnp.take(wide, col_ids, axis=0).reshape(tile_rows, per_row, orb, width)
    direct = jnp.einsum("tpio,tpok->tik", grouped, picked, preferred_element_type=jnp.float32)
    part_rows = lax.psum_scatter(
        direct.reshape(tile_rows * orb, width).astype(jnp.bfloat16),
        "row",
        scatter_dimension=0,
        tiled=True,
    ).astype(jnp.float32)
    tall = lax.all_gather(send, "row", axis=0, tiled=True).reshape(tile_rows, orb, width)
    mirrored = jnp.einsum("tpio,tik->tpok", grouped, tall, preferred_element_type=jnp.float32)
    mirrored = mirrored.reshape(tile_rows * per_row, orb, width)
    high_part = mirrored.astype(jnp.bfloat16)
    low_part = (mirrored - high_part.astype(jnp.float32)).astype(jnp.bfloat16)
    summed = onehot_sum(onehot, high_part, low_part)
    part_cols = lax.psum_scatter(
        summed.reshape(tile_cols * orb, width).astype(jnp.bfloat16),
        "col",
        scatter_dimension=0,
        tiled=True,
    ).astype(jnp.float32)
    return part_rows + part_cols


def spread_plan(vectors, blocks, cols):
    tiles = blocks[0, 0]
    col_ids = cols[0, 0]
    slots, orb, _ = tiles.shape
    tile_rows = slots // PER_ROW
    tile_cols = lax.axis_size("col") * (vectors.shape[0] // orb)
    grouped = tiles.reshape(tile_rows, PER_ROW, orb, orb)
    onehot = (col_ids[:, None] == jnp.arange(tile_cols, dtype=jnp.int32)[None, :]).astype(
        jnp.bfloat16
    )
    prev = vectors.astype(jnp.float32)
    now = apply_pair(vectors, grouped, col_ids, onehot)
    for step in range(DEG - 1):
        nxt = 2.0 * apply_pair(now.astype(jnp.bfloat16), grouped, col_ids, onehot) - prev
        prev, now = (now, nxt)
    return (now, prev)


def vmem(count=1):
    return [pl.BlockSpec(memory_space=pltpu.VMEM)] * count


def smem(count=1):
    return [pl.BlockSpec(memory_space=pltpu.SMEM)] * count


def anywhere(count=1):
    return [pl.BlockSpec(memory_space=pl.ANY)] * count


def nothing(*refs):
    pass


def after(value, *others, rank=0):
    return pl.pallas_call(
        nothing,
        out_shape=jax.ShapeDtypeStruct(value.shape, value.dtype),
        in_specs=anywhere(1 + len(others)),
        out_specs=anywhere()[0],
        input_output_aliases={0: 0},
        compiler_params=pltpu.CompilerParams(vmem_limit_bytes=2**20),
        cost_estimate=pl.CostEstimate(flops=0, bytes_accessed=rank * 2**23, transcendentals=0),
    )(value, *others)


def pick_kernel(rows, one_ref, other_ref, *refs):
    out_ref, sem = refs[-2:]
    row = lax.axis_index("row")
    first = (row == rows[0]) | (row == rows[1])

    @pl.when(first)
    def _():
        copy = pltpu.make_async_copy(one_ref, out_ref, sem)
        copy.start()
        copy.wait()

    @pl.when(jnp.logical_not(first))
    def _():
        copy = pltpu.make_async_copy(other_ref, out_ref, sem)
        copy.start()
        copy.wait()


def pick(rows, one, other, *others):
    return pl.pallas_call(
        functools.partial(pick_kernel, rows),
        out_shape=jax.ShapeDtypeStruct(one.shape, one.dtype),
        in_specs=anywhere(2 + len(others)),
        out_specs=anywhere()[0],
        scratch_shapes=[pltpu.SemaphoreType.DMA(())],
        compiler_params=pltpu.CompilerParams(vmem_limit_bytes=2**20),
    )(one, other, *others)


def split_kernel(n_col, n_row, vectors_ref, cols_ref, stay_ref, go_ref, turned):
    col, row = lax.axis_index("col"), lax.axis_index("row")
    count, share, rows = turned.shape
    orb = stay_ref.shape[2]
    per_piece = rows // orb
    whole = vectors_ref[...].T
    for d in range(count):
        turned[d] = whole[d * share : (d + 1) * share]
    orders = [(y, one, three) for y in range(2) for one in range(2) for three in range(2)]
    ids = cols_ref[...]
    piece = jnp.zeros_like(ids)
    for c in range(1, n_col):
        piece += (ids >= c * per_piece).astype(jnp.int32)
    ids = ids - piece * per_piece + (piece * n_row + row) * per_piece
    for core, out_ref in enumerate((stay_ref, go_ref)):
        for k, (y, one, three) in enumerate(orders):
            peer = (col ^ (core + 2 * y)) * n_row + (row ^ one ^ 3 * three)
            for b in range(per_piece):
                out_ref[k * per_piece + b] = turned[peer, :, b * orb : (b + 1) * orb]
        out_ref[len(orders) * per_piece] = ids.astype(jnp.float32).astype(out_ref.dtype)


def regroup_kernel(sources, count, stay_ref, came_ref, *outs):
    per_piece = (stay_ref.shape[0] - sources) // (sources * count)
    kept = max(count // 2, 1)
    for h, out_ref in enumerate(outs):
        for s in range(2 * sources):
            ref = stay_ref if s < sources else came_ref
            ids = ref[sources * count * per_piece + s % sources]
            if h == 1 and count == 1:
                out_ref[s : s + 1] = ids.astype(jnp.float32)[:1].astype(jnp.int32)
                continue
            for k in range(kept * per_piece):
                out_ref[s * kept * per_piece + k] = ref[(s % sources * count + h * kept) * per_piece + k]
            if count > 1:
                out_ref[2 * sources * kept * per_piece + s] = ids


def regroup(stay, came, sources, per_piece):
    count = (stay.shape[0] // sources - 1) // per_piece
    _, share, orb = stay.shape
    if count > 1:
        out = jax.ShapeDtypeStruct((sources * count * per_piece + 2 * sources, share, orb), stay.dtype)
        outs = [out, out]
    else:
        outs = [
            jax.ShapeDtypeStruct((2 * sources * per_piece, share, orb), stay.dtype),
            jax.ShapeDtypeStruct((2 * sources, orb), jnp.int32),
        ]
    return pl.pallas_call(
        functools.partial(regroup_kernel, sources, count),
        out_shape=outs,
        in_specs=vmem(2),
        out_specs=vmem(2),
        compiler_params=pltpu.CompilerParams(vmem_limit_bytes=2**20),
    )(stay, came)


def place(g, f):
    return (f >> 1) * 8 + ((f & 1) ^ (f >> 1)) * 4 + g


def multiply(t, groups, across, ids_ref, z, straight, scattered):
    tile_rows = z.shape[0] // len(groups)
    orb = z.shape[2]
    for g, group in enumerate(groups):
        if not group:
            continue
        here = across[g] * tile_rows + t
        places = [(tile, t * PER_ROW + p) for tile in group for p in range(PER_ROW)]
        strip = jnp.concatenate([s[slot] for (_, s, _, _), slot in places], axis=1)
        turned = jnp.concatenate([st[i, slot] for (_, _, st, i), slot in places], axis=0)
        where = [ids_ref[place(g, f), slot] for (f, *_), slot in places]
        wide = jnp.concatenate([z[u] for u in where], axis=1)
        straight[here] = jnp.dot(wide, turned, preferred_element_type=jnp.float32)
        mirrored = jnp.dot(z[here], strip, preferred_element_type=jnp.float32)
        for i, u in enumerate(where):
            scattered[i % len(scattered)][u] += mirrored[:, i * orb : (i + 1) * orb]


def clear(refs):
    for ref in refs:
        ref[...] = jnp.zeros_like(ref)


def turn(s_ref, st_ref, i, start, count):
    def four(k, carry):
        for m in range(4):
            st_ref[i, start + 4 * k + m] = s_ref[i, start + 4 * k + m].T
        return carry

    lax.fori_loop(0, count // 4, four, 0)


def turn_all(bufs, st_ref):
    def four(k, carry):
        for i, buf in enumerate(bufs):
            for m in range(4):
                st_ref[i, 4 * k + m] = buf[4 * k + m].T
        return carry

    lax.fori_loop(0, st_ref.shape[1] // 4, four, 0)


def grouped(tiles, n_col, n_row):
    return [[(f, *tiles[g, f]) for f in range(n_row) if (g, f) in tiles] for g in range(n_col)]


def spread_vectors(parts_ref, z, n_col, n_row, now=None):
    per_piece = z.shape[0] // (n_col * n_row)
    across = [lax.axis_index("col") ^ g for g in range(n_col)]
    down = [lax.axis_index("row") ^ f for f in range(n_row)]
    for g in range(n_col):
        for f in range(n_row):
            for b in range(per_piece):
                u = (across[g] * n_row + down[f]) * per_piece + b
                own = parts_ref[place(g, f) * per_piece + b]
                z[u] = own
                if now is not None:
                    now[u] = own.astype(jnp.float32)


def sum_products(groups, n_col, ids_ref, z, straight, scattered):
    across = [lax.axis_index("col") ^ g for g in range(n_col)]
    clear(scattered)

    def block_rows(k, carry):
        for t in range(UNROLL):
            multiply(k * UNROLL + t, groups, across, ids_ref, z, straight, scattered)
        return carry

    lax.fori_loop(0, z.shape[0] // n_col // UNROLL, block_rows, 0)
    total = straight[...]
    for ref in scattered:
        total += ref[...]
    return total


def turned_kernel(*refs):
    turn_all(refs[:-1], refs[-1])


def turned_tiles(*bufs):
    size = len(bufs) * bufs[0].size
    return pl.pallas_call(
        turned_kernel,
        out_shape=jax.ShapeDtypeStruct((len(bufs), *bufs[0].shape), bufs[0].dtype),
        in_specs=vmem(len(bufs)),
        out_specs=vmem()[0],
        compiler_params=pltpu.CompilerParams(vmem_limit_bytes=2**20),
        cost_estimate=pl.CostEstimate(flops=0, bytes_accessed=6 * size, transcendentals=0),
    )(*bufs)


def first_kernel(early, later, n_col, n_row, ids_ref, parts_ref, sta_ref, *refs):
    sa, refs = refs[: len(early)], refs[len(early) :]
    sb, (stb_ref, sum_ref, z, straight, *scattered) = refs[: len(later)], refs[len(later) :]
    spread_vectors(parts_ref, z, n_col, n_row)
    turn_all(sb, stb_ref)
    tiles = {at: (s, sta_ref, i) for i, (at, s) in enumerate(zip(early, sa))}
    tiles.update({at: (s, stb_ref, i) for i, (at, s) in enumerate(zip(later, sb))})
    clear([straight])
    sum_ref[...] = sum_products(grouped(tiles, n_col, n_row), n_col, ids_ref, z, straight, scattered)


def filter_kernel(early, later, late, n_col, n_row, ids_ref, parts_ref, sum_ref, *refs):
    (sta_ref, stb_ref), refs = refs[:2], refs[2:]
    sa, refs = refs[: len(early)], refs[len(early) :]
    sb, refs = refs[: len(later)], refs[len(later) :]
    bufs, (out_ref, s_ref, st_ref, z, now, prev, straight, *scattered, sems) = (
        refs[: len(late)],
        refs[len(late) :],
    )
    n_blocks, share, orb = z.shape
    per_piece = n_blocks // (n_col * n_row)
    rest = sorted({(g, f) for g, f, _ in late})

    copies = []
    for i, (buf, (g, f, start)) in enumerate(zip(bufs, late)):
        target = s_ref.at[rest.index((g, f)), pl.ds(start, buf.shape[0])]
        copies.append(pltpu.make_async_copy(buf, target, sems.at[i]))
        copies[-1].start()
    spread_vectors(parts_ref, z, n_col, n_row, prev)
    for copy, buf, (g, f, start) in zip(copies, bufs, late):
        copy.wait()
        turn(s_ref, st_ref, rest.index((g, f)), start, buf.shape[0])

    tiles = {at: (s_ref.at[i], st_ref, i) for i, at in enumerate(rest)}
    clear([straight])
    total = sum_products(grouped(tiles, n_col, n_row), n_col, ids_ref, z, straight, scattered)
    total += sum_ref[...]
    now[...] = total
    z[...] = total.astype(z.dtype)

    tiles.update({at: (s, sta_ref, i) for i, (at, s) in enumerate(zip(early, sa))})
    tiles.update({at: (s, stb_ref, i) for i, (at, s) in enumerate(zip(later, sb))})
    groups = grouped(tiles, n_col, n_row)

    def one_step(step, carry):
        total = sum_products(groups, n_col, ids_ref, z, straight, scattered)
        total = 2.0 * total - prev[...]
        prev[...] = now[...]
        now[...] = total
        z[...] = total.astype(z.dtype)
        return carry

    lax.fori_loop(1, DEG, one_step, 0)
    for p in range(n_col * n_row):
        for b in range(per_piece):
            u = p * per_piece + b
            out_ref[p, 0, :, b * orb : (b + 1) * orb] = now[u].astype(out_ref.dtype)
            out_ref[p, 1, :, b * orb : (b + 1) * orb] = prev[u].astype(out_ref.dtype)


def result_kernel(back_ref, marker_ref, last_ref, before_ref):
    count, _, share, rows = back_ref.shape
    for i, out_ref in enumerate((last_ref, before_ref)):
        whole = jnp.concatenate([back_ref[d, i] for d in range(count)], axis=0)
        out_ref[...] = whole.astype(jnp.float32).T


def gather_plan(vectors, blocks, cols):
    n_dev = lax.axis_size(LANES)
    n_col, n_row = lax.axis_size("col"), lax.axis_size("row")
    rows, width = vectors.shape
    slots, orb = blocks.shape[2:4]
    share = width // n_dev
    per_piece = rows // orb
    n_blocks = n_dev * per_piece
    half = slots // 2

    def send(buf, flip_col, flip_row, from_rows=range(n_row)):
        pairs = [
            (c * n_row + r, (c ^ flip_col) * n_row + (r ^ flip_row))
            for c in range(n_col)
            for r in from_rows
        ]
        return lax.ppermute(buf, LANES, pairs)

    def to_mate(*bufs):
        return [send(buf, 1, 0) for buf in bufs]

    own = blocks[0, 0]
    near = send(own, 0, 1)
    inner = send(own, 0, 3, INNER)
    over_own = after(send(own, 2, 0), rank=1)

    own_cols = jnp.broadcast_to(jnp.pad(cols[0, 0], (0, orb - slots)), (share, orb))
    shares = jax.ShapeDtypeStruct((n_dev // 2 * per_piece + 1, share, orb), vectors.dtype)
    stay, go = pl.pallas_call(
        functools.partial(split_kernel, n_col, n_row),
        out_shape=[shares, shares],
        in_specs=vmem(2),
        out_specs=vmem(2),
        scratch_shapes=[pltpu.VMEM((n_dev, share, rows), vectors.dtype)],
        compiler_params=pltpu.CompilerParams(vmem_limit_bytes=4 * 2**20),
    )(vectors, own_cols)
    stay, go = regroup(stay, send(go, 1, 0), 1, per_piece)

    stay, go = regroup(stay, send(go, 2, 0), 2, per_piece)
    mates = to_mate(own)
    near = after(near, over_own, go, inner, *mates)
    over_near = after(send(near, 2, 0), rank=8)
    crossed = after(send(near, 0, 3, INNER), rank=1)
    inner = after(inner, near)
    outward = after(send(inner, 0, 1, INNER), rank=8)
    stay, go = regroup(stay, send(after(go, near), 0, 1), 4, per_piece)
    mates += to_mate(near, over_own)
    two = pick(INNER, crossed, outward, over_near, *mates)

    over_two = send(two, 2, 0)
    outer = after(send(crossed, 0, 1, INNER), rank=1)
    mates += to_mate(two, over_near)
    mine, ids = regroup(stay, send(go, 0, 3), 8, per_piece)
    sa = [own, near, over_own, over_near, *mates[:3]]
    sta = turned_tiles(*sa)
    three = pick(INNER, inner, outer, over_two, mine, *mates[3:])

    over_three = send(three[:half], 2, 0)
    side_three = send(over_two[half:], 0, 1)
    mates += to_mate(three, over_two)
    early = [(0, 0), (0, 1), (2, 0), (2, 1), (1, 0), (1, 1), (3, 0)]
    later = [(0, 2), (2, 2), (0, 3), (1, 2), (3, 1), (1, 3), (3, 2)]
    tiles_of = jax.ShapeDtypeStruct((len(later), slots, orb, orb), blocks.dtype)
    sums = jax.ShapeDtypeStruct((n_blocks, share, orb), jnp.float32)
    sb = [two, over_two, three, *mates[3:]]
    stb, total = pl.pallas_call(
        functools.partial(first_kernel, early, later, n_col, n_row),
        out_shape=[tiles_of, sums],
        in_specs=smem() + vmem(2 + len(early + later)),
        out_specs=vmem(2),
        scratch_shapes=[
            pltpu.VMEM((n_blocks, share, orb), jnp.bfloat16),
            *[pltpu.VMEM((n_blocks, share, orb), jnp.float32)] * (1 + SPLIT),
        ],
        compiler_params=pltpu.CompilerParams(vmem_limit_bytes=6 * 2**20),
        cost_estimate=pl.CostEstimate(
            flops=4 * len(early + later) * slots * orb * orb * share,
            bytes_accessed=6 * len(later) * own.size,
            transcendentals=0,
        ),
    )(ids, mine, sta, *sa, *sb)
    over_three, side_three = after(over_three, stb), after(side_three, stb)
    late = [(2, 3, 0), (2, 3, half), (3, 3, 0), (3, 3, half)]
    late_bufs = [over_three, side_three, *to_mate(over_three, side_three)]

    done = pl.pallas_call(
        functools.partial(filter_kernel, early, later, late, n_col, n_row),
        out_shape=jax.ShapeDtypeStruct((n_dev, 2, share, rows), jnp.bfloat16),
        in_specs=smem() + vmem(4 + len(early + later)) + anywhere(len(late)),
        out_specs=vmem()[0],
        scratch_shapes=[
            *[pltpu.VMEM((2, slots, orb, orb), blocks.dtype)] * 2,
            pltpu.VMEM((n_blocks, share, orb), jnp.bfloat16),
            *[pltpu.VMEM((n_blocks, share, orb), jnp.float32)] * (3 + SPLIT),
            pltpu.SemaphoreType.DMA((len(late),)),
        ],
        compiler_params=pltpu.CompilerParams(vmem_limit_bytes=12 * 2**20),
    )(ids, mine, total, sta, stb, *sa, *sb, *late_bufs)
    back = lax.all_to_all(done, LANES, split_axis=0, concat_axis=0, tiled=True)
    whole = jax.ShapeDtypeStruct((rows, width), jnp.float32)
    return pl.pallas_call(
        result_kernel,
        out_shape=[whole, whole],
        in_specs=vmem() + anywhere(),
        out_specs=vmem(2),
        compiler_params=pltpu.CompilerParams(vmem_limit_bytes=4 * 2**20),
    )(back, after(ids, done, rank=8))


def per_device(vectors, blocks, cols):
    n_dev = lax.axis_size(LANES)
    line_of_four = lax.axis_size("col") == 4 and lax.axis_size("row") == 4
    if line_of_four and n_dev * blocks.size * blocks.dtype.itemsize <= GATHER_LIMIT:
        return gather_plan(vectors, blocks, cols)
    return spread_plan(vectors, blocks, cols)


def solution(mesh):
    return jax.shard_map(
        per_device,
        mesh=mesh,
        in_specs=(
            P(("col", "row"), "dom"),
            P(("dom", "col"), "row", None, None, None),
            P(("dom", "col"), "row", None),
        ),
        out_specs=(P(("col", "row"), "dom"), P(("col", "row"), "dom")),
        check_vma=False,
    )
```

```python
import functools

import jax
import jax.numpy as jnp
from jax import lax
from jax.experimental import pallas as pl
from jax.experimental.pallas import tpu as pltpu
from jax.sharding import PartitionSpec as P

PER_ROW = 2
DEG = 4
SPLIT = 4
GATHER_LIMIT = 12 * 2**20
LANES = ("col", "row")
INNER = (1, 2)


def onehot_sum(selected, high_part, low_part):
    first = jnp.einsum("su,sok->uok", selected, high_part, preferred_element_type=jnp.float32)
    second = jnp.einsum("su,sok->uok", selected, low_part, preferred_element_type=jnp.float32)
    return first + second


def apply_pair(send, grouped, col_ids, onehot):
    tile_rows, per_row, orb, _ = grouped.shape
    piece_rows, width = send.shape
    tile_cols = onehot.shape[1]
    wide = lax.all_gather(send, "col", axis=0, tiled=True).reshape(tile_cols, orb, width)
    picked = jnp.take(wide, col_ids, axis=0).reshape(tile_rows, per_row, orb, width)
    direct = jnp.einsum("tpio,tpok->tik", grouped, picked, preferred_element_type=jnp.float32)
    part_rows = lax.psum_scatter(
        direct.reshape(tile_rows * orb, width).astype(jnp.bfloat16),
        "row",
        scatter_dimension=0,
        tiled=True,
    ).astype(jnp.float32)
    tall = lax.all_gather(send, "row", axis=0, tiled=True).reshape(tile_rows, orb, width)
    mirrored = jnp.einsum("tpio,tik->tpok", grouped, tall, preferred_element_type=jnp.float32)
    mirrored = mirrored.reshape(tile_rows * per_row, orb, width)
    high_part = mirrored.astype(jnp.bfloat16)
    low_part = (mirrored - high_part.astype(jnp.float32)).astype(jnp.bfloat16)
    summed = onehot_sum(onehot, high_part, low_part)
    part_cols = lax.psum_scatter(
        summed.reshape(tile_cols * orb, width).astype(jnp.bfloat16),
        "col",
        scatter_dimension=0,
        tiled=True,
    ).astype(jnp.float32)
    return part_rows + part_cols


def spread_plan(vectors, blocks, cols):
    tiles = blocks[0, 0]
    col_ids = cols[0, 0]
    slots, orb, _ = tiles.shape
    tile_rows = slots // PER_ROW
    tile_cols = lax.axis_size("col") * (vectors.shape[0] // orb)
    grouped = tiles.reshape(tile_rows, PER_ROW, orb, orb)
    onehot = (col_ids[:, None] == jnp.arange(tile_cols, dtype=jnp.int32)[None, :]).astype(
        jnp.bfloat16
    )
    prev = vectors.astype(jnp.float32)
    now = apply_pair(vectors, grouped, col_ids, onehot)
    for step in range(DEG - 1):
        nxt = 2.0 * apply_pair(now.astype(jnp.bfloat16), grouped, col_ids, onehot) - prev
        prev, now = (now, nxt)
    return (now, prev)


def vmem(count=1):
    return [pl.BlockSpec(memory_space=pltpu.VMEM)] * count


def smem(count=1):
    return [pl.BlockSpec(memory_space=pltpu.SMEM)] * count


def anywhere(count=1):
    return [pl.BlockSpec(memory_space=pl.ANY)] * count


def nothing(*refs):
    pass


def after(value, *others, rank=0):
    return pl.pallas_call(
        nothing,
        out_shape=jax.ShapeDtypeStruct(value.shape, value.dtype),
        in_specs=anywhere(1 + len(others)),
        out_specs=anywhere()[0],
        input_output_aliases={0: 0},
        compiler_params=pltpu.CompilerParams(vmem_limit_bytes=2**20),
        cost_estimate=pl.CostEstimate(flops=0, bytes_accessed=rank * 2**23, transcendentals=0),
    )(value, *others)


def pick_kernel(rows, one_ref, other_ref, *refs):
    out_ref, sem = refs[-2:]
    row = lax.axis_index("row")
    first = (row == rows[0]) | (row == rows[1])

    @pl.when(first)
    def _():
        copy = pltpu.make_async_copy(one_ref, out_ref, sem)
        copy.start()
        copy.wait()

    @pl.when(jnp.logical_not(first))
    def _():
        copy = pltpu.make_async_copy(other_ref, out_ref, sem)
        copy.start()
        copy.wait()


def pick(rows, one, other, *others):
    return pl.pallas_call(
        functools.partial(pick_kernel, rows),
        out_shape=jax.ShapeDtypeStruct(one.shape, one.dtype),
        in_specs=anywhere(2 + len(others)),
        out_specs=anywhere()[0],
        scratch_shapes=[pltpu.SemaphoreType.DMA(())],
        compiler_params=pltpu.CompilerParams(vmem_limit_bytes=2**20),
    )(one, other, *others)


def split_kernel(n_col, n_row, vectors_ref, cols_ref, stay_ref, go_ref, turned):
    col, row = lax.axis_index("col"), lax.axis_index("row")
    count, share, rows = turned.shape
    orb = stay_ref.shape[2]
    per_piece = rows // orb
    whole = vectors_ref[...].T
    for d in range(count):
        turned[d] = whole[d * share : (d + 1) * share]
    orders = [(y, one, three) for y in range(2) for one in range(2) for three in range(2)]
    ids = cols_ref[...]
    piece = jnp.zeros_like(ids)
    for c in range(1, n_col):
        piece += (ids >= c * per_piece).astype(jnp.int32)
    ids = ids - piece * per_piece + (piece * n_row + row) * per_piece
    for core, out_ref in enumerate((stay_ref, go_ref)):
        for k, (y, one, three) in enumerate(orders):
            peer = (col ^ (core + 2 * y)) * n_row + (row ^ one ^ 3 * three)
            for b in range(per_piece):
                out_ref[k * per_piece + b] = turned[peer, :, b * orb : (b + 1) * orb]
        out_ref[len(orders) * per_piece] = ids.astype(jnp.float32).astype(out_ref.dtype)


def regroup_kernel(sources, count, stay_ref, came_ref, *outs):
    per_piece = (stay_ref.shape[0] - 1) // (sources * count)
    kept = max(count // 2, 1)
    ids = stay_ref[sources * count * per_piece].astype(jnp.float32)
    came = came_ref[sources * count * per_piece].astype(jnp.float32)
    line = lax.broadcasted_iota(jnp.int32, ids.shape, 0)
    ids = jnp.where(line < sources, ids, pltpu.roll(came, sources, 0))
    for h, out_ref in enumerate(outs):
        if h == 1 and count == 1:
            out_ref[...] = ids.astype(jnp.int32)
            continue
        for s in range(2 * sources):
            ref = stay_ref if s < sources else came_ref
            for k in range(kept * per_piece):
                out_ref[s * kept * per_piece + k] = ref[(s % sources * count + h * kept) * per_piece + k]
        if count > 1:
            out_ref[2 * sources * kept * per_piece] = ids.astype(out_ref.dtype)


def regroup(stay, came, sources, per_piece):
    count = (stay.shape[0] - 1) // (sources * per_piece)
    _, share, orb = stay.shape
    if count > 1:
        outs = [jax.ShapeDtypeStruct(stay.shape, stay.dtype)] * 2
    else:
        outs = [
            jax.ShapeDtypeStruct((2 * sources * per_piece, share, orb), stay.dtype),
            jax.ShapeDtypeStruct((share, orb), jnp.int32),
        ]
    return pl.pallas_call(
        functools.partial(regroup_kernel, sources, count),
        out_shape=outs,
        in_specs=vmem(2),
        out_specs=vmem(2),
        compiler_params=pltpu.CompilerParams(vmem_limit_bytes=2**20),
    )(stay, came)


def place(g, f):
    return (f >> 1) * 8 + ((f & 1) ^ (f >> 1)) * 4 + g


def multiply(t, groups, across, ids_ref, z, straight, scattered):
    tile_rows = z.shape[0] // len(groups)
    orb = z.shape[2]
    for g, group in enumerate(groups):
        if not group:
            continue
        here = across[g] * tile_rows + t
        places = [(tile, t * PER_ROW + p) for tile in group for p in range(PER_ROW)]
        strip = jnp.concatenate([s[slot][...] for (_, s, _, _), slot in places], axis=1)
        turned = jnp.concatenate([st[i, slot] for (_, _, st, i), slot in places], axis=0)
        where = [ids_ref[place(g, f), slot] for (f, *_), slot in places]
        wide = jnp.concatenate([z[u] for u in where], axis=1)
        straight[here] = jnp.dot(wide, turned, preferred_element_type=jnp.float32)
        mirrored = jnp.dot(z[here], strip, preferred_element_type=jnp.float32)
        for i, u in enumerate(where):
            scattered[i % len(scattered)][u] += mirrored[:, i * orb : (i + 1) * orb]


def clear(refs):
    for ref in refs:
        ref[...] = jnp.zeros_like(ref)


def turn_all(bufs, st_ref):
    def four(k, carry):
        for i, buf in enumerate(bufs):
            for m in range(4):
                st_ref[i, 4 * k + m] = buf[4 * k + m].T
        return carry

    lax.fori_loop(0, st_ref.shape[1] // 4, four, 0)


def grouped(tiles, n_col, n_row):
    return [[(f, *tiles[g, f]) for f in range(n_row) if (g, f) in tiles] for g in range(n_col)]


def spread_vectors(parts_ref, z, n_col, n_row, now=None):
    per_piece = z.shape[0] // (n_col * n_row)
    across = [lax.axis_index("col") ^ g for g in range(n_col)]
    down = [lax.axis_index("row") ^ f for f in range(n_row)]
    for g in range(n_col):
        for f in range(n_row):
            for b in range(per_piece):
                u = (across[g] * n_row + down[f]) * per_piece + b
                own = parts_ref[place(g, f) * per_piece + b]
                z[u] = own
                if now is not None:
                    now[u] = own.astype(jnp.float32)


def sum_products(groups, n_col, ids_ref, z, straight, scattered):
    across = [lax.axis_index("col") ^ g for g in range(n_col)]
    clear(scattered)

    for t in range(z.shape[0] // n_col):
        multiply(t, groups, across, ids_ref, z, straight, scattered)
    total = straight[...]
    for ref in scattered:
        total += ref[...]
    return total


def turned_kernel(*refs):
    turn_all(refs[:-1], refs[-1])


def turned_tiles(*bufs):
    size = len(bufs) * bufs[0].size
    return pl.pallas_call(
        turned_kernel,
        out_shape=jax.ShapeDtypeStruct((len(bufs), *bufs[0].shape), bufs[0].dtype),
        in_specs=vmem(len(bufs)),
        out_specs=vmem()[0],
        compiler_params=pltpu.CompilerParams(vmem_limit_bytes=2**20),
        cost_estimate=pl.CostEstimate(flops=0, bytes_accessed=6 * size, transcendentals=0),
    )(*bufs)


def first_kernel(early, later, n_col, n_row, ids_ref, parts_ref, sta_ref, *refs):
    sa, refs = refs[: len(early)], refs[len(early) :]
    sb, (stb_ref, sum_ref, z, straight, *scattered) = refs[: len(later)], refs[len(later) :]
    spread_vectors(parts_ref, z, n_col, n_row)
    turn_all(sb, stb_ref)
    tiles = {at: (s, sta_ref, i) for i, (at, s) in enumerate(zip(early, sa))}
    tiles.update({at: (s, stb_ref, i) for i, (at, s) in enumerate(zip(later, sb))})
    clear([straight])
    sum_ref[...] = sum_products(grouped(tiles, n_col, n_row), n_col, ids_ref, z, straight, scattered)


def filter_kernel(early, later, late, n_col, n_row, ids_ref, parts_ref, sum_ref, *refs):
    (sta_ref, stb_ref), refs = refs[:2], refs[2:]
    sa, refs = refs[: len(early)], refs[len(early) :]
    sb, refs = refs[: len(later)], refs[len(later) :]
    bufs, (out_ref, st_ref, z, now, prev, straight, *scattered) = refs[: len(late)], refs[len(late) :]
    n_blocks, share, orb = z.shape
    per_piece = n_blocks // (n_col * n_row)
    rest = sorted({(g, f) for g, f, _ in late})
    spread_vectors(parts_ref, z, n_col, n_row, prev)
    slots = {at: {} for at in rest}
    for buf, (g, f, start) in zip(bufs, late):
        for k in range(buf.shape[0]):
            slots[g, f][start + k] = buf.at[k]
    for i, at in enumerate(rest):
        for slot, block in slots[at].items():
            st_ref[i, slot] = block[...].T

    tiles = {at: (slots[at], st_ref, i) for i, at in enumerate(rest)}
    clear([straight])
    total = sum_products(grouped(tiles, n_col, n_row), n_col, ids_ref, z, straight, scattered)
    total += sum_ref[...]
    now[...] = total
    z[...] = total.astype(z.dtype)

    tiles.update({at: (s, sta_ref, i) for i, (at, s) in enumerate(zip(early, sa))})
    tiles.update({at: (s, stb_ref, i) for i, (at, s) in enumerate(zip(later, sb))})
    groups = grouped(tiles, n_col, n_row)

    def one_step(step, carry):
        total = sum_products(groups, n_col, ids_ref, z, straight, scattered)
        total = 2.0 * total - prev[...]
        prev[...] = now[...]
        now[...] = total
        z[...] = total.astype(z.dtype)
        return carry

    lax.fori_loop(1, DEG, one_step, 0)
    for p in range(n_col * n_row):
        for b in range(per_piece):
            u = p * per_piece + b
            out_ref[p, 0, :, b * orb : (b + 1) * orb] = now[u].astype(out_ref.dtype)
            out_ref[p, 1, :, b * orb : (b + 1) * orb] = prev[u].astype(out_ref.dtype)


def result_kernel(back_ref, marker_ref, last_ref, before_ref):
    count, _, share, rows = back_ref.shape
    for i, out_ref in enumerate((last_ref, before_ref)):
        whole = jnp.concatenate([back_ref[d, i] for d in range(count)], axis=0)
        out_ref[...] = whole.astype(jnp.float32).T


def gather_plan(vectors, blocks, cols):
    n_dev = lax.axis_size(LANES)
    n_col, n_row = lax.axis_size("col"), lax.axis_size("row")
    rows, width = vectors.shape
    slots, orb = blocks.shape[2:4]
    share = width // n_dev
    per_piece = rows // orb
    n_blocks = n_dev * per_piece
    half = slots // 2

    def send(buf, flip_col, flip_row, from_rows=range(n_row)):
        pairs = [
            (c * n_row + r, (c ^ flip_col) * n_row + (r ^ flip_row))
            for c in range(n_col)
            for r in from_rows
        ]
        return lax.ppermute(buf, LANES, pairs)

    def to_mate(*bufs):
        return [send(buf, 1, 0) for buf in bufs]

    own = blocks[0, 0]
    near = send(own, 0, 1)
    inner = send(own, 0, 3, INNER)
    over_own = after(send(own, 2, 0), rank=1)

    own_cols = jnp.broadcast_to(jnp.pad(cols[0, 0], (0, orb - slots)), (share, orb))
    shares = jax.ShapeDtypeStruct((n_dev // 2 * per_piece + 1, share, orb), vectors.dtype)
    stay, go = pl.pallas_call(
        functools.partial(split_kernel, n_col, n_row),
        out_shape=[shares, shares],
        in_specs=vmem(2),
        out_specs=vmem(2),
        scratch_shapes=[pltpu.VMEM((n_dev, share, rows), vectors.dtype)],
        compiler_params=pltpu.CompilerParams(vmem_limit_bytes=4 * 2**20),
    )(vectors, own_cols)
    stay, go = regroup(stay, send(go, 1, 0), 1, per_piece)

    stay, go = regroup(stay, send(go, 2, 0), 2, per_piece)
    mates = to_mate(own)
    near = after(near, over_own, go, *mates)
    over_near = after(send(near, 2, 0), rank=3)
    crossed = after(send(near, 0, 3, INNER), rank=1)
    inner = after(inner, near)
    outward = after(send(inner, 0, 1, INNER), rank=1)
    stay, go = regroup(stay, send(go, 0, 1), 4, per_piece)
    mates += to_mate(near, over_own)
    two = pick(INNER, crossed, outward, over_near, go, *mates)

    over_two = send(two, 2, 0)
    outer = after(send(crossed, 0, 1, INNER), rank=1)
    mates += to_mate(two, over_near)
    mine, ids = regroup(stay, send(go, 0, 3), 8, per_piece)
    sa = [own, near, over_own, over_near, *mates[:3]]
    sta = turned_tiles(*sa)
    three = pick(INNER, inner, outer, over_two, mine, sta, *mates[3:])

    over_three = send(three[:half], 2, 0)
    side_three = send(over_two[half:], 0, 1)
    mates += to_mate(three, over_two)
    early = [(0, 0), (0, 1), (2, 0), (2, 1), (1, 0), (1, 1), (3, 0)]
    later = [(0, 2), (2, 2), (0, 3), (1, 2), (3, 1), (1, 3), (3, 2)]
    tiles_of = jax.ShapeDtypeStruct((len(later), slots, orb, orb), blocks.dtype)
    sums = jax.ShapeDtypeStruct((n_blocks, share, orb), jnp.float32)
    sb = [two, over_two, three, *mates[3:]]
    stb, total = pl.pallas_call(
        functools.partial(first_kernel, early, later, n_col, n_row),
        out_shape=[tiles_of, sums],
        in_specs=smem() + vmem(2 + len(early + later)),
        out_specs=vmem(2),
        scratch_shapes=[
            pltpu.VMEM((n_blocks, share, orb), jnp.bfloat16),
            *[pltpu.VMEM((n_blocks, share, orb), jnp.float32)] * (1 + SPLIT),
        ],
        compiler_params=pltpu.CompilerParams(vmem_limit_bytes=6 * 2**20),
        cost_estimate=pl.CostEstimate(
            flops=4 * len(early + later) * slots * orb * orb * share,
            bytes_accessed=6 * len(later) * own.size,
            transcendentals=0,
        ),
    )(ids, mine, sta, *sa, *sb)
    over_three, side_three = after(over_three, stb), after(side_three, stb)
    late = [(2, 3, 0), (2, 3, half), (3, 3, 0), (3, 3, half)]
    late_bufs = [over_three, side_three, *to_mate(over_three, side_three)]

    done = pl.pallas_call(
        functools.partial(filter_kernel, early, later, late, n_col, n_row),
        out_shape=jax.ShapeDtypeStruct((n_dev, 2, share, rows), jnp.bfloat16),
        in_specs=smem() + vmem(4 + len(early + later + late)),
        out_specs=vmem()[0],
        scratch_shapes=[
            pltpu.VMEM((2, slots, orb, orb), blocks.dtype),
            pltpu.VMEM((n_blocks, share, orb), jnp.bfloat16),
            *[pltpu.VMEM((n_blocks, share, orb), jnp.float32)] * (3 + SPLIT),
        ],
        compiler_params=pltpu.CompilerParams(vmem_limit_bytes=12 * 2**20),
    )(ids, mine, total, sta, stb, *sa, *sb, *late_bufs)
    back = lax.all_to_all(done, LANES, split_axis=0, concat_axis=0, tiled=True)
    whole = jax.ShapeDtypeStruct((rows, width), jnp.float32)
    return pl.pallas_call(
        result_kernel,
        out_shape=[whole, whole],
        in_specs=vmem() + anywhere(),
        out_specs=vmem(2),
        compiler_params=pltpu.CompilerParams(vmem_limit_bytes=4 * 2**20),
    )(back, after(ids, done, rank=8))


def per_device(vectors, blocks, cols):
    n_dev = lax.axis_size(LANES)
    line_of_four = lax.axis_size("col") == 4 and lax.axis_size("row") == 4
    line_of_four = line_of_four and vectors.shape[1] // n_dev == n_dev
    if line_of_four and n_dev * blocks.size * blocks.dtype.itemsize <= GATHER_LIMIT:
        return gather_plan(vectors, blocks, cols)
    return spread_plan(vectors, blocks, cols)


def solution(mesh):
    return jax.shard_map(
        per_device,
        mesh=mesh,
        in_specs=(
            P(("col", "row"), "dom"),
            P(("dom", "col"), "row", None, None, None),
            P(("dom", "col"), "row", None),
        ),
        out_specs=(P(("col", "row"), "dom"), P(("col", "row"), "dom")),
        check_vma=False,
    )
```

```python
import functools

import jax
import jax.numpy as jnp
from jax import lax
from jax.experimental import pallas as pl
from jax.experimental.pallas import tpu as pltpu
from jax.sharding import PartitionSpec as P

PER_ROW = 2
DEG = 4
SPLIT = 4
GATHER_LIMIT = 12 * 2**20
LANES = ("col", "row")
INNER = (1, 2)


def onehot_sum(selected, high_part, low_part):
    first = jnp.einsum("su,sok->uok", selected, high_part, preferred_element_type=jnp.float32)
    second = jnp.einsum("su,sok->uok", selected, low_part, preferred_element_type=jnp.float32)
    return first + second


def apply_pair(send, grouped, col_ids, onehot):
    tile_rows, per_row, orb, _ = grouped.shape
    piece_rows, width = send.shape
    tile_cols = onehot.shape[1]
    wide = lax.all_gather(send, "col", axis=0, tiled=True).reshape(tile_cols, orb, width)
    picked = jnp.take(wide, col_ids, axis=0).reshape(tile_rows, per_row, orb, width)
    direct = jnp.einsum("tpio,tpok->tik", grouped, picked, preferred_element_type=jnp.float32)
    part_rows = lax.psum_scatter(
        direct.reshape(tile_rows * orb, width).astype(jnp.bfloat16),
        "row",
        scatter_dimension=0,
        tiled=True,
    ).astype(jnp.float32)
    tall = lax.all_gather(send, "row", axis=0, tiled=True).reshape(tile_rows, orb, width)
    mirrored = jnp.einsum("tpio,tik->tpok", grouped, tall, preferred_element_type=jnp.float32)
    mirrored = mirrored.reshape(tile_rows * per_row, orb, width)
    high_part = mirrored.astype(jnp.bfloat16)
    low_part = (mirrored - high_part.astype(jnp.float32)).astype(jnp.bfloat16)
    summed = onehot_sum(onehot, high_part, low_part)
    part_cols = lax.psum_scatter(
        summed.reshape(tile_cols * orb, width).astype(jnp.bfloat16),
        "col",
        scatter_dimension=0,
        tiled=True,
    ).astype(jnp.float32)
    return part_rows + part_cols


def spread_plan(vectors, blocks, cols):
    tiles = blocks[0, 0]
    col_ids = cols[0, 0]
    slots, orb, _ = tiles.shape
    tile_rows = slots // PER_ROW
    tile_cols = lax.axis_size("col") * (vectors.shape[0] // orb)
    grouped = tiles.reshape(tile_rows, PER_ROW, orb, orb)
    onehot = (col_ids[:, None] == jnp.arange(tile_cols, dtype=jnp.int32)[None, :]).astype(
        jnp.bfloat16
    )
    prev = vectors.astype(jnp.float32)
    now = apply_pair(vectors, grouped, col_ids, onehot)
    for step in range(DEG - 1):
        nxt = 2.0 * apply_pair(now.astype(jnp.bfloat16), grouped, col_ids, onehot) - prev
        prev, now = (now, nxt)
    return (now, prev)


def vmem(count=1):
    return [pl.BlockSpec(memory_space=pltpu.VMEM)] * count


def smem(count=1):
    return [pl.BlockSpec(memory_space=pltpu.SMEM)] * count


def anywhere(count=1):
    return [pl.BlockSpec(memory_space=pl.ANY)] * count


def nothing(*refs):
    pass


def after(value, *others, rank=0):
    return pl.pallas_call(
        nothing,
        out_shape=jax.ShapeDtypeStruct(value.shape, value.dtype),
        in_specs=anywhere(1 + len(others)),
        out_specs=anywhere()[0],
        input_output_aliases={0: 0},
        compiler_params=pltpu.CompilerParams(vmem_limit_bytes=2**20),
        cost_estimate=pl.CostEstimate(flops=0, bytes_accessed=rank * 2**23, transcendentals=0),
    )(value, *others)


def copy_kernel(value_ref, *refs):
    out_ref, sem = refs[-2:]
    copy = pltpu.make_async_copy(value_ref, out_ref, sem)
    copy.start()
    copy.wait()


def copy_after(value, *others):
    return pl.pallas_call(
        copy_kernel,
        out_shape=jax.ShapeDtypeStruct(value.shape, value.dtype),
        in_specs=anywhere(1 + len(others)),
        out_specs=anywhere()[0],
        scratch_shapes=[pltpu.SemaphoreType.DMA(())],
        compiler_params=pltpu.CompilerParams(vmem_limit_bytes=2**20),
    )(value, *others)


def pick_kernel(rows, one_ref, other_ref, *refs):
    out_ref, sem = refs[-2:]
    row = lax.axis_index("row")
    first = (row == rows[0]) | (row == rows[1])

    @pl.when(first)
    def _():
        copy = pltpu.make_async_copy(one_ref, out_ref, sem)
        copy.start()
        copy.wait()

    @pl.when(jnp.logical_not(first))
    def _():
        copy = pltpu.make_async_copy(other_ref, out_ref, sem)
        copy.start()
        copy.wait()


def pick(rows, one, other, *others):
    return pl.pallas_call(
        functools.partial(pick_kernel, rows),
        out_shape=jax.ShapeDtypeStruct(one.shape, one.dtype),
        in_specs=anywhere(2 + len(others)),
        out_specs=anywhere()[0],
        scratch_shapes=[pltpu.SemaphoreType.DMA(())],
        compiler_params=pltpu.CompilerParams(vmem_limit_bytes=2**20),
    )(one, other, *others)


def split_kernel(n_col, n_row, vectors_ref, cols_ref, stay_ref, go_ref, turned):
    col, row = lax.axis_index("col"), lax.axis_index("row")
    count, share, rows = turned.shape
    orb = stay_ref.shape[2]
    per_piece = rows // orb
    whole = vectors_ref[...].T
    for d in range(count):
        turned[d] = whole[d * share : (d + 1) * share]
    orders = [(y, one, three) for y in range(2) for one in range(2) for three in range(2)]
    ids = cols_ref[...]
    piece = jnp.zeros_like(ids)
    for c in range(1, n_col):
        piece += (ids >= c * per_piece).astype(jnp.int32)
    ids = ids - piece * per_piece + (piece * n_row + row) * per_piece
    for core, out_ref in enumerate((stay_ref, go_ref)):
        for k, (y, one, three) in enumerate(orders):
            peer = (col ^ (core + 2 * y)) * n_row + (row ^ one ^ 3 * three)
            for b in range(per_piece):
                out_ref[k * per_piece + b] = turned[peer, :, b * orb : (b + 1) * orb]
        out_ref[len(orders) * per_piece] = ids.astype(jnp.float32).astype(out_ref.dtype)


def regroup_kernel(sources, count, stay_ref, came_ref, *outs):
    per_piece = (stay_ref.shape[0] - 1) // (sources * count)
    kept = max(count // 2, 1)
    ids = stay_ref[sources * count * per_piece].astype(jnp.float32)
    came = came_ref[sources * count * per_piece].astype(jnp.float32)
    line = lax.broadcasted_iota(jnp.int32, ids.shape, 0)
    ids = jnp.where(line < sources, ids, pltpu.roll(came, sources, 0))
    for h, out_ref in enumerate(outs):
        if h == 1 and count == 1:
            out_ref[...] = ids.astype(jnp.int32)
            continue
        for s in range(2 * sources):
            ref = stay_ref if s < sources else came_ref
            for k in range(kept * per_piece):
                out_ref[s * kept * per_piece + k] = ref[(s % sources * count + h * kept) * per_piece + k]
        if count > 1:
            out_ref[2 * sources * kept * per_piece] = ids.astype(out_ref.dtype)


def regroup(stay, came, sources, per_piece):
    count = (stay.shape[0] - 1) // (sources * per_piece)
    _, share, orb = stay.shape
    if count > 1:
        outs = [jax.ShapeDtypeStruct(stay.shape, stay.dtype)] * 2
    else:
        outs = [
            jax.ShapeDtypeStruct((2 * sources * per_piece, share, orb), stay.dtype),
            jax.ShapeDtypeStruct((share, orb), jnp.int32),
        ]
    return pl.pallas_call(
        functools.partial(regroup_kernel, sources, count),
        out_shape=outs,
        in_specs=vmem(2),
        out_specs=vmem(2),
        compiler_params=pltpu.CompilerParams(vmem_limit_bytes=2**20),
    )(stay, came)


def place(g, f):
    return (f >> 1) * 8 + ((f & 1) ^ (f >> 1)) * 4 + g


def multiply(t, groups, across, ids_ref, z, straight, scattered):
    tile_rows = z.shape[0] // len(groups)
    orb = z.shape[2]
    for g, group in enumerate(groups):
        if not group:
            continue
        here = across[g] * tile_rows + t
        places = [(tile, t * PER_ROW + p) for tile in group for p in range(PER_ROW)]
        strip = jnp.concatenate([s[slot][...] for (_, s, _, _), slot in places], axis=1)
        turned = jnp.concatenate([st[i, slot] for (_, _, st, i), slot in places], axis=0)
        where = [ids_ref[place(g, f), slot] for (f, *_), slot in places]
        wide = jnp.concatenate([z[u] for u in where], axis=1)
        straight[here] = jnp.dot(wide, turned, preferred_element_type=jnp.float32)
        mirrored = jnp.dot(z[here], strip, preferred_element_type=jnp.float32)
        for i, u in enumerate(where):
            scattered[i % len(scattered)][u] += mirrored[:, i * orb : (i + 1) * orb]


def clear(refs):
    for ref in refs:
        ref[...] = jnp.zeros_like(ref)


def turn_all(bufs, st_ref):
    def four(k, carry):
        for i, buf in enumerate(bufs):
            for m in range(4):
                st_ref[i, 4 * k + m] = buf[4 * k + m].T
        return carry

    lax.fori_loop(0, st_ref.shape[1] // 4, four, 0)


def grouped(tiles, n_col, n_row):
    return [[(f, *tiles[g, f]) for f in range(n_row) if (g, f) in tiles] for g in range(n_col)]


def spread_vectors(parts_ref, z, n_col, n_row, now=None):
    per_piece = z.shape[0] // (n_col * n_row)
    across = [lax.axis_index("col") ^ g for g in range(n_col)]
    down = [lax.axis_index("row") ^ f for f in range(n_row)]
    for g in range(n_col):
        for f in range(n_row):
            for b in range(per_piece):
                u = (across[g] * n_row + down[f]) * per_piece + b
                own = parts_ref[place(g, f) * per_piece + b]
                z[u] = own
                if now is not None:
                    now[u] = own.astype(jnp.float32)


def sum_products(groups, n_col, ids_ref, z, straight, scattered):
    across = [lax.axis_index("col") ^ g for g in range(n_col)]
    clear(scattered)

    for t in range(z.shape[0] // n_col):
        multiply(t, groups, across, ids_ref, z, straight, scattered)
    total = straight[...]
    for ref in scattered:
        total += ref[...]
    return total


def turned_kernel(*refs):
    turn_all(refs[:-1], refs[-1])


def turned_tiles(*bufs):
    size = len(bufs) * bufs[0].size
    return pl.pallas_call(
        turned_kernel,
        out_shape=jax.ShapeDtypeStruct((len(bufs), *bufs[0].shape), bufs[0].dtype),
        in_specs=vmem(len(bufs)),
        out_specs=vmem()[0],
        compiler_params=pltpu.CompilerParams(vmem_limit_bytes=2**20),
        cost_estimate=pl.CostEstimate(flops=0, bytes_accessed=6 * size, transcendentals=0),
    )(*bufs)


def first_kernel(early, later, n_col, n_row, ids_ref, parts_ref, sta_ref, *refs):
    sa, refs = refs[: len(early)], refs[len(early) :]
    sb, (stb_ref, sum_ref, z, straight, *scattered) = refs[: len(later)], refs[len(later) :]
    spread_vectors(parts_ref, z, n_col, n_row)
    turn_all(sb, stb_ref)
    tiles = {at: (s, sta_ref, i) for i, (at, s) in enumerate(zip(early, sa))}
    tiles.update({at: (s, stb_ref, i) for i, (at, s) in enumerate(zip(later, sb))})
    clear([straight])
    sum_ref[...] = sum_products(grouped(tiles, n_col, n_row), n_col, ids_ref, z, straight, scattered)


def filter_kernel(early, later, late, n_col, n_row, ids_ref, parts_ref, sum_ref, *refs):
    (sta_ref, stb_ref), refs = refs[:2], refs[2:]
    sa, refs = refs[: len(early)], refs[len(early) :]
    sb, refs = refs[: len(later)], refs[len(later) :]
    bufs, (out_ref, st_ref, z, now, prev, straight, *scattered) = refs[: len(late)], refs[len(late) :]
    n_blocks, share, orb = z.shape
    per_piece = n_blocks // (n_col * n_row)
    rest = sorted({(g, f) for g, f, _ in late})
    spread_vectors(parts_ref, z, n_col, n_row, prev)
    slots = {at: {} for at in rest}
    for buf, (g, f, start) in zip(bufs, late):
        for k in range(buf.shape[0]):
            slots[g, f][start + k] = buf.at[k]
    for i, at in enumerate(rest):
        for slot, block in slots[at].items():
            st_ref[i, slot] = block[...].T

    tiles = {at: (slots[at], st_ref, i) for i, at in enumerate(rest)}
    clear([straight])
    total = sum_products(grouped(tiles, n_col, n_row), n_col, ids_ref, z, straight, scattered)
    total += sum_ref[...]
    now[...] = total
    z[...] = total.astype(z.dtype)

    tiles.update({at: (s, sta_ref, i) for i, (at, s) in enumerate(zip(early, sa))})
    tiles.update({at: (s, stb_ref, i) for i, (at, s) in enumerate(zip(later, sb))})
    groups = grouped(tiles, n_col, n_row)

    def one_step(step, carry):
        total = sum_products(groups, n_col, ids_ref, z, straight, scattered)
        total = 2.0 * total - prev[...]
        prev[...] = now[...]
        now[...] = total
        z[...] = total.astype(z.dtype)
        return carry

    lax.fori_loop(1, DEG, one_step, 0)
    for p in range(n_col * n_row):
        for b in range(per_piece):
            u = p * per_piece + b
            out_ref[p, 0, :, b * orb : (b + 1) * orb] = now[u].astype(out_ref.dtype)
            out_ref[p, 1, :, b * orb : (b + 1) * orb] = prev[u].astype(out_ref.dtype)


def result_kernel(back_ref, marker_ref, last_ref, before_ref):
    count, _, share, rows = back_ref.shape
    for i, out_ref in enumerate((last_ref, before_ref)):
        whole = jnp.concatenate([back_ref[d, i] for d in range(count)], axis=0)
        out_ref[...] = whole.astype(jnp.float32).T


def gather_plan(vectors, blocks, cols):
    n_dev = lax.axis_size(LANES)
    n_col, n_row = lax.axis_size("col"), lax.axis_size("row")
    rows, width = vectors.shape
    slots, orb = blocks.shape[2:4]
    share = width // n_dev
    per_piece = rows // orb
    n_blocks = n_dev * per_piece
    half = slots // 2

    def send(buf, flip_col, flip_row, from_rows=range(n_row)):
        pairs = [
            (c * n_row + r, (c ^ flip_col) * n_row + (r ^ flip_row))
            for c in range(n_col)
            for r in from_rows
        ]
        return lax.ppermute(buf, LANES, pairs)

    def to_mate(*bufs):
        return [send(buf, 1, 0) for buf in bufs]

    own = blocks[0, 0]
    near = send(own, 0, 1)
    inner = send(own, 0, 3, INNER)
    over_own = after(send(own, 2, 0), rank=1)

    own_cols = jnp.broadcast_to(jnp.pad(cols[0, 0], (0, orb - slots)), (share, orb))
    shares = jax.ShapeDtypeStruct((n_dev // 2 * per_piece + 1, share, orb), vectors.dtype)
    stay, go = pl.pallas_call(
        functools.partial(split_kernel, n_col, n_row),
        out_shape=[shares, shares],
        in_specs=vmem(2),
        out_specs=vmem(2),
        scratch_shapes=[pltpu.VMEM((n_dev, share, rows), vectors.dtype)],
        compiler_params=pltpu.CompilerParams(vmem_limit_bytes=4 * 2**20),
    )(vectors, own_cols)
    stay, go = regroup(stay, send(go, 1, 0), 1, per_piece)

    stay, go = regroup(stay, send(go, 2, 0), 2, per_piece)
    mates = to_mate(own)
    near = after(near, over_own, go, *mates)
    over_near = after(send(near, 2, 0), rank=3)
    mates += to_mate(near)
    crossed = after(send(copy_after(near, mates[1]), 0, 3, INNER), rank=1)
    inner = after(inner, near)
    outward = after(send(inner, 0, 1, INNER), rank=1)
    stay, go = regroup(stay, send(go, 0, 1), 4, per_piece)
    mates += to_mate(over_own)
    two = pick(INNER, crossed, outward, over_near, go, *mates)

    over_two = send(two, 2, 0)
    outer = after(send(crossed, 0, 1, INNER), rank=1)
    mates += to_mate(two, over_near)
    mine, ids = regroup(stay, send(go, 0, 3), 8, per_piece)
    sa = [own, near, over_own, over_near, *mates[:3]]
    sta = turned_tiles(*sa)
    three = pick(INNER, inner, outer, over_two, mine, sta, *mates[3:])

    over_three = send(three[:half], 2, 0)
    side_three = send(over_two[half:], 0, 1)
    mates += to_mate(three, over_two)
    early = [(0, 0), (0, 1), (2, 0), (2, 1), (1, 0), (1, 1), (3, 0)]
    later = [(0, 2), (2, 2), (0, 3), (1, 2), (3, 1), (1, 3), (3, 2)]
    tiles_of = jax.ShapeDtypeStruct((len(later), slots, orb, orb), blocks.dtype)
    sums = jax.ShapeDtypeStruct((n_blocks, share, orb), jnp.float32)
    sb = [two, over_two, three, *mates[3:]]
    stb, total = pl.pallas_call(
        functools.partial(first_kernel, early, later, n_col, n_row),
        out_shape=[tiles_of, sums],
        in_specs=smem() + vmem(2 + len(early + later)),
        out_specs=vmem(2),
        scratch_shapes=[
            pltpu.VMEM((n_blocks, share, orb), jnp.bfloat16),
            *[pltpu.VMEM((n_blocks, share, orb), jnp.float32)] * (1 + SPLIT),
        ],
        compiler_params=pltpu.CompilerParams(vmem_limit_bytes=6 * 2**20),
        cost_estimate=pl.CostEstimate(
            flops=4 * len(early + later) * slots * orb * orb * share,
            bytes_accessed=6 * len(later) * own.size,
            transcendentals=0,
        ),
    )(ids, mine, sta, *sa, *sb)
    over_three, side_three = after(over_three, stb), after(side_three, stb)
    late = [(2, 3, 0), (2, 3, half), (3, 3, 0), (3, 3, half)]
    late_bufs = [over_three, side_three, *to_mate(over_three, side_three)]

    done = pl.pallas_call(
        functools.partial(filter_kernel, early, later, late, n_col, n_row),
        out_shape=jax.ShapeDtypeStruct((n_dev, 2, share, rows), jnp.bfloat16),
        in_specs=smem() + vmem(4 + len(early + later + late)),
        out_specs=vmem()[0],
        scratch_shapes=[
            pltpu.VMEM((2, slots, orb, orb), blocks.dtype),
            pltpu.VMEM((n_blocks, share, orb), jnp.bfloat16),
            *[pltpu.VMEM((n_blocks, share, orb), jnp.float32)] * (3 + SPLIT),
        ],
        compiler_params=pltpu.CompilerParams(vmem_limit_bytes=12 * 2**20),
    )(ids, mine, total, sta, stb, *sa, *sb, *late_bufs)
    back = lax.all_to_all(done, LANES, split_axis=0, concat_axis=0, tiled=True)
    whole = jax.ShapeDtypeStruct((rows, width), jnp.float32)
    return pl.pallas_call(
        result_kernel,
        out_shape=[whole, whole],
        in_specs=vmem() + anywhere(),
        out_specs=vmem(2),
        compiler_params=pltpu.CompilerParams(vmem_limit_bytes=4 * 2**20),
    )(back, after(ids, done, rank=8))


def per_device(vectors, blocks, cols):
    n_dev = lax.axis_size(LANES)
    line_of_four = lax.axis_size("col") == 4 and lax.axis_size("row") == 4
    line_of_four = line_of_four and vectors.shape[1] // n_dev == n_dev
    if line_of_four and n_dev * blocks.size * blocks.dtype.itemsize <= GATHER_LIMIT:
        return gather_plan(vectors, blocks, cols)
    return spread_plan(vectors, blocks, cols)


def solution(mesh):
    return jax.shard_map(
        per_device,
        mesh=mesh,
        in_specs=(
            P(("col", "row"), "dom"),
            P(("dom", "col"), "row", None, None, None),
            P(("dom", "col"), "row", None),
        ),
        out_specs=(P(("col", "row"), "dom"), P(("col", "row"), "dom")),
        check_vma=False,
    )
```

```python
import functools

import jax
import jax.numpy as jnp
from jax import lax
from jax.experimental import pallas as pl
from jax.experimental.pallas import tpu as pltpu
from jax.sharding import PartitionSpec as P

PER_ROW = 2
DEG = 4
SPLIT = 4
GATHER_LIMIT = 12 * 2**20
LANES = ("col", "row")
INNER = (1, 2)


def onehot_sum(selected, high_part, low_part):
    first = jnp.einsum("su,sok->uok", selected, high_part, preferred_element_type=jnp.float32)
    second = jnp.einsum("su,sok->uok", selected, low_part, preferred_element_type=jnp.float32)
    return first + second


def apply_pair(send, grouped, col_ids, onehot):
    tile_rows, per_row, orb, _ = grouped.shape
    piece_rows, width = send.shape
    tile_cols = onehot.shape[1]
    wide = lax.all_gather(send, "col", axis=0, tiled=True).reshape(tile_cols, orb, width)
    picked = jnp.take(wide, col_ids, axis=0).reshape(tile_rows, per_row, orb, width)
    direct = jnp.einsum("tpio,tpok->tik", grouped, picked, preferred_element_type=jnp.float32)
    part_rows = lax.psum_scatter(
        direct.reshape(tile_rows * orb, width).astype(jnp.bfloat16),
        "row",
        scatter_dimension=0,
        tiled=True,
    ).astype(jnp.float32)
    tall = lax.all_gather(send, "row", axis=0, tiled=True).reshape(tile_rows, orb, width)
    mirrored = jnp.einsum("tpio,tik->tpok", grouped, tall, preferred_element_type=jnp.float32)
    mirrored = mirrored.reshape(tile_rows * per_row, orb, width)
    high_part = mirrored.astype(jnp.bfloat16)
    low_part = (mirrored - high_part.astype(jnp.float32)).astype(jnp.bfloat16)
    summed = onehot_sum(onehot, high_part, low_part)
    part_cols = lax.psum_scatter(
        summed.reshape(tile_cols * orb, width).astype(jnp.bfloat16),
        "col",
        scatter_dimension=0,
        tiled=True,
    ).astype(jnp.float32)
    return part_rows + part_cols


def spread_plan(vectors, blocks, cols):
    tiles = blocks[0, 0]
    col_ids = cols[0, 0]
    slots, orb, _ = tiles.shape
    tile_rows = slots // PER_ROW
    tile_cols = lax.axis_size("col") * (vectors.shape[0] // orb)
    grouped = tiles.reshape(tile_rows, PER_ROW, orb, orb)
    onehot = (col_ids[:, None] == jnp.arange(tile_cols, dtype=jnp.int32)[None, :]).astype(
        jnp.bfloat16
    )
    prev = vectors.astype(jnp.float32)
    now = apply_pair(vectors, grouped, col_ids, onehot)
    for step in range(DEG - 1):
        nxt = 2.0 * apply_pair(now.astype(jnp.bfloat16), grouped, col_ids, onehot) - prev
        prev, now = (now, nxt)
    return (now, prev)


def vmem(count=1):
    return [pl.BlockSpec(memory_space=pltpu.VMEM)] * count


def smem(count=1):
    return [pl.BlockSpec(memory_space=pltpu.SMEM)] * count


def anywhere(count=1):
    return [pl.BlockSpec(memory_space=pl.ANY)] * count


def nothing(*refs):
    pass


def after(value, *others, rank=0):
    return pl.pallas_call(
        nothing,
        out_shape=jax.ShapeDtypeStruct(value.shape, value.dtype),
        in_specs=anywhere(1 + len(others)),
        out_specs=anywhere()[0],
        input_output_aliases={0: 0},
        compiler_params=pltpu.CompilerParams(vmem_limit_bytes=2**20),
        cost_estimate=pl.CostEstimate(flops=0, bytes_accessed=rank * 2**23, transcendentals=0),
    )(value, *others)


def pick_kernel(rows, one_ref, other_ref, *refs):
    out_ref, sem = refs[-2:]
    row = lax.axis_index("row")
    first = (row == rows[0]) | (row == rows[1])

    @pl.when(first)
    def _():
        copy = pltpu.make_async_copy(one_ref, out_ref, sem)
        copy.start()
        copy.wait()

    @pl.when(jnp.logical_not(first))
    def _():
        copy = pltpu.make_async_copy(other_ref, out_ref, sem)
        copy.start()
        copy.wait()


def pick(rows, one, other, *others):
    return pl.pallas_call(
        functools.partial(pick_kernel, rows),
        out_shape=jax.ShapeDtypeStruct(one.shape, one.dtype),
        in_specs=anywhere(2 + len(others)),
        out_specs=anywhere()[0],
        scratch_shapes=[pltpu.SemaphoreType.DMA(())],
        compiler_params=pltpu.CompilerParams(vmem_limit_bytes=2**20),
    )(one, other, *others)


def split_kernel(n_col, n_row, vectors_ref, cols_ref, stay_ref, go_ref, turned):
    col, row = lax.axis_index("col"), lax.axis_index("row")
    count, share, rows = turned.shape
    orb = stay_ref.shape[2]
    per_piece = rows // orb
    whole = vectors_ref[...].T
    for d in range(count):
        turned[d] = whole[d * share : (d + 1) * share]
    orders = [(y, one, three) for y in range(2) for one in range(2) for three in range(2)]
    ids = cols_ref[...]
    piece = jnp.zeros_like(ids)
    for c in range(1, n_col):
        piece += (ids >= c * per_piece).astype(jnp.int32)
    ids = ids - piece * per_piece + (piece * n_row + row) * per_piece
    for core, out_ref in enumerate((stay_ref, go_ref)):
        for k, (y, one, three) in enumerate(orders):
            peer = (col ^ (core + 2 * y)) * n_row + (row ^ one ^ 3 * three)
            for b in range(per_piece):
                out_ref[k * per_piece + b] = turned[peer, :, b * orb : (b + 1) * orb]
        out_ref[len(orders) * per_piece] = ids.astype(jnp.float32).astype(out_ref.dtype)


def regroup_kernel(sources, count, stay_ref, came_ref, *outs):
    per_piece = (stay_ref.shape[0] - 1) // (sources * count)
    kept = max(count // 2, 1)
    ids = stay_ref[sources * count * per_piece].astype(jnp.float32)
    came = came_ref[sources * count * per_piece].astype(jnp.float32)
    line = lax.broadcasted_iota(jnp.int32, ids.shape, 0)
    ids = jnp.where(line < sources, ids, pltpu.roll(came, sources, 0))
    for h, out_ref in enumerate(outs):
        if h == 1 and count == 1:
            out_ref[...] = ids.astype(jnp.int32)
            continue
        for s in range(2 * sources):
            ref = stay_ref if s < sources else came_ref
            for k in range(kept * per_piece):
                out_ref[s * kept * per_piece + k] = ref[(s % sources * count + h * kept) * per_piece + k]
        if count > 1:
            out_ref[2 * sources * kept * per_piece] = ids.astype(out_ref.dtype)


def regroup(stay, came, sources, per_piece):
    count = (stay.shape[0] - 1) // (sources * per_piece)
    _, share, orb = stay.shape
    if count > 1:
        outs = [jax.ShapeDtypeStruct(stay.shape, stay.dtype)] * 2
    else:
        outs = [
            jax.ShapeDtypeStruct((2 * sources * per_piece, share, orb), stay.dtype),
            jax.ShapeDtypeStruct((share, orb), jnp.int32),
        ]
    return pl.pallas_call(
        functools.partial(regroup_kernel, sources, count),
        out_shape=outs,
        in_specs=vmem(2),
        out_specs=vmem(2),
        compiler_params=pltpu.CompilerParams(vmem_limit_bytes=2**20),
    )(stay, came)


def place(g, f):
    return (f >> 1) * 8 + ((f & 1) ^ (f >> 1)) * 4 + g


def multiply(t, groups, across, ids_ref, z, straight, scattered):
    tile_rows = z.shape[0] // len(groups)
    orb = z.shape[2]
    for g, group in enumerate(groups):
        if not group:
            continue
        here = across[g] * tile_rows + t
        places = [(tile, t * PER_ROW + p) for tile in group for p in range(PER_ROW)]
        strip = jnp.concatenate([s[slot][...] for (_, s, _, _), slot in places], axis=1)
        turned = jnp.concatenate([st[i, slot] for (_, _, st, i), slot in places], axis=0)
        where = [ids_ref[place(g, f), slot] for (f, *_), slot in places]
        wide = jnp.concatenate([z[u] for u in where], axis=1)
        straight[here] = jnp.dot(wide, turned, preferred_element_type=jnp.float32)
        mirrored = jnp.dot(z[here], strip, preferred_element_type=jnp.float32)
        for i, u in enumerate(where):
            scattered[i % len(scattered)][u] += mirrored[:, i * orb : (i + 1) * orb]


def clear(refs):
    for ref in refs:
        ref[...] = jnp.zeros_like(ref)


def turn_all(bufs, st_ref):
    def four(k, carry):
        for i, buf in enumerate(bufs):
            for m in range(4):
                st_ref[i, 4 * k + m] = buf[4 * k + m].T
        return carry

    lax.fori_loop(0, st_ref.shape[1] // 4, four, 0)


def grouped(tiles, n_col, n_row):
    return [[(f, *tiles[g, f]) for f in range(n_row) if (g, f) in tiles] for g in range(n_col)]


def spread_vectors(parts_ref, z, n_col, n_row, now=None):
    per_piece = z.shape[0] // (n_col * n_row)
    across = [lax.axis_index("col") ^ g for g in range(n_col)]
    down = [lax.axis_index("row") ^ f for f in range(n_row)]
    for g in range(n_col):
        for f in range(n_row):
            for b in range(per_piece):
                u = (across[g] * n_row + down[f]) * per_piece + b
                own = parts_ref[place(g, f) * per_piece + b]
                z[u] = own
                if now is not None:
                    now[u] = own.astype(jnp.float32)


def sum_products(groups, n_col, ids_ref, z, straight, scattered):
    across = [lax.axis_index("col") ^ g for g in range(n_col)]
    clear(scattered)

    for t in range(z.shape[0] // n_col):
        multiply(t, groups, across, ids_ref, z, straight, scattered)
    total = straight[...]
    for ref in scattered:
        total += ref[...]
    return total


def turned_kernel(*refs):
    turn_all(refs[:-1], refs[-1])


def turned_tiles(*bufs):
    size = len(bufs) * bufs[0].size
    return pl.pallas_call(
        turned_kernel,
        out_shape=jax.ShapeDtypeStruct((len(bufs), *bufs[0].shape), bufs[0].dtype),
        in_specs=vmem(len(bufs)),
        out_specs=vmem()[0],
        compiler_params=pltpu.CompilerParams(vmem_limit_bytes=2**20),
        cost_estimate=pl.CostEstimate(flops=0, bytes_accessed=6 * size, transcendentals=0),
    )(*bufs)


def first_kernel(early, later, n_col, n_row, ids_ref, parts_ref, sta_ref, *refs):
    sa, refs = refs[: len(early)], refs[len(early) :]
    sb, (stb_ref, sum_ref, z, straight, *scattered) = refs[: len(later)], refs[len(later) :]
    spread_vectors(parts_ref, z, n_col, n_row)
    turn_all(sb, stb_ref)
    tiles = {at: (s, sta_ref, i) for i, (at, s) in enumerate(zip(early, sa))}
    tiles.update({at: (s, stb_ref, i) for i, (at, s) in enumerate(zip(later, sb))})
    clear([straight])
    sum_ref[...] = sum_products(grouped(tiles, n_col, n_row), n_col, ids_ref, z, straight, scattered)


def filter_kernel(early, later, late, n_col, n_row, ids_ref, parts_ref, sum_ref, *refs):
    (sta_ref, stb_ref), refs = refs[:2], refs[2:]
    sa, refs = refs[: len(early)], refs[len(early) :]
    sb, refs = refs[: len(later)], refs[len(later) :]
    bufs, (out_ref, st_ref, z, now, prev, straight, *scattered) = refs[: len(late)], refs[len(late) :]
    n_blocks, share, orb = z.shape
    per_piece = n_blocks // (n_col * n_row)
    rest = sorted({(g, f) for g, f, _ in late})
    spread_vectors(parts_ref, z, n_col, n_row, prev)
    slots = {at: {} for at in rest}
    for buf, (g, f, start) in zip(bufs, late):
        for k in range(buf.shape[0]):
            slots[g, f][start + k] = buf.at[k]
    for i, at in enumerate(rest):
        for slot, block in slots[at].items():
            st_ref[i, slot] = block[...].T

    tiles = {at: (slots[at], st_ref, i) for i, at in enumerate(rest)}
    clear([straight])
    total = sum_products(grouped(tiles, n_col, n_row), n_col, ids_ref, z, straight, scattered)
    total += sum_ref[...]
    now[...] = total
    z[...] = total.astype(z.dtype)

    tiles.update({at: (s, sta_ref, i) for i, (at, s) in enumerate(zip(early, sa))})
    tiles.update({at: (s, stb_ref, i) for i, (at, s) in enumerate(zip(later, sb))})
    groups = grouped(tiles, n_col, n_row)

    def one_step(step, carry):
        total = sum_products(groups, n_col, ids_ref, z, straight, scattered)
        total = 2.0 * total - prev[...]
        prev[...] = now[...]
        now[...] = total
        z[...] = total.astype(z.dtype)
        return carry

    lax.fori_loop(1, DEG, one_step, 0)
    for p in range(n_col * n_row):
        for b in range(per_piece):
            u = p * per_piece + b
            out_ref[p, 0, :, b * orb : (b + 1) * orb] = now[u].astype(out_ref.dtype)
            out_ref[p, 1, :, b * orb : (b + 1) * orb] = prev[u].astype(out_ref.dtype)


def result_kernel(back_ref, marker_ref, last_ref, before_ref):
    count, _, share, rows = back_ref.shape
    for i, out_ref in enumerate((last_ref, before_ref)):
        whole = jnp.concatenate([back_ref[d, i] for d in range(count)], axis=0)
        out_ref[...] = whole.astype(jnp.float32).T


def gather_plan(vectors, blocks, cols):
    n_dev = lax.axis_size(LANES)
    n_col, n_row = lax.axis_size("col"), lax.axis_size("row")
    rows, width = vectors.shape
    slots, orb = blocks.shape[2:4]
    share = width // n_dev
    per_piece = rows // orb
    n_blocks = n_dev * per_piece
    half = slots // 2

    def send(buf, flip_col, flip_row, from_rows=range(n_row)):
        pairs = [
            (c * n_row + r, (c ^ flip_col) * n_row + (r ^ flip_row))
            for c in range(n_col)
            for r in from_rows
        ]
        return lax.ppermute(buf, LANES, pairs)

    def to_mate(*bufs):
        return [send(buf, 1, 0) for buf in bufs]

    own = blocks[0, 0]
    near = send(own, 0, 1)
    inner = send(own, 0, 3, INNER)
    over_own = after(send(own, 2, 0), rank=1)

    own_cols = jnp.broadcast_to(jnp.pad(cols[0, 0], (0, orb - slots)), (share, orb))
    shares = jax.ShapeDtypeStruct((n_dev // 2 * per_piece + 1, share, orb), vectors.dtype)
    stay, go = pl.pallas_call(
        functools.partial(split_kernel, n_col, n_row),
        out_shape=[shares, shares],
        in_specs=vmem(2),
        out_specs=vmem(2),
        scratch_shapes=[pltpu.VMEM((n_dev, share, rows), vectors.dtype)],
        compiler_params=pltpu.CompilerParams(vmem_limit_bytes=4 * 2**20),
    )(vectors, own_cols)
    stay, go = regroup(stay, send(go, 1, 0), 1, per_piece)

    stay, go = regroup(stay, send(go, 2, 0), 2, per_piece)
    mates = to_mate(own)
    near = after(near, over_own, go, *mates)
    over_near = after(send(near, 2, 0), rank=3)
    crossed = after(send(near, 0, 3, INNER), rank=1)
    outward = send(inner, 0, 1, INNER)
    stay, go = regroup(stay, send(go, 0, 1), 4, per_piece)
    mates += to_mate(near, over_own)
    two = pick(INNER, crossed, outward, over_near, go, *mates)

    over_two = send(two, 2, 0)
    outer = after(send(crossed, 0, 1, INNER), rank=1)
    mates += to_mate(two, over_near)
    mine, ids = regroup(stay, send(go, 0, 3), 8, per_piece)
    sa = [own, near, over_own, over_near, *mates[:3]]
    sta = turned_tiles(*sa)
    three = pick(INNER, inner, outer, over_two, mine, sta, *mates[3:])

    over_three = send(three[:half], 2, 0)
    side_three = send(over_two[half:], 0, 1)
    mates += to_mate(three, over_two)
    early = [(0, 0), (0, 1), (2, 0), (2, 1), (1, 0), (1, 1), (3, 0)]
    later = [(0, 2), (2, 2), (0, 3), (1, 2), (3, 1), (1, 3), (3, 2)]
    tiles_of = jax.ShapeDtypeStruct((len(later), slots, orb, orb), blocks.dtype)
    sums = jax.ShapeDtypeStruct((n_blocks, share, orb), jnp.float32)
    sb = [two, over_two, three, *mates[3:]]
    stb, total = pl.pallas_call(
        functools.partial(first_kernel, early, later, n_col, n_row),
        out_shape=[tiles_of, sums],
        in_specs=smem() + vmem(2 + len(early + later)),
        out_specs=vmem(2),
        scratch_shapes=[
            pltpu.VMEM((n_blocks, share, orb), jnp.bfloat16),
            *[pltpu.VMEM((n_blocks, share, orb), jnp.float32)] * (1 + SPLIT),
        ],
        compiler_params=pltpu.CompilerParams(vmem_limit_bytes=6 * 2**20),
        cost_estimate=pl.CostEstimate(
            flops=4 * len(early + later) * slots * orb * orb * share,
            bytes_accessed=6 * len(later) * own.size,
            transcendentals=0,
        ),
    )(ids, mine, sta, *sa, *sb)
    over_three, side_three = after(over_three, stb), after(side_three, stb)
    late = [(2, 3, 0), (2, 3, half), (3, 3, 0), (3, 3, half)]
    late_bufs = [over_three, side_three, *to_mate(over_three, side_three)]

    done = pl.pallas_call(
        functools.partial(filter_kernel, early, later, late, n_col, n_row),
        out_shape=jax.ShapeDtypeStruct((n_dev, 2, share, rows), jnp.bfloat16),
        in_specs=smem() + vmem(4 + len(early + later + late)),
        out_specs=vmem()[0],
        scratch_shapes=[
            pltpu.VMEM((2, slots, orb, orb), blocks.dtype),
            pltpu.VMEM((n_blocks, share, orb), jnp.bfloat16),
            *[pltpu.VMEM((n_blocks, share, orb), jnp.float32)] * (3 + SPLIT),
        ],
        compiler_params=pltpu.CompilerParams(vmem_limit_bytes=12 * 2**20),
    )(ids, mine, total, sta, stb, *sa, *sb, *late_bufs)
    back = lax.all_to_all(done, LANES, split_axis=0, concat_axis=0, tiled=True)
    whole = jax.ShapeDtypeStruct((rows, width), jnp.float32)
    return pl.pallas_call(
        result_kernel,
        out_shape=[whole, whole],
        in_specs=vmem() + anywhere(),
        out_specs=vmem(2),
        compiler_params=pltpu.CompilerParams(vmem_limit_bytes=4 * 2**20),
    )(back, after(ids, done, rank=8))


def per_device(vectors, blocks, cols):
    n_dev = lax.axis_size(LANES)
    line_of_four = lax.axis_size("col") == 4 and lax.axis_size("row") == 4
    line_of_four = line_of_four and vectors.shape[1] // n_dev == n_dev
    if line_of_four and n_dev * blocks.size * blocks.dtype.itemsize <= GATHER_LIMIT:
        return gather_plan(vectors, blocks, cols)
    return spread_plan(vectors, blocks, cols)


def solution(mesh):
    return jax.shard_map(
        per_device,
        mesh=mesh,
        in_specs=(
            P(("col", "row"), "dom"),
            P(("dom", "col"), "row", None, None, None),
            P(("dom", "col"), "row", None),
        ),
        out_specs=(P(("col", "row"), "dom"), P(("col", "row"), "dom")),
        check_vma=False,
    )
```

```python
import functools

import jax
import jax.numpy as jnp
from jax import lax
from jax.experimental import pallas as pl
from jax.experimental.pallas import tpu as pltpu
from jax.sharding import PartitionSpec as P

PER_ROW = 2
DEG = 4
SPLIT = 4
GATHER_LIMIT = 12 * 2**20
LANES = ("col", "row")
INNER = (1, 2)


def onehot_sum(selected, high_part, low_part):
    first = jnp.einsum("su,sok->uok", selected, high_part, preferred_element_type=jnp.float32)
    second = jnp.einsum("su,sok->uok", selected, low_part, preferred_element_type=jnp.float32)
    return first + second


def apply_pair(send, grouped, col_ids, onehot):
    tile_rows, per_row, orb, _ = grouped.shape
    piece_rows, width = send.shape
    tile_cols = onehot.shape[1]
    wide = lax.all_gather(send, "col", axis=0, tiled=True).reshape(tile_cols, orb, width)
    picked = jnp.take(wide, col_ids, axis=0).reshape(tile_rows, per_row, orb, width)
    direct = jnp.einsum("tpio,tpok->tik", grouped, picked, preferred_element_type=jnp.float32)
    part_rows = lax.psum_scatter(
        direct.reshape(tile_rows * orb, width).astype(jnp.bfloat16),
        "row",
        scatter_dimension=0,
        tiled=True,
    ).astype(jnp.float32)
    tall = lax.all_gather(send, "row", axis=0, tiled=True).reshape(tile_rows, orb, width)
    mirrored = jnp.einsum("tpio,tik->tpok", grouped, tall, preferred_element_type=jnp.float32)
    mirrored = mirrored.reshape(tile_rows * per_row, orb, width)
    high_part = mirrored.astype(jnp.bfloat16)
    low_part = (mirrored - high_part.astype(jnp.float32)).astype(jnp.bfloat16)
    summed = onehot_sum(onehot, high_part, low_part)
    part_cols = lax.psum_scatter(
        summed.reshape(tile_cols * orb, width).astype(jnp.bfloat16),
        "col",
        scatter_dimension=0,
        tiled=True,
    ).astype(jnp.float32)
    return part_rows + part_cols


def spread_plan(vectors, blocks, cols):
    tiles = blocks[0, 0]
    col_ids = cols[0, 0]
    slots, orb, _ = tiles.shape
    tile_rows = slots // PER_ROW
    tile_cols = lax.axis_size("col") * (vectors.shape[0] // orb)
    grouped = tiles.reshape(tile_rows, PER_ROW, orb, orb)
    onehot = (col_ids[:, None] == jnp.arange(tile_cols, dtype=jnp.int32)[None, :]).astype(
        jnp.bfloat16
    )
    prev = vectors.astype(jnp.float32)
    now = apply_pair(vectors, grouped, col_ids, onehot)
    for step in range(DEG - 1):
        nxt = 2.0 * apply_pair(now.astype(jnp.bfloat16), grouped, col_ids, onehot) - prev
        prev, now = (now, nxt)
    return (now, prev)


def vmem(count=1):
    return [pl.BlockSpec(memory_space=pltpu.VMEM)] * count


def smem(count=1):
    return [pl.BlockSpec(memory_space=pltpu.SMEM)] * count


def anywhere(count=1):
    return [pl.BlockSpec(memory_space=pl.ANY)] * count


def nothing(*refs):
    pass


def after(value, *others, rank=0):
    return pl.pallas_call(
        nothing,
        out_shape=jax.ShapeDtypeStruct(value.shape, value.dtype),
        in_specs=anywhere(1 + len(others)),
        out_specs=anywhere()[0],
        input_output_aliases={0: 0},
        compiler_params=pltpu.CompilerParams(vmem_limit_bytes=2**20),
        cost_estimate=pl.CostEstimate(flops=0, bytes_accessed=rank * 2**23, transcendentals=0),
    )(value, *others)


def copy_kernel(value_ref, *refs):
    out_ref, sem = refs[-2:]
    copy = pltpu.make_async_copy(value_ref, out_ref, sem)
    copy.start()
    copy.wait()


def copy_after(value, *others):
    return pl.pallas_call(
        copy_kernel,
        out_shape=jax.ShapeDtypeStruct(value.shape, value.dtype),
        in_specs=anywhere(1 + len(others)),
        out_specs=anywhere()[0],
        scratch_shapes=[pltpu.SemaphoreType.DMA(())],
        compiler_params=pltpu.CompilerParams(vmem_limit_bytes=2**20),
    )(value, *others)


def pick_kernel(rows, one_ref, other_ref, *refs):
    out_ref, sem = refs[-2:]
    row = lax.axis_index("row")
    first = (row == rows[0]) | (row == rows[1])

    @pl.when(first)
    def _():
        copy = pltpu.make_async_copy(one_ref, out_ref, sem)
        copy.start()
        copy.wait()

    @pl.when(jnp.logical_not(first))
    def _():
        copy = pltpu.make_async_copy(other_ref, out_ref, sem)
        copy.start()
        copy.wait()


def pick(rows, one, other, *others):
    return pl.pallas_call(
        functools.partial(pick_kernel, rows),
        out_shape=jax.ShapeDtypeStruct(one.shape, one.dtype),
        in_specs=anywhere(2 + len(others)),
        out_specs=anywhere()[0],
        scratch_shapes=[pltpu.SemaphoreType.DMA(())],
        compiler_params=pltpu.CompilerParams(vmem_limit_bytes=2**20),
    )(one, other, *others)


def split_kernel(n_col, n_row, vectors_ref, cols_ref, stay_ref, go_ref, turned):
    col, row = lax.axis_index("col"), lax.axis_index("row")
    count, share, rows = turned.shape
    orb = stay_ref.shape[2]
    per_piece = rows // orb
    whole = vectors_ref[...].T
    for d in range(count):
        turned[d] = whole[d * share : (d + 1) * share]
    orders = [(y, one, three) for y in range(2) for one in range(2) for three in range(2)]
    ids = cols_ref[...]
    piece = jnp.zeros_like(ids)
    for c in range(1, n_col):
        piece += (ids >= c * per_piece).astype(jnp.int32)
    ids = ids - piece * per_piece + (piece * n_row + row) * per_piece
    for core, out_ref in enumerate((stay_ref, go_ref)):
        for k, (y, one, three) in enumerate(orders):
            peer = (col ^ (core + 2 * y)) * n_row + (row ^ one ^ 3 * three)
            for b in range(per_piece):
                out_ref[k * per_piece + b] = turned[peer, :, b * orb : (b + 1) * orb]
        out_ref[len(orders) * per_piece] = ids.astype(jnp.float32).astype(out_ref.dtype)


def regroup_kernel(sources, count, stay_ref, came_ref, *outs):
    per_piece = (stay_ref.shape[0] - 1) // (sources * count)
    kept = max(count // 2, 1)
    ids = stay_ref[sources * count * per_piece].astype(jnp.float32)
    came = came_ref[sources * count * per_piece].astype(jnp.float32)
    line = lax.broadcasted_iota(jnp.int32, ids.shape, 0)
    ids = jnp.where(line < sources, ids, pltpu.roll(came, sources, 0))
    for h, out_ref in enumerate(outs):
        if h == 1 and count == 1:
            out_ref[...] = ids.astype(jnp.int32)
            continue
        for s in range(2 * sources):
            ref = stay_ref if s < sources else came_ref
            for k in range(kept * per_piece):
                out_ref[s * kept * per_piece + k] = ref[(s % sources * count + h * kept) * per_piece + k]
        if count > 1:
            out_ref[2 * sources * kept * per_piece] = ids.astype(out_ref.dtype)


def regroup(stay, came, sources, per_piece):
    count = (stay.shape[0] - 1) // (sources * per_piece)
    _, share, orb = stay.shape
    if count > 1:
        outs = [jax.ShapeDtypeStruct(stay.shape, stay.dtype)] * 2
    else:
        outs = [
            jax.ShapeDtypeStruct((2 * sources * per_piece, share, orb), stay.dtype),
            jax.ShapeDtypeStruct((share, orb), jnp.int32),
        ]
    return pl.pallas_call(
        functools.partial(regroup_kernel, sources, count),
        out_shape=outs,
        in_specs=vmem(2),
        out_specs=vmem(2),
        compiler_params=pltpu.CompilerParams(vmem_limit_bytes=2**20),
    )(stay, came)


def place(g, f):
    return (f >> 1) * 8 + ((f & 1) ^ (f >> 1)) * 4 + g


def multiply(t, groups, across, ids_ref, z, straight, scattered):
    tile_rows = z.shape[0] // len(groups)
    orb = z.shape[2]
    for g, group in enumerate(groups):
        if not group:
            continue
        here = across[g] * tile_rows + t
        places = [(tile, t * PER_ROW + p) for tile in group for p in range(PER_ROW)]
        strip = jnp.concatenate([s[slot][...] for (_, s, _, _), slot in places], axis=1)
        turned = jnp.concatenate([st[i, slot] for (_, _, st, i), slot in places], axis=0)
        where = [ids_ref[place(g, f), slot] for (f, *_), slot in places]
        wide = jnp.concatenate([z[u] for u in where], axis=1)
        straight[here] = jnp.dot(wide, turned, preferred_element_type=jnp.float32)
        mirrored = jnp.dot(z[here], strip, preferred_element_type=jnp.float32)
        for i, u in enumerate(where):
            scattered[i % len(scattered)][u] += mirrored[:, i * orb : (i + 1) * orb]


def clear(refs):
    for ref in refs:
        ref[...] = jnp.zeros_like(ref)


def turn_all(bufs, st_ref):
    def four(k, carry):
        for i, buf in enumerate(bufs):
            for m in range(4):
                st_ref[i, 4 * k + m] = buf[4 * k + m].T
        return carry

    lax.fori_loop(0, st_ref.shape[1] // 4, four, 0)


def grouped(tiles, n_col, n_row):
    return [[(f, *tiles[g, f]) for f in range(n_row) if (g, f) in tiles] for g in range(n_col)]


def spread_vectors(parts_ref, z, n_col, n_row, now=None):
    per_piece = z.shape[0] // (n_col * n_row)
    across = [lax.axis_index("col") ^ g for g in range(n_col)]
    down = [lax.axis_index("row") ^ f for f in range(n_row)]
    for g in range(n_col):
        for f in range(n_row):
            for b in range(per_piece):
                u = (across[g] * n_row + down[f]) * per_piece + b
                own = parts_ref[place(g, f) * per_piece + b]
                z[u] = own
                if now is not None:
                    now[u] = own.astype(jnp.float32)


def sum_products(groups, n_col, ids_ref, z, straight, scattered):
    across = [lax.axis_index("col") ^ g for g in range(n_col)]
    clear(scattered)

    for t in range(z.shape[0] // n_col):
        multiply(t, groups, across, ids_ref, z, straight, scattered)
    total = straight[...]
    for ref in scattered:
        total += ref[...]
    return total


def turned_kernel(*refs):
    turn_all(refs[:-1], refs[-1])


def turned_tiles(*bufs):
    size = len(bufs) * bufs[0].size
    return pl.pallas_call(
        turned_kernel,
        out_shape=jax.ShapeDtypeStruct((len(bufs), *bufs[0].shape), bufs[0].dtype),
        in_specs=vmem(len(bufs)),
        out_specs=vmem()[0],
        compiler_params=pltpu.CompilerParams(vmem_limit_bytes=2**20),
        cost_estimate=pl.CostEstimate(flops=0, bytes_accessed=6 * size, transcendentals=0),
    )(*bufs)


def first_kernel(early, later, n_col, n_row, ids_ref, parts_ref, sta_ref, *refs):
    sa, refs = refs[: len(early)], refs[len(early) :]
    sb, (stb_ref, sum_ref, z, straight, *scattered) = refs[: len(later)], refs[len(later) :]
    spread_vectors(parts_ref, z, n_col, n_row)
    turn_all(sb, stb_ref)
    tiles = {at: (s, sta_ref, i) for i, (at, s) in enumerate(zip(early, sa))}
    tiles.update({at: (s, stb_ref, i) for i, (at, s) in enumerate(zip(later, sb))})
    clear([straight])
    sum_ref[...] = sum_products(grouped(tiles, n_col, n_row), n_col, ids_ref, z, straight, scattered)


def filter_kernel(early, later, late, n_col, n_row, ids_ref, parts_ref, sum_ref, *refs):
    (sta_ref, stb_ref), refs = refs[:2], refs[2:]
    sa, refs = refs[: len(early)], refs[len(early) :]
    sb, refs = refs[: len(later)], refs[len(later) :]
    bufs, (out_ref, st_ref, z, now, prev, straight, *scattered) = refs[: len(late)], refs[len(late) :]
    n_blocks, share, orb = z.shape
    per_piece = n_blocks // (n_col * n_row)
    rest = sorted({(g, f) for g, f, _ in late})
    spread_vectors(parts_ref, z, n_col, n_row, prev)
    slots = {at: {} for at in rest}
    for buf, (g, f, start) in zip(bufs, late):
        for k in range(buf.shape[0]):
            slots[g, f][start + k] = buf.at[k]
    for i, at in enumerate(rest):
        for slot, block in slots[at].items():
            st_ref[i, slot] = block[...].T

    tiles = {at: (slots[at], st_ref, i) for i, at in enumerate(rest)}
    clear([straight])
    total = sum_products(grouped(tiles, n_col, n_row), n_col, ids_ref, z, straight, scattered)
    total += sum_ref[...]
    now[...] = total
    z[...] = total.astype(z.dtype)

    tiles.update({at: (s, sta_ref, i) for i, (at, s) in enumerate(zip(early, sa))})
    tiles.update({at: (s, stb_ref, i) for i, (at, s) in enumerate(zip(later, sb))})
    groups = grouped(tiles, n_col, n_row)

    def one_step(step, carry):
        total = sum_products(groups, n_col, ids_ref, z, straight, scattered)
        total = 2.0 * total - prev[...]
        prev[...] = now[...]
        now[...] = total
        z[...] = total.astype(z.dtype)
        return carry

    lax.fori_loop(1, DEG, one_step, 0)
    for p in range(n_col * n_row):
        for b in range(per_piece):
            u = p * per_piece + b
            out_ref[p, 0, :, b * orb : (b + 1) * orb] = now[u].astype(out_ref.dtype)
            out_ref[p, 1, :, b * orb : (b + 1) * orb] = prev[u].astype(out_ref.dtype)


def result_kernel(back_ref, marker_ref, last_ref, before_ref):
    count, _, share, rows = back_ref.shape
    for i, out_ref in enumerate((last_ref, before_ref)):
        whole = jnp.concatenate([back_ref[d, i] for d in range(count)], axis=0)
        out_ref[...] = whole.astype(jnp.float32).T


def gather_plan(vectors, blocks, cols):
    n_dev = lax.axis_size(LANES)
    n_col, n_row = lax.axis_size("col"), lax.axis_size("row")
    rows, width = vectors.shape
    slots, orb = blocks.shape[2:4]
    share = width // n_dev
    per_piece = rows // orb
    n_blocks = n_dev * per_piece
    half = slots // 2

    def send(buf, flip_col, flip_row, from_rows=range(n_row)):
        pairs = [
            (c * n_row + r, (c ^ flip_col) * n_row + (r ^ flip_row))
            for c in range(n_col)
            for r in from_rows
        ]
        return lax.ppermute(buf, LANES, pairs)

    def to_mate(*bufs):
        return [send(buf, 1, 0) for buf in bufs]

    own = blocks[0, 0]
    near = send(own, 0, 1)
    inner = send(own, 0, 3, INNER)
    over_own = after(send(own, 2, 0), rank=1)

    own_cols = jnp.broadcast_to(jnp.pad(cols[0, 0], (0, orb - slots)), (share, orb))
    shares = jax.ShapeDtypeStruct((n_dev // 2 * per_piece + 1, share, orb), vectors.dtype)
    stay, go = pl.pallas_call(
        functools.partial(split_kernel, n_col, n_row),
        out_shape=[shares, shares],
        in_specs=vmem(2),
        out_specs=vmem(2),
        scratch_shapes=[pltpu.VMEM((n_dev, share, rows), vectors.dtype)],
        compiler_params=pltpu.CompilerParams(vmem_limit_bytes=4 * 2**20),
    )(vectors, own_cols)
    stay, go = regroup(stay, send(go, 1, 0), 1, per_piece)

    stay, go = regroup(stay, send(go, 2, 0), 2, per_piece)
    mates = to_mate(own)
    near = after(near, over_own, go, *mates)
    over_near = after(send(near, 2, 0), rank=3)
    mates += to_mate(near)
    crossed = after(send(copy_after(near, mates[1]), 0, 3, INNER), rank=1)
    outward = send(inner, 0, 1, INNER)
    stay, go = regroup(stay, send(go, 0, 1), 4, per_piece)
    mates += to_mate(over_own)
    two = pick(INNER, crossed, outward, over_near, go, *mates)

    over_two = send(two, 2, 0)
    outer = after(send(crossed, 0, 1, INNER), rank=1)
    mates += to_mate(two, over_near)
    mine, ids = regroup(stay, send(go, 0, 3), 8, per_piece)
    sa = [own, near, over_own, over_near, *mates[:3]]
    sta = turned_tiles(*sa)
    three = pick(INNER, inner, outer, over_two, mine, sta, *mates[3:])

    over_three = send(three[:half], 2, 0)
    side_three = send(over_two[half:], 0, 1)
    mates += to_mate(three, over_two)
    early = [(0, 0), (0, 1), (2, 0), (2, 1), (1, 0), (1, 1), (3, 0)]
    later = [(0, 2), (2, 2), (0, 3), (1, 2), (3, 1), (1, 3), (3, 2)]
    tiles_of = jax.ShapeDtypeStruct((len(later), slots, orb, orb), blocks.dtype)
    sums = jax.ShapeDtypeStruct((n_blocks, share, orb), jnp.float32)
    sb = [two, over_two, three, *mates[3:]]
    stb, total = pl.pallas_call(
        functools.partial(first_kernel, early, later, n_col, n_row),
        out_shape=[tiles_of, sums],
        in_specs=smem() + vmem(2 + len(early + later)),
        out_specs=vmem(2),
        scratch_shapes=[
            pltpu.VMEM((n_blocks, share, orb), jnp.bfloat16),
            *[pltpu.VMEM((n_blocks, share, orb), jnp.float32)] * (1 + SPLIT),
        ],
        compiler_params=pltpu.CompilerParams(vmem_limit_bytes=6 * 2**20),
        cost_estimate=pl.CostEstimate(
            flops=4 * len(early + later) * slots * orb * orb * share,
            bytes_accessed=6 * len(later) * own.size,
            transcendentals=0,
        ),
    )(ids, mine, sta, *sa, *sb)
    over_three, side_three = after(over_three, stb), after(side_three, stb)
    late = [(2, 3, 0), (2, 3, half), (3, 3, 0), (3, 3, half)]
    late_bufs = [over_three, side_three, *to_mate(over_three, side_three)]

    done = pl.pallas_call(
        functools.partial(filter_kernel, early, later, late, n_col, n_row),
        out_shape=jax.ShapeDtypeStruct((n_dev, 2, share, rows), jnp.bfloat16),
        in_specs=smem() + vmem(4 + len(early + later + late)),
        out_specs=vmem()[0],
        scratch_shapes=[
            pltpu.VMEM((2, slots, orb, orb), blocks.dtype),
            pltpu.VMEM((n_blocks, share, orb), jnp.bfloat16),
            *[pltpu.VMEM((n_blocks, share, orb), jnp.float32)] * (3 + SPLIT),
        ],
        compiler_params=pltpu.CompilerParams(vmem_limit_bytes=12 * 2**20),
    )(ids, mine, total, sta, stb, *sa, *sb, *late_bufs)
    back = lax.all_to_all(done, LANES, split_axis=0, concat_axis=0, tiled=True)
    whole = jax.ShapeDtypeStruct((rows, width), jnp.float32)
    return pl.pallas_call(
        result_kernel,
        out_shape=[whole, whole],
        in_specs=vmem() + anywhere(),
        out_specs=vmem(2),
        compiler_params=pltpu.CompilerParams(vmem_limit_bytes=4 * 2**20),
    )(back, after(ids, done, rank=8))


def per_device(vectors, blocks, cols):
    n_dev = lax.axis_size(LANES)
    line_of_four = lax.axis_size("col") == 4 and lax.axis_size("row") == 4
    line_of_four = line_of_four and vectors.shape[1] // n_dev == n_dev
    if line_of_four and n_dev * blocks.size * blocks.dtype.itemsize <= GATHER_LIMIT:
        return gather_plan(vectors, blocks, cols)
    return spread_plan(vectors, blocks, cols)


def solution(mesh):
    return jax.shard_map(
        per_device,
        mesh=mesh,
        in_specs=(
            P(("col", "row"), "dom"),
            P(("dom", "col"), "row", None, None, None),
            P(("dom", "col"), "row", None),
        ),
        out_specs=(P(("col", "row"), "dom"), P(("col", "row"), "dom")),
        check_vma=False,
    )
```

```python
import functools

import jax
import jax.numpy as jnp
from jax import lax
from jax.experimental import pallas as pl
from jax.experimental.pallas import tpu as pltpu
from jax.sharding import PartitionSpec as P

PER_ROW = 2
DEG = 4
SPLIT = 8
GATHER_LIMIT = 12 * 2**20
LANES = ("col", "row")
INNER = (1, 2)


def onehot_sum(selected, high_part, low_part):
    first = jnp.einsum("su,sok->uok", selected, high_part, preferred_element_type=jnp.float32)
    second = jnp.einsum("su,sok->uok", selected, low_part, preferred_element_type=jnp.float32)
    return first + second


def apply_pair(send, grouped, col_ids, onehot):
    tile_rows, per_row, orb, _ = grouped.shape
    piece_rows, width = send.shape
    tile_cols = onehot.shape[1]
    wide = lax.all_gather(send, "col", axis=0, tiled=True).reshape(tile_cols, orb, width)
    picked = jnp.take(wide, col_ids, axis=0).reshape(tile_rows, per_row, orb, width)
    direct = jnp.einsum("tpio,tpok->tik", grouped, picked, preferred_element_type=jnp.float32)
    part_rows = lax.psum_scatter(
        direct.reshape(tile_rows * orb, width).astype(jnp.bfloat16),
        "row",
        scatter_dimension=0,
        tiled=True,
    ).astype(jnp.float32)
    tall = lax.all_gather(send, "row", axis=0, tiled=True).reshape(tile_rows, orb, width)
    mirrored = jnp.einsum("tpio,tik->tpok", grouped, tall, preferred_element_type=jnp.float32)
    mirrored = mirrored.reshape(tile_rows * per_row, orb, width)
    high_part = mirrored.astype(jnp.bfloat16)
    low_part = (mirrored - high_part.astype(jnp.float32)).astype(jnp.bfloat16)
    summed = onehot_sum(onehot, high_part, low_part)
    part_cols = lax.psum_scatter(
        summed.reshape(tile_cols * orb, width).astype(jnp.bfloat16),
        "col",
        scatter_dimension=0,
        tiled=True,
    ).astype(jnp.float32)
    return part_rows + part_cols


def spread_plan(vectors, blocks, cols):
    tiles = blocks[0, 0]
    col_ids = cols[0, 0]
    slots, orb, _ = tiles.shape
    tile_rows = slots // PER_ROW
    tile_cols = lax.axis_size("col") * (vectors.shape[0] // orb)
    grouped = tiles.reshape(tile_rows, PER_ROW, orb, orb)
    onehot = (col_ids[:, None] == jnp.arange(tile_cols, dtype=jnp.int32)[None, :]).astype(
        jnp.bfloat16
    )
    prev = vectors.astype(jnp.float32)
    now = apply_pair(vectors, grouped, col_ids, onehot)
    for step in range(DEG - 1):
        nxt = 2.0 * apply_pair(now.astype(jnp.bfloat16), grouped, col_ids, onehot) - prev
        prev, now = (now, nxt)
    return (now, prev)


def vmem(count=1):
    return [pl.BlockSpec(memory_space=pltpu.VMEM)] * count


def smem(count=1):
    return [pl.BlockSpec(memory_space=pltpu.SMEM)] * count


def anywhere(count=1):
    return [pl.BlockSpec(memory_space=pl.ANY)] * count


def nothing(*refs):
    pass


def after(value, *others, rank=0):
    return pl.pallas_call(
        nothing,
        out_shape=jax.ShapeDtypeStruct(value.shape, value.dtype),
        in_specs=anywhere(1 + len(others)),
        out_specs=anywhere()[0],
        input_output_aliases={0: 0},
        compiler_params=pltpu.CompilerParams(vmem_limit_bytes=2**20),
        cost_estimate=pl.CostEstimate(flops=0, bytes_accessed=rank * 2**23, transcendentals=0),
    )(value, *others)


def pick_kernel(rows, one_ref, other_ref, *refs):
    out_ref, sem = refs[-2:]
    row = lax.axis_index("row")
    first = (row == rows[0]) | (row == rows[1])

    @pl.when(first)
    def _():
        copy = pltpu.make_async_copy(one_ref, out_ref, sem)
        copy.start()
        copy.wait()

    @pl.when(jnp.logical_not(first))
    def _():
        copy = pltpu.make_async_copy(other_ref, out_ref, sem)
        copy.start()
        copy.wait()


def pick(rows, one, other, *others):
    return pl.pallas_call(
        functools.partial(pick_kernel, rows),
        out_shape=jax.ShapeDtypeStruct(one.shape, one.dtype),
        in_specs=anywhere(2 + len(others)),
        out_specs=anywhere()[0],
        scratch_shapes=[pltpu.SemaphoreType.DMA(())],
        compiler_params=pltpu.CompilerParams(vmem_limit_bytes=2**20),
    )(one, other, *others)


def split_kernel(n_col, n_row, vectors_ref, cols_ref, stay_ref, go_ref, turned):
    col, row = lax.axis_index("col"), lax.axis_index("row")
    count, share, rows = turned.shape
    orb = stay_ref.shape[2]
    per_piece = rows // orb
    whole = vectors_ref[...].T
    for d in range(count):
        turned[d] = whole[d * share : (d + 1) * share]
    orders = [(y, one, three) for y in range(2) for one in range(2) for three in range(2)]
    ids = cols_ref[...]
    piece = jnp.zeros_like(ids)
    for c in range(1, n_col):
        piece += (ids >= c * per_piece).astype(jnp.int32)
    ids = ids - piece * per_piece + (piece * n_row + row) * per_piece
    for core, out_ref in enumerate((stay_ref, go_ref)):
        for k, (y, one, three) in enumerate(orders):
            peer = (col ^ (core + 2 * y)) * n_row + (row ^ one ^ 3 * three)
            for b in range(per_piece):
                out_ref[k * per_piece + b] = turned[peer, :, b * orb : (b + 1) * orb]
        out_ref[len(orders) * per_piece] = ids.astype(jnp.float32).astype(out_ref.dtype)


def regroup_kernel(sources, count, stay_ref, came_ref, *outs):
    per_piece = (stay_ref.shape[0] - 1) // (sources * count)
    kept = max(count // 2, 1)
    ids = stay_ref[sources * count * per_piece].astype(jnp.float32)
    came = came_ref[sources * count * per_piece].astype(jnp.float32)
    line = lax.broadcasted_iota(jnp.int32, ids.shape, 0)
    ids = jnp.where(line < sources, ids, pltpu.roll(came, sources, 0))
    for h, out_ref in enumerate(outs):
        if h == 1 and count == 1:
            out_ref[...] = ids.astype(jnp.int32)
            continue
        for s in range(2 * sources):
            ref = stay_ref if s < sources else came_ref
            for k in range(kept * per_piece):
                out_ref[s * kept * per_piece + k] = ref[(s % sources * count + h * kept) * per_piece + k]
        if count > 1:
            out_ref[2 * sources * kept * per_piece] = ids.astype(out_ref.dtype)


def regroup(stay, came, sources, per_piece):
    count = (stay.shape[0] - 1) // (sources * per_piece)
    _, share, orb = stay.shape
    if count > 1:
        outs = [jax.ShapeDtypeStruct(stay.shape, stay.dtype)] * 2
    else:
        outs = [
            jax.ShapeDtypeStruct((2 * sources * per_piece, share, orb), stay.dtype),
            jax.ShapeDtypeStruct((share, orb), jnp.int32),
        ]
    return pl.pallas_call(
        functools.partial(regroup_kernel, sources, count),
        out_shape=outs,
        in_specs=vmem(2),
        out_specs=vmem(2),
        compiler_params=pltpu.CompilerParams(vmem_limit_bytes=2**20),
    )(stay, came)


def place(g, f):
    return (f >> 1) * 8 + ((f & 1) ^ (f >> 1)) * 4 + g


def multiply(t, groups, across, ids_ref, z, straight, scattered):
    tile_rows = z.shape[0] // len(groups)
    orb = z.shape[2]
    for g, group in enumerate(groups):
        if not group:
            continue
        here = across[g] * tile_rows + t
        places = [(tile, t * PER_ROW + p) for tile in group for p in range(PER_ROW)]
        strip = jnp.concatenate([s[slot][...] for (_, s, _, _), slot in places], axis=1)
        turned = jnp.concatenate([st[i, slot] for (_, _, st, i), slot in places], axis=0)
        where = [ids_ref[place(g, f), slot] for (f, *_), slot in places]
        wide = jnp.concatenate([z[u] for u in where], axis=1)
        straight[here] = jnp.dot(wide, turned, preferred_element_type=jnp.float32)
        mirrored = jnp.dot(z[here], strip, preferred_element_type=jnp.float32)
        for i, u in enumerate(where):
            scattered[i % len(scattered)][u] += mirrored[:, i * orb : (i + 1) * orb]


def clear(refs):
    for ref in refs:
        ref[...] = jnp.zeros_like(ref)


def turn_all(bufs, st_ref):
    def four(k, carry):
        for i, buf in enumerate(bufs):
            for m in range(4):
                st_ref[i, 4 * k + m] = buf[4 * k + m].T
        return carry

    lax.fori_loop(0, st_ref.shape[1] // 4, four, 0)


def grouped(tiles, n_col, n_row):
    return [[(f, *tiles[g, f]) for f in range(n_row) if (g, f) in tiles] for g in range(n_col)]


def spread_vectors(parts_ref, z, n_col, n_row, now=None):
    per_piece = z.shape[0] // (n_col * n_row)
    across = [lax.axis_index("col") ^ g for g in range(n_col)]
    down = [lax.axis_index("row") ^ f for f in range(n_row)]
    for g in range(n_col):
        for f in range(n_row):
            for b in range(per_piece):
                u = (across[g] * n_row + down[f]) * per_piece + b
                own = parts_ref[place(g, f) * per_piece + b]
                z[u] = own
                if now is not None:
                    now[u] = own.astype(jnp.float32)


def sum_products(groups, n_col, ids_ref, z, straight, scattered):
    across = [lax.axis_index("col") ^ g for g in range(n_col)]
    clear(scattered)

    for t in range(z.shape[0] // n_col):
        multiply(t, groups, across, ids_ref, z, straight, scattered)
    total = straight[...]
    for ref in scattered:
        total += ref[...]
    return total


def turned_kernel(*refs):
    turn_all(refs[:-1], refs[-1])


def turned_tiles(*bufs):
    size = len(bufs) * bufs[0].size
    return pl.pallas_call(
        turned_kernel,
        out_shape=jax.ShapeDtypeStruct((len(bufs), *bufs[0].shape), bufs[0].dtype),
        in_specs=vmem(len(bufs)),
        out_specs=vmem()[0],
        compiler_params=pltpu.CompilerParams(vmem_limit_bytes=2**20),
        cost_estimate=pl.CostEstimate(flops=0, bytes_accessed=6 * size, transcendentals=0),
    )(*bufs)


def first_kernel(early, later, n_col, n_row, ids_ref, parts_ref, sta_ref, *refs):
    sa, refs = refs[: len(early)], refs[len(early) :]
    sb, (stb_ref, sum_ref, z, straight, *scattered) = refs[: len(later)], refs[len(later) :]
    spread_vectors(parts_ref, z, n_col, n_row)
    turn_all(sb, stb_ref)
    tiles = {at: (s, sta_ref, i) for i, (at, s) in enumerate(zip(early, sa))}
    tiles.update({at: (s, stb_ref, i) for i, (at, s) in enumerate(zip(later, sb))})
    clear([straight])
    sum_ref[...] = sum_products(grouped(tiles, n_col, n_row), n_col, ids_ref, z, straight, scattered)


def filter_kernel(early, later, late, n_col, n_row, ids_ref, parts_ref, sum_ref, *refs):
    (sta_ref, stb_ref), refs = refs[:2], refs[2:]
    sa, refs = refs[: len(early)], refs[len(early) :]
    sb, refs = refs[: len(later)], refs[len(later) :]
    bufs, (out_ref, st_ref, z, now, prev, straight, *scattered) = refs[: len(late)], refs[len(late) :]
    n_blocks, share, orb = z.shape
    per_piece = n_blocks // (n_col * n_row)
    rest = sorted({(g, f) for g, f, _ in late})
    spread_vectors(parts_ref, z, n_col, n_row, prev)
    slots = {at: {} for at in rest}
    for buf, (g, f, start) in zip(bufs, late):
        for k in range(buf.shape[0]):
            slots[g, f][start + k] = buf.at[k]
    for i, at in enumerate(rest):
        for slot, block in slots[at].items():
            st_ref[i, slot] = block[...].T

    tiles = {at: (slots[at], st_ref, i) for i, at in enumerate(rest)}
    clear([straight])
    total = sum_products(grouped(tiles, n_col, n_row), n_col, ids_ref, z, straight, scattered)
    total += sum_ref[...]
    now[...] = total
    z[...] = total.astype(z.dtype)

    tiles.update({at: (s, sta_ref, i) for i, (at, s) in enumerate(zip(early, sa))})
    tiles.update({at: (s, stb_ref, i) for i, (at, s) in enumerate(zip(later, sb))})
    groups = grouped(tiles, n_col, n_row)

    def one_step(step, carry):
        total = sum_products(groups, n_col, ids_ref, z, straight, scattered)
        total = 2.0 * total - prev[...]
        prev[...] = now[...]
        now[...] = total
        z[...] = total.astype(z.dtype)
        return carry

    lax.fori_loop(1, DEG, one_step, 0)
    for p in range(n_col * n_row):
        for b in range(per_piece):
            u = p * per_piece + b
            out_ref[p, 0, :, b * orb : (b + 1) * orb] = now[u].astype(out_ref.dtype)
            out_ref[p, 1, :, b * orb : (b + 1) * orb] = prev[u].astype(out_ref.dtype)


def result_kernel(back_ref, marker_ref, last_ref, before_ref):
    count, _, share, rows = back_ref.shape
    for i, out_ref in enumerate((last_ref, before_ref)):
        whole = jnp.concatenate([back_ref[d, i] for d in range(count)], axis=0)
        out_ref[...] = whole.astype(jnp.float32).T


def gather_plan(vectors, blocks, cols):
    n_dev = lax.axis_size(LANES)
    n_col, n_row = lax.axis_size("col"), lax.axis_size("row")
    rows, width = vectors.shape
    slots, orb = blocks.shape[2:4]
    share = width // n_dev
    per_piece = rows // orb
    n_blocks = n_dev * per_piece
    half = slots // 2

    def send(buf, flip_col, flip_row, from_rows=range(n_row)):
        pairs = [
            (c * n_row + r, (c ^ flip_col) * n_row + (r ^ flip_row))
            for c in range(n_col)
            for r in from_rows
        ]
        return lax.ppermute(buf, LANES, pairs)

    def to_mate(*bufs):
        return [send(buf, 1, 0) for buf in bufs]

    own = blocks[0, 0]
    near = send(own, 0, 1)
    inner = send(own, 0, 3, INNER)
    over_own = after(send(own, 2, 0), rank=1)

    own_cols = jnp.broadcast_to(jnp.pad(cols[0, 0], (0, orb - slots)), (share, orb))
    shares = jax.ShapeDtypeStruct((n_dev // 2 * per_piece + 1, share, orb), vectors.dtype)
    stay, go = pl.pallas_call(
        functools.partial(split_kernel, n_col, n_row),
        out_shape=[shares, shares],
        in_specs=vmem(2),
        out_specs=vmem(2),
        scratch_shapes=[pltpu.VMEM((n_dev, share, rows), vectors.dtype)],
        compiler_params=pltpu.CompilerParams(vmem_limit_bytes=4 * 2**20),
    )(vectors, own_cols)
    stay, go = regroup(stay, send(go, 1, 0), 1, per_piece)

    stay, go = regroup(stay, send(go, 2, 0), 2, per_piece)
    mates = to_mate(own)
    near = after(near, over_own, go, *mates)
    over_near = after(send(near, 2, 0), rank=3)
    crossed = after(send(near, 0, 3, INNER), rank=1)
    inner = after(inner, near)
    outward = after(send(inner, 0, 1, INNER), rank=1)
    stay, go = regroup(stay, send(go, 0, 1), 4, per_piece)
    mates += to_mate(near, over_own)
    two = pick(INNER, crossed, outward, over_near, go, *mates)

    over_two = send(two, 2, 0)
    outer = after(send(crossed, 0, 1, INNER), rank=1)
    mates += to_mate(two, over_near)
    mine, ids = regroup(stay, send(go, 0, 3), 8, per_piece)
    sa = [own, near, over_own, over_near, *mates[:3]]
    sta = turned_tiles(*sa)
    three = pick(INNER, inner, outer, over_two, mine, sta, *mates[3:])

    over_three = send(three[:half], 2, 0)
    side_three = send(over_two[half:], 0, 1)
    mates += to_mate(three, over_two)
    early = [(0, 0), (0, 1), (2, 0), (2, 1), (1, 0), (1, 1), (3, 0)]
    later = [(0, 2), (2, 2), (0, 3), (1, 2), (3, 1), (1, 3), (3, 2)]
    tiles_of = jax.ShapeDtypeStruct((len(later), slots, orb, orb), blocks.dtype)
    sums = jax.ShapeDtypeStruct((n_blocks, share, orb), jnp.float32)
    sb = [two, over_two, three, *mates[3:]]
    stb, total = pl.pallas_call(
        functools.partial(first_kernel, early, later, n_col, n_row),
        out_shape=[tiles_of, sums],
        in_specs=smem() + vmem(2 + len(early + later)),
        out_specs=vmem(2),
        scratch_shapes=[
            pltpu.VMEM((n_blocks, share, orb), jnp.bfloat16),
            *[pltpu.VMEM((n_blocks, share, orb), jnp.float32)] * (1 + SPLIT),
        ],
        compiler_params=pltpu.CompilerParams(vmem_limit_bytes=6 * 2**20),
        cost_estimate=pl.CostEstimate(
            flops=4 * len(early + later) * slots * orb * orb * share,
            bytes_accessed=6 * len(later) * own.size,
            transcendentals=0,
        ),
    )(ids, mine, sta, *sa, *sb)
    over_three, side_three = after(over_three, stb), after(side_three, stb)
    late = [(2, 3, 0), (2, 3, half), (3, 3, 0), (3, 3, half)]
    late_bufs = [over_three, side_three, *to_mate(over_three, side_three)]

    done = pl.pallas_call(
        functools.partial(filter_kernel, early, later, late, n_col, n_row),
        out_shape=jax.ShapeDtypeStruct((n_dev, 2, share, rows), jnp.bfloat16),
        in_specs=smem() + vmem(4 + len(early + later + late)),
        out_specs=vmem()[0],
        scratch_shapes=[
            pltpu.VMEM((2, slots, orb, orb), blocks.dtype),
            pltpu.VMEM((n_blocks, share, orb), jnp.bfloat16),
            *[pltpu.VMEM((n_blocks, share, orb), jnp.float32)] * (3 + SPLIT),
        ],
        compiler_params=pltpu.CompilerParams(vmem_limit_bytes=12 * 2**20),
    )(ids, mine, total, sta, stb, *sa, *sb, *late_bufs)
    back = lax.all_to_all(done, LANES, split_axis=0, concat_axis=0, tiled=True)
    whole = jax.ShapeDtypeStruct((rows, width), jnp.float32)
    return pl.pallas_call(
        result_kernel,
        out_shape=[whole, whole],
        in_specs=vmem() + anywhere(),
        out_specs=vmem(2),
        compiler_params=pltpu.CompilerParams(vmem_limit_bytes=4 * 2**20),
    )(back, after(ids, done, rank=8))


def per_device(vectors, blocks, cols):
    n_dev = lax.axis_size(LANES)
    line_of_four = lax.axis_size("col") == 4 and lax.axis_size("row") == 4
    line_of_four = line_of_four and vectors.shape[1] // n_dev == n_dev
    if line_of_four and n_dev * blocks.size * blocks.dtype.itemsize <= GATHER_LIMIT:
        return gather_plan(vectors, blocks, cols)
    return spread_plan(vectors, blocks, cols)


def solution(mesh):
    return jax.shard_map(
        per_device,
        mesh=mesh,
        in_specs=(
            P(("col", "row"), "dom"),
            P(("dom", "col"), "row", None, None, None),
            P(("dom", "col"), "row", None),
        ),
        out_specs=(P(("col", "row"), "dom"), P(("col", "row"), "dom")),
        check_vma=False,
    )
```
